256 devices in a mesh: dp: 32 (over z, x_lo, core), tensor: 8 (over y, x_hi).
Axes of the slice: x: 4 (x_hi: 2, x_lo: 2; x = x_hi * 2 + x_lo), y: 4, z: 8, core: 2. Of those that a mesh axis runs over, the one named last changes fastest.
Arguments:
- inputs: bfloat16 [32768, 5120], P(('dp', 'tensor')), may hold values from -36 to 36
- norm_gain: bfloat16 [5120], replicated, may hold values from 0.099609375 to 1.8984375
- key_weight: bfloat16 [5120, 1024], P('dp', 'tensor'), may hold values from -0.078125 to 0.078125
- value_weight: bfloat16 [5120, 1024], P('dp', 'tensor'), may hold values from -0.078125 to 0.078125
- head_gain: bfloat16 [128], replicated, may hold values from 0.099609375 to 1.8984375
- key_cotangent: bfloat16 [32768, 1024], P('dp', 'tensor'), may hold values from -6 to 6
- value_cotangent: bfloat16 [32768, 1024], P('dp', 'tensor'), may hold values from -6 to 6
Outputs:
- key_states: bfloat16 [32768, 1024], P('dp', 'tensor')
- value_states: bfloat16 [32768, 1024], P('dp', 'tensor')
- input_grad: bfloat16 [32768, 5120], P(('dp', 'tensor'))
- key_weight_grad: float32 [5120, 1024], P('dp', 'tensor')
- value_weight_grad: float32 [5120, 1024], P('dp', 'tensor')
- norm_gain_grad: float32 [5120], replicated
- head_gain_grad: float32 [128], replicated
The draws below stay inside these ranges and needn't reach their ends.
All inputs are finite; a program needn't handle non-finite values.
Results may differ from the reference program's by a relative error of at most 0.005.
Values may be sent and summed in bfloat16 or wider, within the bound.
A program may use at most 128 MiB of HBM per device.

```python
import math
import jax
import jax.numpy as jnp
from jax import lax

D = 5120
KV_HEADS = 8
HEAD = 128
KVD = 1024
TOKENS = 32768


def draw_inputs(key, part):
    key = jax.random.fold_in(key, 11)
    first, second, third = jax.random.split(key, 3)
    base = jnp.clip(jax.random.normal(first, (TOKENS, D), jnp.float32), -4.0, 4.0)
    row_scale = jnp.exp(jax.random.uniform(second, (TOKENS, 1), jnp.float32, math.log(0.3), math.log(3.0)))
    column_scale = jnp.exp(jax.random.uniform(third, (1, D), jnp.float32, math.log(0.3), math.log(3.0)))
    return (base * row_scale * column_scale).astype(jnp.bfloat16)


def level_of(key, shape, shards, low, high):
    level = 1.0
    for position, blocks in shards:
        steps = jax.random.uniform(jax.random.fold_in(jax.random.fold_in(key, 6), position), (blocks,), jnp.float32, low / len(shards), high / len(shards))
        level = level * jnp.repeat(jnp.exp(steps), shape[position] // blocks).reshape((-1,) + (1,) * (len(shape) - 1 - position))
    return level


def centred(stream_key, dims, deviation, limit, cuts=(), dtype=jnp.bfloat16):
    array = deviation * jax.random.normal(stream_key, dims, jnp.float32)
    if cuts:
        array = array * level_of(stream_key, dims, cuts, -0.22, 0.18)
    return jnp.clip(array, -limit, limit).astype(dtype)


def setup_inputs(seed: int = 0) -> dict:
    streams_of = jax.random.split(jax.random.key(seed), 8)
    return {
        "inputs": draw_inputs(jax.random.fold_in(streams_of[7], 71), 0),
        "norm_gain": jnp.clip(1.0 + 0.18 * jax.random.normal(streams_of[1], (D,), jnp.float32), 0.099609375, 1.8984375).astype(jnp.bfloat16),
        "key_weight": centred(streams_of[2], (D, KVD), D ** -0.5, 0.078125, ((0, 32), (1, 8))),
        "value_weight": centred(streams_of[3], (D, KVD), D ** -0.5, 0.078125, ((0, 32), (1, 8))),
        "head_gain": jnp.clip(1.0 + 0.18 * jax.random.normal(streams_of[4], (HEAD,), jnp.float32), 0.099609375, 1.8984375).astype(jnp.bfloat16),
        "key_cotangent": centred(streams_of[5], (TOKENS, KVD), 1.0, 6.0, ((0, 32), (1, 8))),
        "value_cotangent": centred(streams_of[6], (TOKENS, KVD), 1.0, 6.0, ((0, 32), (1, 8))),
    }


eps = 1e-06

def reference(inputs, norm_gain, key_weight, value_weight, head_gain, key_cotangent, value_cotangent):
    xf = inputs.astype(jnp.float32)
    rinv = lax.rsqrt(lax.optimization_barrier(jnp.mean(xf * xf, axis=-1, keepdims=True)) + eps)
    normed = xf * rinv
    gain_in = norm_gain.astype(jnp.float32)
    hidden = (normed * gain_in).astype(jnp.bfloat16)
    key_raw = jnp.dot(hidden, key_weight, preferred_element_type=jnp.float32)
    value_states = jnp.dot(hidden, value_weight, preferred_element_type=jnp.float32).astype(jnp.bfloat16)
    heads = key_raw.reshape(TOKENS, KV_HEADS, HEAD)
    krinv = lax.rsqrt(lax.optimization_barrier(jnp.mean(heads * heads, axis=-1, keepdims=True)) + eps)
    key_normed = heads * krinv
    gain_head = head_gain.astype(jnp.float32)
    key_states = (key_normed * gain_head).reshape(TOKENS, KVD).astype(jnp.bfloat16)
    cot_heads = key_cotangent.astype(jnp.float32).reshape(TOKENS, KV_HEADS, HEAD)
    key_back = cot_heads * gain_head
    key_raw_grad = krinv * (key_back - key_normed * lax.optimization_barrier(jnp.mean(key_back * key_normed, axis=-1, keepdims=True)))
    key_raw_grad = key_raw_grad.reshape(TOKENS, KVD).astype(jnp.bfloat16)
    head_gain_grad = lax.optimization_barrier(jnp.sum(cot_heads * key_normed, axis=(0, 1)))
    key_weight_grad = jnp.dot(hidden.T, key_raw_grad, preferred_element_type=jnp.float32)
    value_weight_grad = jnp.dot(hidden.T, value_cotangent, preferred_element_type=jnp.float32)
    hidden_grad = jnp.dot(key_raw_grad, key_weight.T, preferred_element_type=jnp.float32)
    hidden_grad = hidden_grad + jnp.dot(value_cotangent, value_weight.T, preferred_element_type=jnp.float32)
    norm_gain_grad = lax.optimization_barrier(jnp.sum(hidden_grad * normed, axis=0))
    back = hidden_grad * gain_in
    input_grad = (rinv * (back - normed * lax.optimization_barrier(jnp.mean(back * normed, axis=-1, keepdims=True)))).astype(jnp.bfloat16)
    return (key_states, value_states, input_grad, key_weight_grad, value_weight_grad, norm_gain_grad, head_gain_grad)
```

```python
import jax
import jax.numpy as jnp
from jax import lax
from jax.experimental import pallas as pl
from jax.experimental.pallas import tpu as pltpu
from jax.sharding import PartitionSpec as P

eps = 1e-06
MESH = pl.DeviceIdType.MESH
T = 128
D = 5120
DC = 1280
R = 160
H = 128
bf16 = jnp.bfloat16
f32 = jnp.float32


def dot(a, b):
    return jnp.dot(a, b, preferred_element_type=f32)


def dot_nt(a, b):
    return lax.dot_general(a, b, (((1,), (1,)), ((), ())), preferred_element_type=f32)


def loop(n, body):
    def step(i, carry):
        body(i)
        return carry

    lax.fori_loop(0, n, step, 0)


def kernel(
    x_ref,
    gain_ref,
    wk_ref,
    wv_ref,
    hgain_ref,
    kcot_ref,
    vcot_ref,
    ks_ref,
    vs_ref,
    ig_ref,
    dwk_ref,
    dwv_ref,
    ng_ref,
    hg_ref,
    hid,
    hc,
    hct,
    w,
    psend,
    precv,
    own,
    cot,
    cb,
    oown,
    orecv,
    dhv,
    dhs,
    dhr,
    dw,
    dwc,
    dwx,
    zs,
    zr,
    fin,
    finr,
    vx,
    vz,
    vc,
    vy,
    rinv_s,
    s_w0,
    s_wz,
    s_wx,
    s_wc,
    s_hid,
    s_cot,
    s_va,
    s_ka,
    s_p,
    s_out,
    s_dh,
    s_dc,
    s_dx,
    s_dz,
    s_dp,
    s_vx,
    s_vz,
    s_vc,
    s_vy,
):
    dp, tn = lax.axis_index("dp"), lax.axis_index("tensor")
    z, xl, c = lax.div(dp, 4), lax.rem(lax.div(dp, 2), 2), lax.rem(dp, 2)
    y, xh = lax.div(tn, 2), lax.rem(tn, 2)
    x = 2 * xh + xl
    zh, ze = lax.div(z, 2), lax.rem(z, 2)

    def device(x, y, z, c):
        return (z * 4 + lax.rem(x, 2) * 2 + c, y * 2 + lax.div(x, 2))

    def ring_x(d):
        return lax.rem(x + d, 4)

    def ring_y(d):
        return lax.rem(y + d, 4)

    def ring_z(d):
        return lax.rem(z + d, 8)

    def at_x(px):
        return device(px, y, z, c)

    def at_y(py):
        return device(x, py, z, c)

    def at_z(pz):
        return device(x, y, pz, c)

    core = device(x, y, z, 1 - c)
    opposite = device(2 * (1 - xh) + xl, y, z, c)
    partner = device(x, zh, 2 * y + ze, c)
    moved = zh != y

    def send(src, dst, sems, s_at, r_at, to):
        pltpu.make_async_remote_copy(
            src_ref=src,
            dst_ref=dst,
            send_sem=sems.at[(0,) + s_at],
            recv_sem=sems.at[(1,) + r_at],
            device_id=to,
            device_id_type=MESH,
        ).start()

    def copy_of(ref, sems, at):
        return pltpu.make_async_remote_copy(
            src_ref=ref,
            dst_ref=ref,
            send_sem=sems.at[(0,) + at],
            recv_sem=sems.at[(1,) + at],
            device_id=core,
            device_id_type=MESH,
        )

    def arrived(ref, sems, at):
        copy_of(ref, sems, at).wait_recv()

    def sent(ref, sems, at):
        copy_of(ref, sems, at).wait_send()

    barrier = pltpu.get_barrier_semaphore()

    def hello(to):
        pl.semaphore_signal(barrier, inc=1, device_id=to, device_id_type=MESH)

    for d in range(1, 4):
        hello(at_x(ring_x(d)))
        hello(at_y(ring_y(d)))
    for d in range(1, 8):
        hello(at_z(ring_z(d)))
    hello(core)

    @pl.when(moved)
    def _():
        hello(partner)

    def norm_rows(i):
        rows = pl.ds(pl.multiple_of(i * 16, 16), 16)
        xf = x_ref[rows, :].astype(f32)
        rinv = lax.rsqrt(jnp.mean(xf * xf, axis=-1, keepdims=True) + eps)
        rinv_s[rows, :] = jnp.broadcast_to(rinv, (16, 128))
        hd = (xf * rinv * gain_ref[...]).astype(bf16)
        for k in range(4):
            hid[k, rows, :] = hd[:, k * DC : (k + 1) * DC]

    loop(8, norm_rows)
    hc[y] = hid[y]
    cb[1, y, xh] = vcot_ref[:, xh]
    cot[xh] = kcot_ref[:, xh]

    pl.semaphore_wait(barrier, jnp.where(moved, 15, 14))

    def w_own(kv):
        return w.at[kv, zh, xh, ze, xl, c]

    @pl.when(moved)
    def _():
        for kv, ref in ((0, wk_ref), (1, wv_ref)):
            send(ref, w.at[kv, y, xh, ze, xl, c], s_w0, (kv,), (kv,), partner)

    @pl.when(jnp.logical_not(moved))
    def _():
        for kv, ref in ((0, wk_ref), (1, wv_ref)):
            w[kv, zh, xh, ze, xl, c] = ref[...]

    for d in (1, 3, 2):
        py = ring_y(d)
        send(hid.at[py], hc.at[y], s_hid, (py,), (y,), at_y(py))
    send(vcot_ref.at[:, 1 - xh], cb.at[1, y, xh], s_cot, (1,), (1,), opposite)
    send(kcot_ref.at[:, 1 - xh], cot.at[xh], s_cot, (0,), (0,), opposite)

    def z_sends(kv):
        @pl.when(moved)
        def _():
            arrived(w_own(kv), s_w0, (kv,))

        def body(i):
            pz = ring_z(i + 1)
            send(w_own(kv), w_own(kv), s_wz, (kv, pz), (kv, z), at_z(pz))

        loop(7, body)

    def x_sends(kv, i):
        h = ring_y(i + 1)

        def wait_z(e):
            pz = 2 * h + e

            @pl.when(pz != z)
            def _():
                arrived(w.at[kv, h, xh, e, xl, c], s_wz, (kv, pz))

        loop(2, wait_z)
        part = w.at[kv, h, xh, :, xl, c]
        for d in (1, 3, 2):
            px = ring_x(d)
            send(part, part, s_wx, (kv, h, px), (kv, h, x), at_x(px))

    def core_sends(kv, i):
        h = ring_y(i + 1)

        def wait_x(d):
            px = ring_x(d + 1)
            pxl, pxh = lax.rem(px, 2), lax.div(px, 2)
            arrived(w.at[kv, h, pxh, :, pxl, c], s_wx, (kv, h, px))

        loop(3, wait_x)
        part = w.at[kv, h, :, :, :, c]
        send(part, part, s_wc, (kv, h), (kv, h), core)

    z_sends(0)
    z_sends(1)
    arrived(cb.at[1, y, 1 - xh], s_cot, (1,))
    for d in (1, 3, 2):
        py = ring_y(d)
        send(cb.at[1, y], cb.at[1, y], s_va, (py,), (y,), at_y(py))
    loop(4, lambda i: x_sends(0, i))

    def panel(kv, h):
        return jnp.concatenate(
            [w[kv, h, 0].reshape(DC, H), w[kv, h, 1].reshape(DC, H)], axis=1
        )

    def tokens():
        return hc[...].reshape(4 * T, DC)

    def forward(kv, i):
        h = ring_y(i + 1)
        arrived(w.at[kv, h, :, :, :, 1 - c], s_wc, (kv, h))
        part = dot(tokens(), panel(kv, h))

        @pl.when(h != y)
        def _():
            psend[kv, h] = part.astype(bf16)

        @pl.when(h == y)
        def _():
            own[kv] = part

    def partial_send(kv, d):
        py = ring_y(d)
        send(psend.at[kv, py], precv.at[kv, y], s_p, (kv, py), (kv, y), at_y(py))

    def hidden_wait(d):
        py = ring_y(d + 1)
        arrived(hc.at[py], s_hid, (py,))

    loop(3, hidden_wait)

    def key_step(i):
        @pl.when(i < 4)
        def _():
            core_sends(0, i)
            x_sends(1, i)

        @pl.when(i > 0)
        def _():
            forward(0, i - 1)

        @pl.when(jnp.logical_and(i > 0, i < 4))
        def _():
            partial_send(0, i)

    loop(5, key_step)

    for k in range(4):
        hct[:, k * T : (k + 1) * T] = hc[k].T

    def grad_tile(kv, h):
        ct = jnp.concatenate(
            [cb[kv, h, 0].reshape(4 * T, H), cb[kv, h, 1].reshape(4 * T, H)], axis=1
        )
        g = dot(hct[...], ct).astype(bf16).reshape(2, 2, 2, R, 2 * H)
        for pc in range(2):
            for ph in range(2):
                for pxl in range(2):
                    dw[kv, h, pc, 2 * ph + pxl] = g[:, pxl, pc, :, ph * H : (ph + 1) * H]
        send(dw.at[kv, h, 1 - c], dwc.at[kv, h], s_dc, (kv, h), (kv, h), core)

    def grad_core(kv, h):
        arrived(dwc.at[kv, h], s_dc, (kv, h))
        dw[kv, h, c] = (dw[kv, h, c].astype(f32) + dwc[kv, h].astype(f32)).astype(bf16)
        for d in (1, 3, 2):
            px = ring_x(d)
            send(
                dw.at[kv, h, c, px], dwx.at[kv, h, x], s_dx, (kv, h, px), (kv, h, x), at_x(px)
            )

    def grad_x(kv, h):
        total = dw[kv, h, c, x].astype(f32)
        for d in range(1, 4):
            px = ring_x(d)
            arrived(dwx.at[kv, h, px], s_dx, (kv, h, px))
            total = total + dwx[kv, h, px].astype(f32)
        zs[kv, h] = total.astype(bf16)

        def body(e):
            pz = 2 * h + e

            @pl.when(pz != z)
            def _():
                send(zs.at[kv, h, e], zr.at[kv, z], s_dz, (kv, pz), (kv, z), at_z(pz))

        loop(2, body)

    def grad_z(kv):
        total = zs[kv, zh, ze].astype(f32)
        for d in range(1, 8):
            pz = ring_z(d)
            arrived(zr.at[kv, pz], s_dz, (kv, pz))
            total = total + zr[kv, pz].astype(f32)

        @pl.when(moved)
        def _():
            fin[kv] = total
            send(fin.at[kv], finr.at[kv], s_dp, (kv,), (kv,), partner)

        @pl.when(jnp.logical_not(moved))
        def _():
            finr[kv] = total

    def value_wait(d):
        py = ring_y(d + 1)
        arrived(cb.at[1, py], s_va, (py,))

    loop(3, value_wait)
    loop(4, lambda i: grad_tile(1, ring_y(i)))

    arrived(cot.at[1 - xh], s_cot, (0,))

    def wait_partial(kv):
        def body(d):
            py = ring_y(d + 1)
            arrived(precv.at[kv, py], s_p, (kv, py))

        loop(3, body)

    def summed(kv, t, s):
        rows = pl.ds(pl.multiple_of(t * T, T), T)
        cols = slice(s * H, (s + 1) * H)
        total = own[kv, rows, cols]
        for d in range(1, 4):
            total = total + precv[kv, ring_y(d), rows, cols].astype(f32)
        return total

    wait_partial(0)
    hgain = hgain_ref[...]
    vx[x] = jnp.zeros((1, DC + H), f32)

    def key_block(t):
        for s in range(2):
            key = summed(0, t, s)
            krinv = lax.rsqrt(jnp.mean(key * key, axis=-1, keepdims=True) + eps)
            kn = key * krinv
            oown[0, s, t] = (kn * hgain).astype(bf16)
            ct = cot[s, t].astype(f32)
            back = ct * hgain
            grad = krinv * (back - kn * jnp.mean(back * kn, axis=-1, keepdims=True))
            cb[0, y, s, t] = grad.astype(bf16)
            vx[x, :, DC:] += jnp.sum(ct * kn, axis=0, keepdims=True)

    loop(4, key_block)

    def key_gather(i):
        for d in (1, 3, 2):
            py = ring_y(d)
            t = lax.rem(py + 1 + i, 4)
            part = cb.at[0, y, :, t]
            send(part, part, s_ka, (py, t), (y, t), at_y(py))

    loop(4, key_gather)
    send(oown.at[0, 1 - xh], orecv.at[0], s_out, (0,), (0,), opposite)

    loop(4, lambda i: core_sends(1, i))
    loop(4, lambda i: grad_core(1, ring_y(i)))
    grad_tile(0, y)
    loop(4, lambda i: forward(1, i))

    def values_back(i):
        ct = jnp.concatenate(
            [cb[1, i, 0].reshape(4 * T, H), cb[1, i, 1].reshape(4 * T, H)], axis=1
        )
        part = dot_nt(ct, panel(1, i)).reshape(4, T, DC)

        @pl.when(i == 0)
        def _():
            dhv[...] = part

        @pl.when(i > 0)
        def _():
            dhv[...] += part

    loop(4, values_back)

    def hidden_back(i):
        t = ring_y(i + 1)
        for d in range(1, 4):
            py = ring_y(d)
            arrived(cb.at[0, py, :, t], s_ka, (py, t))
        total = dhv[t]
        for k in range(4):
            ct = jnp.concatenate([cb[0, k, 0, t], cb[0, k, 1, t]], axis=1)
            total = total + dot_nt(ct, panel(0, k))
        vx[x, :, :DC] += jnp.sum(total * hc[t].astype(f32), axis=0, keepdims=True)

        @pl.when(t != y)
        def _():
            dhs[t] = total.astype(bf16)
            send(dhs.at[t], dhr.at[y], s_dh, (t,), (y,), at_y(t))

        @pl.when(t == y)
        def _():
            dhr[y] = total.astype(bf16)

    loop(4, hidden_back)
    loop(3, lambda i: grad_tile(0, ring_y(i + 1)))
    for d in (1, 3, 2):
        partial_send(1, d)
    for d in range(1, 4):
        px = ring_x(d)
        send(vx.at[x], vx.at[x], s_vx, (px,), (x,), at_x(px))
    loop(4, lambda i: grad_core(0, ring_y(i)))
    loop(4, lambda i: grad_x(1, ring_y(i)))

    def vec_wait(ref, sems, me, n):
        def body(i):
            p = lax.rem(me + 1 + i, n)
            arrived(ref.at[p], sems, (p,))

        loop(n - 1, body)

    vec_wait(vx, s_vx, x, 4)
    vz[z] = (vx[0] + vx[1]) + (vx[2] + vx[3])

    def vz_send(i):
        pz = ring_z(i + 1)
        send(vz.at[z], vz.at[z], s_vz, (pz,), (z,), at_z(pz))

    loop(7, vz_send)

    def dh_wait(d):
        py = ring_y(d + 1)
        arrived(dhr.at[py], s_dh, (py,))

    loop(3, dh_wait)

    def input_rows(i):
        rows = pl.ds(pl.multiple_of(i * 16, 16), 16)
        rinv = rinv_s[rows, 0:1]
        mean = jnp.zeros((16, 1), f32)
        for k in range(4):
            cols = slice(k * DC, (k + 1) * DC)
            normed = x_ref[rows, cols].astype(f32) * rinv
            back = dhr[k, rows, :].astype(f32) * gain_ref[:, cols]
            mean = mean + jnp.sum(back * normed, axis=-1, keepdims=True)
        mean = mean * (1.0 / D)
        for k in range(4):
            cols = slice(k * DC, (k + 1) * DC)
            normed = x_ref[rows, cols].astype(f32) * rinv
            back = dhr[k, rows, :].astype(f32) * gain_ref[:, cols]
            ig_ref[rows, cols] = (rinv * (back - normed * mean)).astype(bf16)

    loop(8, input_rows)
    vec_wait(vz, s_vz, z, 8)
    vc[c] = ((vz[0] + vz[1]) + (vz[2] + vz[3])) + ((vz[4] + vz[5]) + (vz[6] + vz[7]))
    send(vc.at[c], vc.at[c], s_vc, (0,), (0,), core)
    loop(4, lambda i: grad_x(0, ring_y(i)))

    wait_partial(1)

    def value_block(t):
        for s in range(2):
            oown[1, s, t] = summed(1, t, s).astype(bf16)

    loop(4, value_block)
    send(oown.at[1, 1 - xh], orecv.at[1], s_out, (1,), (1,), opposite)

    arrived(vc.at[1 - c], s_vc, (0,))
    vy[y] = vc[0] + vc[1]
    for d in range(1, 4):
        py = ring_y(d)
        send(vy.at[y], vy.at[y], s_vy, (py,), (y,), at_y(py))

    grad_z(1)
    grad_z(0)

    vec_wait(vy, s_vy, y, 4)
    for k in range(4):
        cols = slice(k * DC, (k + 1) * DC)
        ng_ref[:, cols] = vy[k, :, :DC] / gain_ref[:, cols]
    hg_ref[...] = (vy[0, :, DC:] + vy[1, :, DC:]) + (vy[2, :, DC:] + vy[3, :, DC:])
    for kv, ref in ((0, ks_ref), (1, vs_ref)):
        arrived(orecv.at[kv], s_out, (kv,))
        ref[:, xh] = oown[kv, xh]
        ref[:, 1 - xh] = orecv[kv]
    for kv, ref in ((0, dwk_ref), (1, dwv_ref)):

        @pl.when(moved)
        def _():
            arrived(finr.at[kv], s_dp, (kv,))

        ref[...] = finr[kv]

    @pl.when(moved)
    def _():
        for kv, ref in ((0, wk_ref), (1, wv_ref)):
            sent(ref, s_w0, (kv,))
            sent(fin.at[kv], s_dp, (kv,))

    for kv, ref in ((0, kcot_ref), (1, vcot_ref)):
        sent(ref.at[:, 1 - xh], s_cot, (kv,))
        sent(oown.at[kv, 1 - xh], s_out, (kv,))

    def sent_z(i):
        pz = ring_z(i + 1)
        for kv in range(2):
            sent(w_own(kv), s_wz, (kv, pz))
            sent(zs.at[kv, lax.div(pz, 2), lax.rem(pz, 2)], s_dz, (kv, pz))
        sent(vz.at[z], s_vz, (pz,))

    loop(7, sent_z)

    def sent_x(i):
        px = ring_x(i + 1)
        sent(vx.at[x], s_vx, (px,))
        for kv in range(2):
            for h in range(4):
                sent(w.at[kv, h, xh, :, xl, c], s_wx, (kv, h, px))
                sent(dw.at[kv, h, c, px], s_dx, (kv, h, px))

    loop(3, sent_x)

    def sent_core(h):
        for kv in range(2):
            sent(w.at[kv, h, :, :, :, c], s_wc, (kv, h))
            sent(dw.at[kv, h, 1 - c], s_dc, (kv, h))

    loop(4, sent_core)
    sent(vc.at[c], s_vc, (0,))

    def sent_y(i):
        py = ring_y(i + 1)
        sent(hid.at[py], s_hid, (py,))
        sent(cb.at[1, y], s_va, (py,))
        for t in range(4):
            sent(cb.at[0, y, :, t], s_ka, (py, t))
        for kv in range(2):
            sent(psend.at[kv, py], s_p, (kv, py))
        sent(dhs.at[py], s_dh, (py,))
        sent(vy.at[y], s_vy, (py,))

    loop(3, sent_y)


def on_device(
    inputs, norm_gain, key_weight, value_weight, head_gain, key_cotangent, value_cotangent
):
    def sems(*shape):
        return pltpu.SemaphoreType.DMA((2,) + shape)

    scratch = [
        pltpu.VMEM((4, T, DC), bf16),
        pltpu.VMEM((4, T, DC), bf16),
        pltpu.VMEM((DC, 4 * T), bf16),
        pltpu.VMEM((2, 4, 2, 2, 2, 2, R, H), bf16),
        pltpu.VMEM((2, 4, 4 * T, 2 * H), bf16),
        pltpu.VMEM((2, 4, 4 * T, 2 * H), bf16),
        pltpu.VMEM((2, 4 * T, 2 * H), f32),
        pltpu.VMEM((2, 4, T, H), bf16),
        pltpu.VMEM((2, 4, 2, 4, T, H), bf16),
        pltpu.VMEM((2, 2, 4, T, H), bf16),
        pltpu.VMEM((2, 4, T, H), bf16),
        pltpu.VMEM((4, T, DC), f32),
        pltpu.VMEM((4, T, DC), bf16),
        pltpu.VMEM((4, T, DC), bf16),
        pltpu.VMEM((2, 4, 2, 4, 2, R, H), bf16),
        pltpu.VMEM((2, 4, 4, 2, R, H), bf16),
        pltpu.VMEM((2, 4, 4, 2, R, H), bf16),
        pltpu.VMEM((2, 4, 2, R, H), bf16),
        pltpu.VMEM((2, 8, R, H), bf16),
        pltpu.VMEM((2, R, H), f32),
        pltpu.VMEM((2, R, H), f32),
        pltpu.VMEM((4, 1, DC + H), f32),
        pltpu.VMEM((8, 1, DC + H), f32),
        pltpu.VMEM((2, 1, DC + H), f32),
        pltpu.VMEM((4, 1, DC + H), f32),
        pltpu.VMEM((T, 128), f32),
        sems(2),
        sems(2, 8),
        sems(2, 4, 4),
        sems(2, 4),
        sems(4),
        sems(2),
        sems(4),
        sems(4, 4),
        sems(2, 4),
        sems(2),
        sems(4),
        sems(2, 4),
        sems(2, 4, 4),
        sems(2, 8),
        sems(2),
        sems(4),
        sems(8),
        sems(1),
        sems(4),
    ]
    outs = (
        jax.ShapeDtypeStruct((4, 2, T, H), bf16),
        jax.ShapeDtypeStruct((4, 2, T, H), bf16),
        jax.ShapeDtypeStruct((T, D), bf16),
        jax.ShapeDtypeStruct((R, H), f32),
        jax.ShapeDtypeStruct((R, H), f32),
        jax.ShapeDtypeStruct((1, D), f32),
        jax.ShapeDtypeStruct((1, H), f32),
    )
    vmem = pl.BlockSpec(memory_space=pltpu.VMEM)
    ks, vs, ig, dwk, dwv, ng, hg = pl.pallas_call(
        kernel,
        out_shape=outs,
        in_specs=[vmem] * 7,
        out_specs=(vmem,) * 7,
        scratch_shapes=scratch,
        compiler_params=pltpu.CompilerParams(
            collective_id=0, has_side_effects=True, vmem_limit_bytes=60 * 1024 * 1024
        ),
        cost_estimate=pl.CostEstimate(
            flops=6 * 512 * DC * 2048, bytes_accessed=6 * 1024 * 1024, transcendentals=0
        ),
    )(
        inputs,
        norm_gain.astype(f32).reshape(1, D),
        key_weight,
        value_weight,
        head_gain.astype(f32).reshape(1, H),
        key_cotangent.reshape(4, 2, T, H),
        value_cotangent.reshape(4, 2, T, H),
    )
    return (
        ks.reshape(8 * T, H),
        vs.reshape(8 * T, H),
        ig,
        dwk,
        dwv,
        ng.reshape(D),
        hg.reshape(H),
    )


def solution(mesh):
    in_specs = (
        P(("dp", "tensor"), None),
        P(),
        P("dp", "tensor"),
        P("dp", "tensor"),
        P(),
        P("dp", "tensor"),
        P("dp", "tensor"),
    )
    out_specs = (
        P("dp", "tensor"),
        P("dp", "tensor"),
        P(("dp", "tensor"), None),
        P("dp", "tensor"),
        P("dp", "tensor"),
        P(),
        P(),
    )
    return jax.shard_map(
        on_device, mesh=mesh, in_specs=in_specs, out_specs=out_specs, check_vma=False
    )
```

```python
import jax
import jax.numpy as jnp
from jax import lax
from jax.experimental import pallas as pl
from jax.experimental.pallas import tpu as pltpu
from jax.sharding import PartitionSpec as P

eps = 1e-06
MESH = pl.DeviceIdType.MESH
T = 128
D = 5120
DC = 1280
R = 160
RA = 128
H = 128
bf16 = jnp.bfloat16
f32 = jnp.float32


def dot(a, b):
    return jnp.dot(a, b, preferred_element_type=f32)


def dot_nt(a, b):
    return lax.dot_general(a, b, (((1,), (1,)), ((), ())), preferred_element_type=f32)


def loop(n, body):
    def step(i, carry):
        body(i)
        return carry

    lax.fori_loop(0, n, step, 0)


def kernel(
    x_hbm,
    gain_ref,
    wk_ref,
    wv_ref,
    hgain_ref,
    kcot_ref,
    vcot_ref,
    ks_ref,
    vs_ref,
    ig_ref,
    dwk_ref,
    dwv_ref,
    ng_ref,
    hg_ref,
    hid,
    hc,
    hct,
    w,
    psend,
    precv,
    own,
    cot,
    cb,
    oown,
    orecv,
    dhv,
    dhs,
    dhr,
    dw,
    dwc,
    dwx,
    zs,
    zr,
    fin,
    finr,
    vx,
    vz,
    vc,
    vy,
    rinv_s,
    gain_s,
    x_ref,
    s_w0,
    s_wz,
    s_wx,
    s_wy,
    s_wr,
    s_wc,
    s_hid,
    s_cot,
    s_ag,
    s_p,
    s_out,
    s_dh,
    s_dc,
    s_dx,
    s_dz,
    s_dp,
    s_vx,
    s_vz,
    s_vc,
    s_vy,
    s_in,
):
    dp, tn = lax.axis_index("dp"), lax.axis_index("tensor")
    z, xl, c = lax.div(dp, 4), lax.rem(lax.div(dp, 2), 2), lax.rem(dp, 2)
    y, xh = lax.div(tn, 2), lax.rem(tn, 2)
    x = 2 * xh + xl
    zh, ze = lax.div(z, 2), lax.rem(z, 2)

    def device(x, y, z, c):
        return (z * 4 + lax.rem(x, 2) * 2 + c, y * 2 + lax.div(x, 2))

    def ring_x(d):
        return lax.rem(x + d, 4)

    def ring_y(d):
        return lax.rem(y + d, 4)

    def ring_z(d):
        return lax.rem(z + d, 8)

    def at_x(px):
        return device(px, y, z, c)

    def at_y(py):
        return device(x, py, z, c)

    def at_z(pz):
        return device(x, y, pz, c)

    core = device(x, y, z, 1 - c)
    opposite = device(2 * (1 - xh) + xl, y, z, c)
    partner = device(x, zh, 2 * y + ze, c)
    moved = zh != y

    def send(src, dst, sems, s_at, r_at, to):
        pltpu.make_async_remote_copy(
            src_ref=src,
            dst_ref=dst,
            send_sem=sems.at[(0,) + s_at],
            recv_sem=sems.at[(1,) + r_at],
            device_id=to,
            device_id_type=MESH,
        ).start()

    def copy_of(ref, sems, at):
        return pltpu.make_async_remote_copy(
            src_ref=ref,
            dst_ref=ref,
            send_sem=sems.at[(0,) + at],
            recv_sem=sems.at[(1,) + at],
            device_id=core,
            device_id_type=MESH,
        )

    def arrived(ref, sems, at):
        copy_of(ref, sems, at).wait_recv()

    def sent(ref, sems, at):
        copy_of(ref, sems, at).wait_send()

    barrier = pltpu.get_barrier_semaphore()

    def hello(to):
        pl.semaphore_signal(barrier, inc=1, device_id=to, device_id_type=MESH)

    for d in range(1, 4):
        hello(at_x(ring_x(d)))
        hello(at_y(ring_y(d)))
    for d in range(1, 8):
        hello(at_z(ring_z(d)))
    hello(core)

    @pl.when(moved)
    def _():
        hello(partner)

    local = [
        pltpu.make_async_copy(x_hbm, x_ref, s_in.at[0]),
        pltpu.make_async_copy(vcot_ref.at[:, xh], cb.at[1, y, xh], s_in.at[1]),
        pltpu.make_async_copy(kcot_ref.at[:, xh], cot.at[xh], s_in.at[2]),
    ]
    for copy in local:
        copy.start()
    for k in range(D // 128):
        gain_s[:, k * 128 : (k + 1) * 128] = gain_ref[k : k + 1, :].astype(f32)

    def w_own(kv):
        return w.at[kv, zh, xh, ze, xl, c]

    @pl.when(jnp.logical_not(moved))
    def _():
        for kv, ref in ((0, wk_ref), (1, wv_ref)):
            w[kv, zh, xh, ze, xl, c] = ref[...]

    pl.semaphore_wait(barrier, jnp.where(moved, 15, 14))

    def w_move(kv):
        @pl.when(moved)
        def _():
            ref = (wk_ref, wv_ref)[kv]
            send(ref, w.at[kv, y, xh, ze, xl, c], s_w0, (kv,), (kv,), partner)

    w_move(0)
    send(vcot_ref.at[:, 1 - xh], cb.at[1, y, xh], s_cot, (1,), (1,), opposite)

    def norm_rows(i):
        rows = pl.ds(pl.multiple_of(i * 16, 16), 16)
        xf = x_ref[rows, :].astype(f32)
        rinv = lax.rsqrt(jnp.mean(xf * xf, axis=-1, keepdims=True) + eps)
        rinv_s[rows, :] = jnp.broadcast_to(rinv, (16, 128))
        hd = (xf * rinv * gain_s[...]).astype(bf16)
        for k in range(4):
            hid[k, rows, :] = hd[:, k * DC : (k + 1) * DC]

    local[0].wait()
    loop(8, norm_rows)
    for d in (1, 3, 2):
        py = ring_y(d)
        send(hid.at[py], hc.at[y], s_hid, (py,), (y,), at_y(py))
    hc[y] = hid[y]
    local[1].wait()
    local[2].wait()


    def moved_in(kv):
        @pl.when(moved)
        def _():
            arrived(w_own(kv), s_w0, (kv,))

    def w_first(kv):
        moved_in(kv)
        part = w.at[kv, zh, xh, ze, xl, c, 0:RA]

        def z_send(i):
            pz = ring_z(i + 1)
            send(part, part, s_wz, (kv, pz), (kv, z), at_z(pz))

        loop(7, z_send)
        rest = w.at[kv, zh, xh, ze, xl, c, RA:R]
        for d in (1, 3, 2):
            px = ring_x(d)
            send(rest, rest, s_wy, (kv, px), (kv, x), at_x(px))

    def w_second(kv):
        for d in range(1, 4):
            px = ring_x(d)
            pxl, pxh = lax.rem(px, 2), lax.div(px, 2)
            arrived(w.at[kv, zh, pxh, ze, pxl, c, RA:R], s_wy, (kv, px))
        part = w.at[kv, zh, :, ze, :, c, RA:R]

        def z_send(i):
            pz = ring_z(i + 1)
            send(part, part, s_wr, (kv, pz), (kv, z), at_z(pz))

        loop(7, z_send)

    def w_x(kv, i):
        h = ring_y(i + 1)

        def wait_z(e):
            pz = 2 * h + e

            @pl.when(pz != z)
            def _():
                arrived(w.at[kv, h, xh, e, xl, c, 0:RA], s_wz, (kv, pz))

        loop(2, wait_z)
        part = w.at[kv, h, xh, :, xl, c, 0:RA]
        for d in (1, 3, 2):
            px = ring_x(d)
            send(part, part, s_wx, (kv, h, px), (kv, h, x), at_x(px))

    def w_core(kv, i):
        h = ring_y(i + 1)

        def wait_x(d):
            px = ring_x(d + 1)
            pxl, pxh = lax.rem(px, 2), lax.div(px, 2)
            arrived(w.at[kv, h, pxh, :, pxl, c, 0:RA], s_wx, (kv, h, px))

        def wait_z(e):
            pz = 2 * h + e

            @pl.when(pz != z)
            def _():
                arrived(w.at[kv, h, :, e, :, c, RA:R], s_wr, (kv, pz))

        loop(3, wait_x)
        loop(2, wait_z)
        part = w.at[kv, h, :, :, :, c]
        send(part, part, s_wc, (kv, h), (kv, h), core)

    w_first(0)
    w_move(1)
    loop(4, lambda i: w_x(0, i))
    w_second(0)
    w_first(1)
    send(kcot_ref.at[:, 1 - xh], cot.at[xh], s_cot, (0,), (0,), opposite)

    def panel(kv, h):
        return jnp.concatenate(
            [w[kv, h, 0].reshape(DC, H), w[kv, h, 1].reshape(DC, H)], axis=1
        )

    def forward(kv, i):
        h = ring_y(i + 1)
        part = dot(hc[...].reshape(4 * T, DC), panel(kv, h))

        @pl.when(h != y)
        def _():
            psend[kv, h] = part.astype(bf16)

        @pl.when(h == y)
        def _():
            own[kv] = part

    def partial_send(kv, d):
        py = ring_y(d)
        send(psend.at[kv, py], precv.at[kv, y], s_p, (kv, py), (kv, y), at_y(py))

    def hidden_wait(d):
        py = ring_y(d + 1)
        arrived(hc.at[py], s_hid, (py,))

    loop(3, hidden_wait)

    def gather(kv):
        for d, slot in ((1, 0), (3, 1)):
            send(cb.at[kv, y], cb.at[kv, y], s_ag, (kv, slot), (kv, slot), at_y(ring_y(d)))

    def gather_near(kv):
        for d, slot in ((3, 0), (1, 1)):
            arrived(cb.at[kv, ring_y(d)], s_ag, (kv, slot))
        for d, to, half, slot in ((3, 1, 0, 2), (1, 3, 2, 3)):
            part = cb.at[kv, ring_y(d), :, half : half + 2]
            send(part, part, s_ag, (kv, slot), (kv, slot), at_y(ring_y(to)))

    def gather_far(kv):
        for half, slot in ((0, 2), (2, 3)):
            arrived(cb.at[kv, ring_y(2), :, half : half + 2], s_ag, (kv, slot))

    arrived(cb.at[1, y, 1 - xh], s_cot, (1,))
    gather(1)
    for k in range(4):
        hct[:, k * T : (k + 1) * T] = hc[k].T

    def key_tile(i):
        h = ring_y(i + 1)
        arrived(w.at[0, h, :, :, :, 1 - c], s_wc, (0, h))
        forward(0, i)

        @pl.when(i < 3)
        def _():
            partial_send(0, i + 1)

    def key_step(i):
        w_core(0, i)

        @pl.when(i > 0)
        def _():
            key_tile(i - 1)

    loop(3, key_step)
    w_second(1)
    loop(4, lambda i: w_x(1, i))
    key_step(3)
    key_tile(3)
    gather_near(1)

    def cots(kv, h):
        return jnp.concatenate(
            [cb[kv, h, 0].reshape(4 * T, H), cb[kv, h, 1].reshape(4 * T, H)], axis=1
        )

    def grad_tile(kv, h):
        g = dot(hct[...], cots(kv, h)).astype(bf16).reshape(2, 2, 2, R, 2 * H)
        for pc in range(2):
            for ph in range(2):
                for pxl in range(2):
                    dw[kv, h, pc, 2 * ph + pxl] = g[:, pxl, pc, :, ph * H : (ph + 1) * H]
        send(dw.at[kv, h, 1 - c], dwc.at[kv, h], s_dc, (kv, h), (kv, h), core)

    def grad_core(kv, h):
        arrived(dwc.at[kv, h], s_dc, (kv, h))
        dw[kv, h, c] = (dw[kv, h, c].astype(f32) + dwc[kv, h].astype(f32)).astype(bf16)
        for d in (1, 3, 2):
            px = ring_x(d)
            send(
                dw.at[kv, h, c, px], dwx.at[kv, h, x], s_dx, (kv, h, px), (kv, h, x), at_x(px)
            )

    def grad_x(kv, h):
        total = dw[kv, h, c, x].astype(f32)
        for d in range(1, 4):
            px = ring_x(d)
            arrived(dwx.at[kv, h, px], s_dx, (kv, h, px))
            total = total + dwx[kv, h, px].astype(f32)
        zs[kv, h] = total.astype(bf16)

        def body(e):
            pz = 2 * h + e

            @pl.when(pz != z)
            def _():
                send(zs.at[kv, h, e], zr.at[kv, z], s_dz, (kv, pz), (kv, z), at_z(pz))

        loop(2, body)

    def grad_z(kv):
        total = zs[kv, zh, ze].astype(f32)
        for d in range(1, 8):
            pz = ring_z(d)
            arrived(zr.at[kv, pz], s_dz, (kv, pz))
            total = total + zr[kv, pz].astype(f32)

        @pl.when(moved)
        def _():
            fin[kv] = total
            send(fin.at[kv], finr.at[kv], s_dp, (kv,), (kv,), partner)

        @pl.when(jnp.logical_not(moved))
        def _():
            finr[kv] = total

    loop(3, lambda i: grad_tile(1, ring_y(i + lax.div(i, 2))))
    loop(3, lambda i: grad_core(1, ring_y(i + lax.div(i, 2))))

    arrived(cot.at[1 - xh], s_cot, (0,))

    def wait_partial(kv):
        def body(d):
            py = ring_y(d + 1)
            arrived(precv.at[kv, py], s_p, (kv, py))

        loop(3, body)

    def summed(kv, t, s):
        rows = pl.ds(pl.multiple_of(t * T, T), T)
        cols = slice(s * H, (s + 1) * H)
        total = own[kv, rows, cols]
        for d in range(1, 4):
            total = total + precv[kv, ring_y(d), rows, cols].astype(f32)
        return total

    wait_partial(0)
    hgain = hgain_ref[...].astype(f32)
    vx[x] = jnp.zeros((1, DC + H), f32)

    def key_block(t):
        for s in range(2):
            key = summed(0, t, s)
            krinv = lax.rsqrt(jnp.mean(key * key, axis=-1, keepdims=True) + eps)
            kn = key * krinv
            oown[0, s, t] = (kn * hgain).astype(bf16)
            ct = cot[s, t].astype(f32)
            back = ct * hgain
            grad = krinv * (back - kn * jnp.mean(back * kn, axis=-1, keepdims=True))
            cb[0, y, s, t] = grad.astype(bf16)
            vx[x, :, DC:] += jnp.sum(ct * kn, axis=0, keepdims=True)

    loop(4, key_block)
    gather(0)
    send(oown.at[0, 1 - xh], orecv.at[0], s_out, (0,), (0,), opposite)

    def back_panel(kv, h, first):
        part = dot_nt(cots(kv, h), panel(kv, h)).reshape(4, T, DC)
        if first:
            dhv[...] = part
        else:
            dhv[...] += part

    gather_far(1)
    grad_tile(1, ring_y(2))
    grad_tile(0, y)
    back_panel(0, y, True)
    grad_core(1, ring_y(2))
    grad_core(0, y)
    loop(4, lambda i: w_core(1, i))
    gather_near(0)

    def value_tile(i):
        h = ring_y(i + 1)
        arrived(w.at[1, h, :, :, :, 1 - c], s_wc, (1, h))
        forward(1, i)

        @pl.when(i < 3)
        def _():
            partial_send(1, i + 1)

    loop(4, value_tile)
    loop(2, lambda i: grad_tile(0, ring_y(2 * i + 1)))
    loop(4, lambda i: back_panel(1, i, False))
    loop(2, lambda i: grad_core(0, ring_y(2 * i + 1)))
    loop(2, lambda i: back_panel(0, ring_y(2 * i + 1), False))
    gather_far(0)

    def hidden_back(i):
        t = ring_y(i + 1)
        far = ring_y(2)
        ct = jnp.concatenate([cb[0, far, 0, t], cb[0, far, 1, t]], axis=1)
        total = dhv[t] + dot_nt(ct, panel(0, far))
        vx[x, :, :DC] += jnp.sum(total * hc[t].astype(f32), axis=0, keepdims=True)

        @pl.when(t != y)
        def _():
            dhs[t] = total.astype(bf16)
            send(dhs.at[t], dhr.at[y], s_dh, (t,), (y,), at_y(t))

        @pl.when(t == y)
        def _():
            dhr[y] = total.astype(bf16)

    loop(4, hidden_back)
    for d in range(1, 4):
        px = ring_x(d)
        send(vx.at[x], vx.at[x], s_vx, (px,), (x,), at_x(px))
    grad_tile(0, ring_y(2))

    grad_core(0, ring_y(2))

    def vec_wait(ref, sems, me, n):
        def body(i):
            p = lax.rem(me + 1 + i, n)
            arrived(ref.at[p], sems, (p,))

        loop(n - 1, body)

    loop(4, lambda i: grad_x(1, ring_y(i)))
    vec_wait(vx, s_vx, x, 4)
    vz[z] = (vx[0] + vx[1]) + (vx[2] + vx[3])

    def vz_send(i):
        pz = ring_z(i + 1)
        send(vz.at[z], vz.at[z], s_vz, (pz,), (z,), at_z(pz))

    loop(7, vz_send)
    grad_x(0, y)
    loop(2, lambda i: grad_x(0, ring_y(2 * i + 1)))
    grad_z(1)
    vec_wait(vz, s_vz, z, 8)
    vc[c] = ((vz[0] + vz[1]) + (vz[2] + vz[3])) + ((vz[4] + vz[5]) + (vz[6] + vz[7]))
    send(vc.at[c], vc.at[c], s_vc, (0,), (0,), core)
    grad_x(0, ring_y(2))
    arrived(vc.at[1 - c], s_vc, (0,))
    vy[y] = vc[0] + vc[1]
    for d in range(1, 4):
        py = ring_y(d)
        send(vy.at[y], vy.at[y], s_vy, (py,), (y,), at_y(py))

    wait_partial(1)

    def value_block(t):
        for s in range(2):
            oown[1, s, t] = summed(1, t, s).astype(bf16)

    loop(4, value_block)
    send(oown.at[1, 1 - xh], orecv.at[1], s_out, (1,), (1,), opposite)

    def dh_wait(d):
        py = ring_y(d + 1)
        arrived(dhr.at[py], s_dh, (py,))

    loop(3, dh_wait)

    def input_rows(i):
        rows = pl.ds(pl.multiple_of(i * 16, 16), 16)
        rinv = rinv_s[rows, 0:1]
        mean = jnp.zeros((16, 1), f32)
        for k in range(4):
            cols = slice(k * DC, (k + 1) * DC)
            normed = x_ref[rows, cols].astype(f32) * rinv
            back = dhr[k, rows, :].astype(f32) * gain_s[:, cols]
            mean = mean + jnp.sum(back * normed, axis=-1, keepdims=True)
        mean = mean * (1.0 / D)
        for k in range(4):
            cols = slice(k * DC, (k + 1) * DC)
            normed = x_ref[rows, cols].astype(f32) * rinv
            back = dhr[k, rows, :].astype(f32) * gain_s[:, cols]
            ig_ref[rows, cols] = (rinv * (back - normed * mean)).astype(bf16)

    loop(8, input_rows)
    grad_z(0)

    vec_wait(vy, s_vy, y, 4)
    for k in range(4):
        cols = slice(k * DC, (k + 1) * DC)
        ng_ref[:, cols] = vy[k, :, :DC] / gain_s[:, cols]
    hg_ref[...] = (vy[0, :, DC:] + vy[1, :, DC:]) + (vy[2, :, DC:] + vy[3, :, DC:])
    for kv, ref in ((0, ks_ref), (1, vs_ref)):
        arrived(orecv.at[kv], s_out, (kv,))
        ref[:, xh] = oown[kv, xh]
        ref[:, 1 - xh] = orecv[kv]
    for kv, ref in ((0, dwk_ref), (1, dwv_ref)):

        @pl.when(moved)
        def _():
            arrived(finr.at[kv], s_dp, (kv,))

        ref[...] = finr[kv]

    @pl.when(moved)
    def _():
        for kv, ref in ((0, wk_ref), (1, wv_ref)):
            sent(ref, s_w0, (kv,))
            sent(fin.at[kv], s_dp, (kv,))

    for kv, ref in ((0, kcot_ref), (1, vcot_ref)):
        sent(ref.at[:, 1 - xh], s_cot, (kv,))
        sent(oown.at[kv, 1 - xh], s_out, (kv,))

    def sent_z(i):
        pz = ring_z(i + 1)
        for kv in range(2):
            sent(w.at[kv, zh, xh, ze, xl, c, 0:RA], s_wz, (kv, pz))
            sent(w.at[kv, zh, :, ze, :, c, RA:R], s_wr, (kv, pz))
            sent(zs.at[kv, lax.div(pz, 2), lax.rem(pz, 2)], s_dz, (kv, pz))
        sent(vz.at[z], s_vz, (pz,))

    loop(7, sent_z)

    def sent_x(i):
        px = ring_x(i + 1)
        sent(vx.at[x], s_vx, (px,))
        for kv in range(2):
            sent(w.at[kv, zh, xh, ze, xl, c, RA:R], s_wy, (kv, px))
            for h in range(4):
                sent(w.at[kv, h, xh, :, xl, c, 0:RA], s_wx, (kv, h, px))
                sent(dw.at[kv, h, c, px], s_dx, (kv, h, px))

    loop(3, sent_x)

    def sent_core(h):
        for kv in range(2):
            sent(w.at[kv, h, :, :, :, c], s_wc, (kv, h))
            sent(dw.at[kv, h, 1 - c], s_dc, (kv, h))

    loop(4, sent_core)
    sent(vc.at[c], s_vc, (0,))
    for kv in range(2):
        for slot in range(2):
            sent(cb.at[kv, y], s_ag, (kv, slot))
            sent(cb.at[kv, y, :, 0:2], s_ag, (kv, slot + 2))

    def sent_y(i):
        py = ring_y(i + 1)
        sent(hid.at[py], s_hid, (py,))
        for kv in range(2):
            sent(psend.at[kv, py], s_p, (kv, py))
        sent(dhs.at[py], s_dh, (py,))
        sent(vy.at[y], s_vy, (py,))

    loop(3, sent_y)


def hand_out(*refs):
    ins, outs, held, sems = refs[:7], refs[7:14], refs[14:21], refs[21]
    first = [pltpu.make_async_copy(ins[i], held[i], sems.at[0, i]) for i in range(7)]
    last = [pltpu.make_async_copy(held[i], outs[i], sems.at[1, i]) for i in range(7)]
    for copy in first:
        copy.start()
    for i in range(7):
        first[i].wait()
        last[i].start()
    for copy in last:
        copy.wait()


def on_device(
    inputs, norm_gain, key_weight, value_weight, head_gain, key_cotangent, value_cotangent
):
    def sems(*shape):
        return pltpu.SemaphoreType.DMA((2,) + shape)

    scratch = [
        pltpu.VMEM((4, T, DC), bf16),
        pltpu.VMEM((4, T, DC), bf16),
        pltpu.VMEM((DC, 4 * T), bf16),
        pltpu.VMEM((2, 4, 2, 2, 2, 2, R, H), bf16),
        pltpu.VMEM((2, 4, 4 * T, 2 * H), bf16),
        pltpu.VMEM((2, 4, 4 * T, 2 * H), bf16),
        pltpu.VMEM((2, 4 * T, 2 * H), f32),
        pltpu.VMEM((2, 4, T, H), bf16),
        pltpu.VMEM((2, 4, 2, 4, T, H), bf16),
        pltpu.VMEM((2, 2, 4, T, H), bf16),
        pltpu.VMEM((2, 4, T, H), bf16),
        pltpu.VMEM((4, T, DC), f32),
        pltpu.VMEM((4, T, DC), bf16),
        pltpu.VMEM((4, T, DC), bf16),
        pltpu.VMEM((2, 4, 2, 4, 2, R, H), bf16),
        pltpu.VMEM((2, 4, 4, 2, R, H), bf16),
        pltpu.VMEM((2, 4, 4, 2, R, H), bf16),
        pltpu.VMEM((2, 4, 2, R, H), bf16),
        pltpu.VMEM((2, 8, R, H), bf16),
        pltpu.VMEM((2, R, H), f32),
        pltpu.VMEM((2, R, H), f32),
        pltpu.VMEM((4, 1, DC + H), f32),
        pltpu.VMEM((8, 1, DC + H), f32),
        pltpu.VMEM((2, 1, DC + H), f32),
        pltpu.VMEM((4, 1, DC + H), f32),
        pltpu.VMEM((T, 128), f32),
        pltpu.VMEM((1, D), f32),
        pltpu.VMEM((T, D), bf16),
        sems(2),
        sems(2, 8),
        sems(2, 4, 4),
        sems(2, 4),
        sems(2, 8),
        sems(2, 4),
        sems(4),
        sems(2),
        sems(2, 4),
        sems(2, 4),
        sems(2),
        sems(4),
        sems(2, 4),
        sems(2, 4, 4),
        sems(2, 8),
        sems(2),
        sems(4),
        sems(8),
        sems(1),
        sems(4),
        pltpu.SemaphoreType.DMA((3,)),
    ]
    outs = (
        jax.ShapeDtypeStruct((4, 2, T, H), bf16),
        jax.ShapeDtypeStruct((4, 2, T, H), bf16),
        jax.ShapeDtypeStruct((T, D), bf16),
        jax.ShapeDtypeStruct((R, H), f32),
        jax.ShapeDtypeStruct((R, H), f32),
        jax.ShapeDtypeStruct((1, D), f32),
        jax.ShapeDtypeStruct((1, H), f32),
    )
    vmem = pl.BlockSpec(memory_space=pltpu.VMEM)
    anywhere = pl.BlockSpec(memory_space=pl.ANY)
    results = pl.pallas_call(
        kernel,
        out_shape=outs,
        in_specs=[anywhere, vmem, vmem, vmem, vmem, anywhere, anywhere],
        out_specs=(vmem,) * 7,
        scratch_shapes=scratch,
        compiler_params=pltpu.CompilerParams(
            collective_id=0, has_side_effects=True, vmem_limit_bytes=60 * 1024 * 1024
        ),
        cost_estimate=pl.CostEstimate(
            flops=6 * 512 * DC * 2048, bytes_accessed=6 * 1024 * 1024, transcendentals=0
        ),
    )(
        inputs,
        norm_gain.reshape(D // 128, 128),
        key_weight,
        value_weight,
        head_gain.reshape(1, H),
        key_cotangent.reshape(4, 2, T, H),
        value_cotangent.reshape(4, 2, T, H),
    )
    ks, vs, ig, dwk, dwv, ng, hg = pl.pallas_call(
        hand_out,
        out_shape=outs,
        in_specs=[pl.BlockSpec(memory_space=pl.ANY)] * 7,
        out_specs=(pl.BlockSpec(memory_space=pl.ANY),) * 7,
        scratch_shapes=[pltpu.VMEM(o.shape, o.dtype) for o in outs]
        + [pltpu.SemaphoreType.DMA((2, 7))],
        compiler_params=pltpu.CompilerParams(vmem_limit_bytes=60 * 1024 * 1024),
    )(*results)
    return (
        ks.reshape(8 * T, H),
        vs.reshape(8 * T, H),
        ig,
        dwk,
        dwv,
        ng.reshape(D),
        hg.reshape(H),
    )


def solution(mesh):
    in_specs = (
        P(("dp", "tensor"), None),
        P(),
        P("dp", "tensor"),
        P("dp", "tensor"),
        P(),
        P("dp", "tensor"),
        P("dp", "tensor"),
    )
    out_specs = (
        P("dp", "tensor"),
        P("dp", "tensor"),
        P(("dp", "tensor"), None),
        P("dp", "tensor"),
        P("dp", "tensor"),
        P(),
        P(),
    )
    return jax.shard_map(
        on_device, mesh=mesh, in_specs=in_specs, out_specs=out_specs, check_vma=False
    )
```

```python
import jax
import jax.numpy as jnp
from jax import lax
from jax.experimental import pallas as pl
from jax.experimental.pallas import tpu as pltpu
from jax.sharding import PartitionSpec as P

eps = 1e-06
MESH = pl.DeviceIdType.MESH
T = 128
D = 5120
DC = 1280
R = 160
RA = 112
H = 128
bf16 = jnp.bfloat16
f32 = jnp.float32


def dot(a, b):
    return jnp.dot(a, b, preferred_element_type=f32)


def dot_nt(a, b):
    return lax.dot_general(a, b, (((1,), (1,)), ((), ())), preferred_element_type=f32)


def loop(n, body):
    def step(i, carry):
        body(i)
        return carry

    lax.fori_loop(0, n, step, 0)


def kernel(
    x_hbm,
    gain_ref,
    wk_ref,
    wv_ref,
    hgain_ref,
    kcot_ref,
    vcot_ref,
    ks_ref,
    vs_ref,
    ig_ref,
    dwk_ref,
    dwv_ref,
    ng_ref,
    hg_ref,
    hid,
    hc,
    hct,
    w,
    psend,
    precv,
    pfar,
    own,
    cot,
    cb,
    oown,
    orecv,
    dhv,
    dhs,
    dhr,
    dw,
    dwc,
    dwx,
    dwf,
    dwd,
    zs,
    zr,
    fin,
    finr,
    vx,
    vz,
    vc,
    vy,
    rinv_s,
    gain_s,
    x_ref,
    s_w0,
    s_wz,
    s_wx,
    s_wy,
    s_wr,
    s_wc,
    s_hid,
    s_cot,
    s_ag,
    s_p,
    s_pf,
    s_pn,
    s_out,
    s_dh,
    s_dc,
    s_dx,
    s_df,
    s_dz,
    s_dp,
    s_vx,
    s_vz,
    s_vc,
    s_vy,
    s_in,
):
    dp, tn = lax.axis_index("dp"), lax.axis_index("tensor")
    z, xl, c = lax.div(dp, 4), lax.rem(lax.div(dp, 2), 2), lax.rem(dp, 2)
    y, xh = lax.div(tn, 2), lax.rem(tn, 2)
    x = 2 * xh + xl
    zh, ze = lax.div(z, 2), lax.rem(z, 2)

    def device(x, y, z, c):
        return (z * 4 + lax.rem(x, 2) * 2 + c, y * 2 + lax.div(x, 2))

    def ring_x(d):
        return lax.rem(x + d, 4)

    def ring_y(d):
        return lax.rem(y + d, 4)

    def ring_z(d):
        return lax.rem(z + d, 8)

    def at_x(px):
        return device(px, y, z, c)

    def at_y(py):
        return device(x, py, z, c)

    def at_z(pz):
        return device(x, y, pz, c)

    core = device(x, y, z, 1 - c)
    opposite = device(2 * (1 - xh) + xl, y, z, c)
    partner = device(x, zh, 2 * y + ze, c)
    moved = zh != y

    def send(src, dst, sems, s_at, r_at, to):
        pltpu.make_async_remote_copy(
            src_ref=src,
            dst_ref=dst,
            send_sem=sems.at[(0,) + s_at],
            recv_sem=sems.at[(1,) + r_at],
            device_id=to,
            device_id_type=MESH,
        ).start()

    def copy_of(ref, sems, at):
        return pltpu.make_async_remote_copy(
            src_ref=ref,
            dst_ref=ref,
            send_sem=sems.at[(0,) + at],
            recv_sem=sems.at[(1,) + at],
            device_id=core,
            device_id_type=MESH,
        )

    def arrived(ref, sems, at):
        copy_of(ref, sems, at).wait_recv()

    def sent(ref, sems, at):
        copy_of(ref, sems, at).wait_send()

    barrier = pltpu.get_barrier_semaphore()

    def hello(to):
        pl.semaphore_signal(barrier, inc=1, device_id=to, device_id_type=MESH)

    for d in range(1, 4):
        hello(at_x(ring_x(d)))
        hello(at_y(ring_y(d)))
    for d in range(1, 8):
        hello(at_z(ring_z(d)))
    hello(core)

    @pl.when(moved)
    def _():
        hello(partner)

    local = [
        pltpu.make_async_copy(x_hbm, x_ref, s_in.at[0]),
        pltpu.make_async_copy(vcot_ref.at[:, xh], cb.at[1, y, xh], s_in.at[1]),
        pltpu.make_async_copy(kcot_ref.at[:, xh], cot.at[xh], s_in.at[2]),
    ]
    for copy in local:
        copy.start()
    for k in range(D // 128):
        gain_s[:, k * 128 : (k + 1) * 128] = gain_ref[k : k + 1, :].astype(f32)

    def w_own(kv):
        return w.at[kv, zh, xh, ze, xl, c]

    @pl.when(jnp.logical_not(moved))
    def _():
        for kv, ref in ((0, wk_ref), (1, wv_ref)):
            w[kv, zh, xh, ze, xl, c] = ref[...]

    pl.semaphore_wait(barrier, jnp.where(moved, 15, 14))

    def w_move(kv):
        @pl.when(moved)
        def _():
            ref = (wk_ref, wv_ref)[kv]
            send(ref, w.at[kv, y, xh, ze, xl, c], s_w0, (kv,), (kv,), partner)

    w_move(0)
    send(vcot_ref.at[:, 1 - xh], cb.at[1, y, xh], s_cot, (1,), (1,), opposite)

    def norm_rows(i):
        rows = pl.ds(pl.multiple_of(i * 16, 16), 16)
        xf = x_ref[rows, :].astype(f32)
        rinv = lax.rsqrt(jnp.mean(xf * xf, axis=-1, keepdims=True) + eps)
        rinv_s[rows, :] = jnp.broadcast_to(rinv, (16, 128))
        hd = (xf * rinv * gain_s[...]).astype(bf16)
        for k in range(4):
            hid[k, rows, :] = hd[:, k * DC : (k + 1) * DC]

    local[0].wait()
    loop(8, norm_rows)
    for d in (1, 3, 2):
        py = ring_y(d)
        send(hid.at[py], hc.at[y], s_hid, (py,), (y,), at_y(py))
    hc[y] = hid[y]
    local[1].wait()
    local[2].wait()


    def moved_in(kv):
        @pl.when(moved)
        def _():
            arrived(w_own(kv), s_w0, (kv,))

    def w_first(kv):
        moved_in(kv)
        part = w.at[kv, zh, xh, ze, xl, c, 0:RA]

        def z_send(i):
            pz = ring_z(i + 1)
            send(part, part, s_wz, (kv, pz), (kv, z), at_z(pz))

        loop(7, z_send)
        rest = w.at[kv, zh, xh, ze, xl, c, RA:R]
        for d in (1, 3, 2):
            px = ring_x(d)
            send(rest, rest, s_wy, (kv, px), (kv, x), at_x(px))

    def w_second(kv):
        for d in range(1, 4):
            px = ring_x(d)
            pxl, pxh = lax.rem(px, 2), lax.div(px, 2)
            arrived(w.at[kv, zh, pxh, ze, pxl, c, RA:R], s_wy, (kv, px))
        part = w.at[kv, zh, :, ze, :, c, RA:R]

        def z_send(i):
            pz = ring_z(i + 1)
            send(part, part, s_wr, (kv, pz), (kv, z), at_z(pz))

        loop(7, z_send)

    def w_x(kv, i):
        h = ring_y(i + 1)

        def wait_z(e):
            pz = 2 * h + e

            @pl.when(pz != z)
            def _():
                arrived(w.at[kv, h, xh, e, xl, c, 0:RA], s_wz, (kv, pz))

        loop(2, wait_z)
        part = w.at[kv, h, xh, :, xl, c, 0:RA]
        for d, slot in ((1, 0), (3, 1)):
            send(part, part, s_wx, (kv, h, slot), (kv, h, slot), at_x(ring_x(d)))

    def of_x(kv, h, px):
        return w.at[kv, h, lax.div(px, 2), :, lax.rem(px, 2), c, 0:RA]

    def far_x(kv, h, px, e):
        return w.at[kv, h, lax.div(px, 2), e, lax.rem(px, 2), c, 0:RA]

    def w_on(kv, i):
        h = ring_y(i + 1)
        for d, slot in ((3, 0), (1, 1)):
            arrived(of_x(kv, h, ring_x(d)), s_wx, (kv, h, slot))
        for d, to, e in ((3, 1, 0), (1, 3, 1)):
            part = far_x(kv, h, ring_x(d), e)
            send(part, part, s_wx, (kv, h, 2 + e), (kv, h, 2 + e), at_x(ring_x(to)))

    def w_core(kv, i):
        h = ring_y(i + 1)
        for e in range(2):
            arrived(far_x(kv, h, ring_x(2), e), s_wx, (kv, h, 2 + e))

        def wait_z(e):
            pz = 2 * h + e

            @pl.when(pz != z)
            def _():
                arrived(w.at[kv, h, :, e, :, c, RA:R], s_wr, (kv, pz))

        loop(2, wait_z)
        part = w.at[kv, h, :, :, :, c]
        send(part, part, s_wc, (kv, h), (kv, h), core)

    w_first(0)
    w_move(1)
    loop(4, lambda i: w_x(0, i))
    w_second(0)
    w_first(1)
    loop(4, lambda i: w_on(0, i))
    send(kcot_ref.at[:, 1 - xh], cot.at[xh], s_cot, (0,), (0,), opposite)

    def panel(kv, h):
        return jnp.concatenate(
            [w[kv, h, 0].reshape(DC, H), w[kv, h, 1].reshape(DC, H)], axis=1
        )

    def forward(kv, i):
        h = ring_y(i + 1)
        part = dot(hc[...].reshape(4 * T, DC), panel(kv, h))

        @pl.when(h != y)
        def _():
            psend[kv, h] = part.astype(bf16)

        @pl.when(h == y)
        def _():
            own[kv] = part

    def partial_send(kv, d):
        py = ring_y(d)
        send(psend.at[kv, py], precv.at[kv, y], s_p, (kv, py), (kv, y), at_y(py))

    def halves(ref, half):
        return ref.at[half * 2 * T : (half + 1) * 2 * T]

    def far_send():
        for d, half in ((1, 0), (3, 1)):
            part = halves(psend.at[1, ring_y(2)], half)
            send(part, pfar.at[half], s_pf, (half,), (half,), at_y(ring_y(d)))

    def near_send(d, slot, half):
        src = halves(psend.at[1, ring_y(d)], half)
        dst = halves(precv.at[1, slot], half)
        send(src, dst, s_pn, (slot, half), (slot, half), at_y(ring_y(d)))

    def near_added():
        for d, slot in ((1, 0), (3, 1)):
            arrived(pfar.at[slot], s_pf, (slot,))
            rows = slice(slot * 2 * T, (slot + 1) * 2 * T)
            total = psend[1, ring_y(d), rows].astype(f32) + pfar[slot].astype(f32)
            psend[1, ring_y(d), rows] = total.astype(bf16)
            near_send(d, slot, slot)

    def hidden_wait(d):
        py = ring_y(d + 1)
        arrived(hc.at[py], s_hid, (py,))

    loop(3, hidden_wait)

    def gather(kv):
        for d, slot in ((1, 0), (3, 1)):
            send(cb.at[kv, y], cb.at[kv, y], s_ag, (kv, slot), (kv, slot), at_y(ring_y(d)))

    def gather_near(kv):
        for d, slot in ((3, 0), (1, 1)):
            arrived(cb.at[kv, ring_y(d)], s_ag, (kv, slot))
        for d, to, half, slot in ((3, 1, 0, 2), (1, 3, 2, 3)):
            part = cb.at[kv, ring_y(d), :, half : half + 2]
            send(part, part, s_ag, (kv, slot), (kv, slot), at_y(ring_y(to)))

    def gather_far(kv):
        for half, slot in ((0, 2), (2, 3)):
            arrived(cb.at[kv, ring_y(2), :, half : half + 2], s_ag, (kv, slot))

    arrived(cb.at[1, y, 1 - xh], s_cot, (1,))
    gather(1)
    for k in range(4):
        hct[:, k * T : (k + 1) * T] = hc[k].T

    def key_tile(i):
        h = ring_y(i + 1)
        arrived(w.at[0, h, :, :, :, 1 - c], s_wc, (0, h))
        forward(0, i)

        @pl.when(i < 3)
        def _():
            partial_send(0, i + 1)

    def key_step(i):
        w_core(0, i)

        @pl.when(i > 0)
        def _():
            key_tile(i - 1)

    loop(4, key_step)
    key_tile(3)
    gather_near(1)
    w_second(1)
    loop(4, lambda i: w_x(1, i))

    def cots(kv, h):
        return jnp.concatenate(
            [cb[kv, h, 0].reshape(4 * T, H), cb[kv, h, 1].reshape(4 * T, H)], axis=1
        )

    def grad_tile(kv, h):
        g = dot(hct[...], cots(kv, h)).astype(bf16).reshape(2, 2, 2, R, 2 * H)
        for pc in range(2):
            for ph in range(2):
                for pxl in range(2):
                    dw[kv, h, pc, 2 * ph + pxl] = g[:, pxl, pc, :, ph * H : (ph + 1) * H]
        send(dw.at[kv, h, 1 - c], dwc.at[kv, h], s_dc, (kv, h), (kv, h), core)

    def grad_near(kv, h, d, slot, e):
        at = (kv, h, slot, e)
        src, dst = dw.at[kv, h, c, ring_x(d), e], dwx.at[kv, h, slot, e]
        send(src, dst, s_dx, at, at, at_x(ring_x(d)))

    def grad_core(kv, h):
        arrived(dwc.at[kv, h], s_dc, (kv, h))
        dw[kv, h, c] = (dw[kv, h, c].astype(f32) + dwc[kv, h].astype(f32)).astype(bf16)
        for d, e in ((1, 0), (3, 1)):
            part = dw.at[kv, h, c, ring_x(2), e]
            send(part, dwf.at[kv, h, e], s_df, (kv, h, e), (kv, h, e), at_x(ring_x(d)))
        grad_near(kv, h, 1, 0, 1)
        grad_near(kv, h, 3, 1, 0)

    def grad_last(h):
        arrived(dwc.at[0, h], s_dc, (0, h))
        dw[0, h, c] = (dw[0, h, c].astype(f32) + dwc[0, h].astype(f32)).astype(bf16)
        for d, slot in ((1, 0), (3, 1)):
            for e in range(2):
                grad_near(0, h, d, slot, e)
        send(dw.at[0, h, c, ring_x(2)], dwd, s_df, (0, h, 0), (0, h, 0), at_x(ring_x(2)))

    def grad_added(kv, h):
        for d, slot in ((1, 0), (3, 1)):
            arrived(dwf.at[kv, h, slot], s_df, (kv, h, slot))
            mine = dw[kv, h, c, ring_x(d), slot].astype(f32)
            total = mine + dwf[kv, h, slot].astype(f32)
            dw[kv, h, c, ring_x(d), slot] = total.astype(bf16)
            grad_near(kv, h, d, slot, slot)

    def grad_x(kv, h, last=False):
        total = dw[kv, h, c, x].astype(f32)
        if last:
            arrived(dwd, s_df, (0, h, 0))
            total = total + dwd[...].astype(f32)
        for slot in range(2):
            for e in range(2):
                arrived(dwx.at[kv, h, slot, e], s_dx, (kv, h, slot, e))
            total = total + dwx[kv, h, slot].astype(f32)
        zs[kv, h] = total.astype(bf16)

        def body(e):
            pz = 2 * h + e

            @pl.when(pz != z)
            def _():
                send(zs.at[kv, h, e], zr.at[kv, z], s_dz, (kv, pz), (kv, z), at_z(pz))

        loop(2, body)

    def grad_z(kv):
        total = zs[kv, zh, ze].astype(f32)
        for d in range(1, 8):
            pz = ring_z(d)
            arrived(zr.at[kv, pz], s_dz, (kv, pz))
            total = total + zr[kv, pz].astype(f32)

        @pl.when(moved)
        def _():
            fin[kv] = total
            send(fin.at[kv], finr.at[kv], s_dp, (kv,), (kv,), partner)

        @pl.when(jnp.logical_not(moved))
        def _():
            finr[kv] = total

    loop(3, lambda i: grad_tile(1, ring_y(i + lax.div(i, 2))))
    loop(3, lambda i: grad_core(1, ring_y(i + lax.div(i, 2))))

    arrived(cot.at[1 - xh], s_cot, (0,))

    def wait_partial(d):
        py = ring_y(d + 1)
        arrived(precv.at[0, py], s_p, (0, py))

    def rows_cols(t, s):
        return pl.ds(pl.multiple_of(t * T, T), T), slice(s * H, (s + 1) * H)

    def key_sum(t, s):
        rows, cols = rows_cols(t, s)
        total = own[0, rows, cols]
        for d in range(1, 4):
            total = total + precv[0, ring_y(d), rows, cols].astype(f32)
        return total

    def value_sum(t, s):
        rows, cols = rows_cols(t, s)
        near = precv[1, 0, rows, cols].astype(f32) + precv[1, 1, rows, cols].astype(f32)
        return own[1, rows, cols] + near

    loop(4, lambda i: w_on(1, i))
    loop(3, wait_partial)
    hgain = hgain_ref[...].astype(f32)
    vx[x] = jnp.zeros((1, DC + H), f32)

    def key_block(t):
        for s in range(2):
            key = key_sum(t, s)
            krinv = lax.rsqrt(jnp.mean(key * key, axis=-1, keepdims=True) + eps)
            kn = key * krinv
            oown[0, s, t] = (kn * hgain).astype(bf16)
            ct = cot[s, t].astype(f32)
            back = ct * hgain
            grad = krinv * (back - kn * jnp.mean(back * kn, axis=-1, keepdims=True))
            cb[0, y, s, t] = grad.astype(bf16)
            vx[x, :, DC:] += jnp.sum(ct * kn, axis=0, keepdims=True)

    loop(4, key_block)
    gather(0)
    send(oown.at[0, 1 - xh], orecv.at[0], s_out, (0,), (0,), opposite)

    def back_panel(kv, h, first):
        part = dot_nt(cots(kv, h), panel(kv, h)).reshape(4, T, DC)
        if first:
            dhv[...] = part
        else:
            dhv[...] += part

    loop(3, lambda i: grad_added(1, ring_y(i + lax.div(i, 2))))
    gather_far(1)
    grad_tile(1, ring_y(2))
    grad_tile(0, y)
    loop(4, lambda i: w_core(1, i))
    back_panel(0, y, True)
    grad_core(1, ring_y(2))
    grad_core(0, y)

    def value_tile(i):
        k = jnp.where(i == 0, 1, jnp.where(i == 1, 0, i))
        h = ring_y(k + 1)
        arrived(w.at[1, h, :, :, :, 1 - c], s_wc, (1, h))
        forward(1, k)

        @pl.when(i == 0)
        def _():
            far_send()

        @pl.when(i == 1)
        def _():
            near_send(1, 0, 1)

        @pl.when(i == 2)
        def _():
            near_send(3, 1, 0)

    loop(3, value_tile)
    gather_near(0)
    value_tile(jnp.int32(3))
    loop(3, lambda i: grad_x(1, ring_y(i + lax.div(i, 2))))
    loop(2, lambda i: grad_tile(0, ring_y(2 * i + 1)))
    loop(2, lambda i: grad_core(0, ring_y(2 * i + 1)))
    grad_added(1, ring_y(2))
    grad_added(0, y)
    loop(4, lambda i: back_panel(1, i, False))
    loop(2, lambda i: back_panel(0, ring_y(2 * i + 1), False))
    near_added()
    loop(2, lambda i: grad_added(0, ring_y(2 * i + 1)))
    gather_far(0)

    def hidden_back(i):
        t = ring_y(i + 1)
        far = ring_y(2)
        ct = jnp.concatenate([cb[0, far, 0, t], cb[0, far, 1, t]], axis=1)
        total = dhv[t] + dot_nt(ct, panel(0, far))
        vx[x, :, :DC] += jnp.sum(total * hc[t].astype(f32), axis=0, keepdims=True)

        @pl.when(t != y)
        def _():
            dhs[t] = total.astype(bf16)
            send(dhs.at[t], dhr.at[y], s_dh, (t,), (y,), at_y(t))

        @pl.when(t == y)
        def _():
            dhr[y] = total.astype(bf16)

    loop(4, hidden_back)
    for d in range(1, 4):
        px = ring_x(d)
        send(vx.at[x], vx.at[x], s_vx, (px,), (x,), at_x(px))
    grad_tile(0, ring_y(2))
    grad_last(ring_y(2))
    grad_x(1, ring_y(2))
    grad_x(0, y)

    def vec_wait(ref, sems, me, n):
        def body(i):
            p = lax.rem(me + 1 + i, n)
            arrived(ref.at[p], sems, (p,))

        loop(n - 1, body)

    vec_wait(vx, s_vx, x, 4)
    vz[z] = (vx[0] + vx[1]) + (vx[2] + vx[3])

    def vz_send(i):
        pz = ring_z(i + 1)
        send(vz.at[z], vz.at[z], s_vz, (pz,), (z,), at_z(pz))

    loop(7, vz_send)
    loop(2, lambda i: grad_x(0, ring_y(2 * i + 1)))
    grad_z(1)
    grad_x(0, ring_y(2), True)
    vec_wait(vz, s_vz, z, 8)
    vc[c] = ((vz[0] + vz[1]) + (vz[2] + vz[3])) + ((vz[4] + vz[5]) + (vz[6] + vz[7]))
    send(vc.at[c], vc.at[c], s_vc, (0,), (0,), core)
    grad_z(0)
    arrived(vc.at[1 - c], s_vc, (0,))
    vy[y] = vc[0] + vc[1]
    for d in range(1, 4):
        py = ring_y(d)
        send(vy.at[y], vy.at[y], s_vy, (py,), (y,), at_y(py))

    for slot in range(2):
        for half in range(2):
            arrived(halves(precv.at[1, slot], half), s_pn, (slot, half))

    def value_block(t):
        for s in range(2):
            oown[1, s, t] = value_sum(t, s).astype(bf16)

    loop(4, value_block)
    send(oown.at[1, 1 - xh], orecv.at[1], s_out, (1,), (1,), opposite)

    def dh_wait(d):
        py = ring_y(d + 1)
        arrived(dhr.at[py], s_dh, (py,))

    loop(3, dh_wait)

    def input_rows(i):
        rows = pl.ds(pl.multiple_of(i * 16, 16), 16)
        rinv = rinv_s[rows, 0:1]
        mean = jnp.zeros((16, 1), f32)
        for k in range(4):
            cols = slice(k * DC, (k + 1) * DC)
            normed = x_ref[rows, cols].astype(f32) * rinv
            back = dhr[k, rows, :].astype(f32) * gain_s[:, cols]
            mean = mean + jnp.sum(back * normed, axis=-1, keepdims=True)
        mean = mean * (1.0 / D)
        for k in range(4):
            cols = slice(k * DC, (k + 1) * DC)
            normed = x_ref[rows, cols].astype(f32) * rinv
            back = dhr[k, rows, :].astype(f32) * gain_s[:, cols]
            ig_ref[rows, cols] = (rinv * (back - normed * mean)).astype(bf16)

    loop(8, input_rows)
    vec_wait(vy, s_vy, y, 4)
    for k in range(4):
        cols = slice(k * DC, (k + 1) * DC)
        ng_ref[:, cols] = vy[k, :, :DC] / gain_s[:, cols]
    hg_ref[...] = (vy[0, :, DC:] + vy[1, :, DC:]) + (vy[2, :, DC:] + vy[3, :, DC:])
    for kv, ref in ((0, ks_ref), (1, vs_ref)):
        arrived(orecv.at[kv], s_out, (kv,))
        ref[:, xh] = oown[kv, xh]
        ref[:, 1 - xh] = orecv[kv]
    for kv, ref in ((0, dwk_ref), (1, dwv_ref)):

        @pl.when(moved)
        def _():
            arrived(finr.at[kv], s_dp, (kv,))

        ref[...] = finr[kv]

    @pl.when(moved)
    def _():
        for kv, ref in ((0, wk_ref), (1, wv_ref)):
            sent(ref, s_w0, (kv,))
            sent(fin.at[kv], s_dp, (kv,))

    for kv, ref in ((0, kcot_ref), (1, vcot_ref)):
        sent(ref.at[:, 1 - xh], s_cot, (kv,))
        sent(oown.at[kv, 1 - xh], s_out, (kv,))

    def sent_z(i):
        pz = ring_z(i + 1)
        for kv in range(2):
            sent(w.at[kv, zh, xh, ze, xl, c, 0:RA], s_wz, (kv, pz))
            sent(w.at[kv, zh, :, ze, :, c, RA:R], s_wr, (kv, pz))
            sent(zs.at[kv, lax.div(pz, 2), lax.rem(pz, 2)], s_dz, (kv, pz))
        sent(vz.at[z], s_vz, (pz,))

    loop(7, sent_z)

    def sent_x(i):
        px = ring_x(i + 1)
        sent(vx.at[x], s_vx, (px,))
        for kv in range(2):
            sent(w.at[kv, zh, xh, ze, xl, c, RA:R], s_wy, (kv, px))

    loop(3, sent_x)

    def sent_core(h):
        for kv in range(2):
            sent(w.at[kv, h, :, :, :, c], s_wc, (kv, h))
            sent(dw.at[kv, h, 1 - c], s_dc, (kv, h))
            for slot in range(2):
                sent(of_x(kv, h, x), s_wx, (kv, h, slot))
                sent(far_x(kv, h, x, slot), s_wx, (kv, h, 2 + slot))
                if kv == 1:
                    sent(dwf.at[kv, h, slot], s_df, (kv, h, slot))
                for e in range(2):
                    sent(dwx.at[kv, h, slot, e], s_dx, (kv, h, slot, e))

    loop(4, sent_core)
    sent(dwd, s_df, (0, ring_y(2), 0))
    for d in (0, 1, 3):
        for slot in range(2):
            sent(dwf.at[0, 0, slot], s_df, (0, ring_y(d), slot))
    sent(vc.at[c], s_vc, (0,))
    for slot in range(2):
        sent(pfar.at[slot], s_pf, (slot,))
        for half in range(2):
            sent(halves(precv.at[1, slot], half), s_pn, (slot, half))
    for kv in range(2):
        for slot in range(2):
            sent(cb.at[kv, y], s_ag, (kv, slot))
            sent(cb.at[kv, y, :, 0:2], s_ag, (kv, slot + 2))

    def sent_y(i):
        py = ring_y(i + 1)
        sent(hid.at[py], s_hid, (py,))
        sent(psend.at[0, py], s_p, (0, py))
        sent(dhs.at[py], s_dh, (py,))
        sent(vy.at[y], s_vy, (py,))

    loop(3, sent_y)


def hand_out(*refs):
    ins, outs, held, sems = refs[:7], refs[7:14], refs[14:21], refs[21]
    first = [pltpu.make_async_copy(ins[i], held[i], sems.at[0, i]) for i in range(7)]
    last = [pltpu.make_async_copy(held[i], outs[i], sems.at[1, i]) for i in range(7)]
    for copy in first:
        copy.start()
    for i in range(7):
        first[i].wait()
        last[i].start()
    for copy in last:
        copy.wait()


def on_device(
    inputs, norm_gain, key_weight, value_weight, head_gain, key_cotangent, value_cotangent
):
    def sems(*shape):
        return pltpu.SemaphoreType.DMA((2,) + shape)

    scratch = [
        pltpu.VMEM((4, T, DC), bf16),
        pltpu.VMEM((4, T, DC), bf16),
        pltpu.VMEM((DC, 4 * T), bf16),
        pltpu.VMEM((2, 4, 2, 2, 2, 2, R, H), bf16),
        pltpu.VMEM((2, 4, 4 * T, 2 * H), bf16),
        pltpu.VMEM((2, 4, 4 * T, 2 * H), bf16),
        pltpu.VMEM((2, 2 * T, 2 * H), bf16),
        pltpu.VMEM((2, 4 * T, 2 * H), f32),
        pltpu.VMEM((2, 4, T, H), bf16),
        pltpu.VMEM((2, 4, 2, 4, T, H), bf16),
        pltpu.VMEM((2, 2, 4, T, H), bf16),
        pltpu.VMEM((2, 4, T, H), bf16),
        pltpu.VMEM((4, T, DC), f32),
        pltpu.VMEM((4, T, DC), bf16),
        pltpu.VMEM((4, T, DC), bf16),
        pltpu.VMEM((2, 4, 2, 4, 2, R, H), bf16),
        pltpu.VMEM((2, 4, 4, 2, R, H), bf16),
        pltpu.VMEM((2, 4, 2, 2, R, H), bf16),
        pltpu.VMEM((2, 4, 2, R, H), bf16),
        pltpu.VMEM((2, R, H), bf16),
        pltpu.VMEM((2, 4, 2, R, H), bf16),
        pltpu.VMEM((2, 8, R, H), bf16),
        pltpu.VMEM((2, R, H), f32),
        pltpu.VMEM((2, R, H), f32),
        pltpu.VMEM((4, 1, DC + H), f32),
        pltpu.VMEM((8, 1, DC + H), f32),
        pltpu.VMEM((2, 1, DC + H), f32),
        pltpu.VMEM((4, 1, DC + H), f32),
        pltpu.VMEM((T, 128), f32),
        pltpu.VMEM((1, D), f32),
        pltpu.VMEM((T, D), bf16),
        sems(2),
        sems(2, 8),
        sems(2, 4, 4),
        sems(2, 4),
        sems(2, 8),
        sems(2, 4),
        sems(4),
        sems(2),
        sems(2, 4),
        sems(2, 4),
        sems(2),
        sems(2, 2),
        sems(2),
        sems(4),
        sems(2, 4),
        sems(2, 4, 2, 2),
        sems(2, 4, 2),
        sems(2, 8),
        sems(2),
        sems(4),
        sems(8),
        sems(1),
        sems(4),
        pltpu.SemaphoreType.DMA((3,)),
    ]
    outs = (
        jax.ShapeDtypeStruct((4, 2, T, H), bf16),
        jax.ShapeDtypeStruct((4, 2, T, H), bf16),
        jax.ShapeDtypeStruct((T, D), bf16),
        jax.ShapeDtypeStruct((R, H), f32),
        jax.ShapeDtypeStruct((R, H), f32),
        jax.ShapeDtypeStruct((1, D), f32),
        jax.ShapeDtypeStruct((1, H), f32),
    )
    vmem = pl.BlockSpec(memory_space=pltpu.VMEM)
    anywhere = pl.BlockSpec(memory_space=pl.ANY)
    results = pl.pallas_call(
        kernel,
        out_shape=outs,
        in_specs=[anywhere, vmem, vmem, vmem, vmem, anywhere, anywhere],
        out_specs=(vmem,) * 7,
        scratch_shapes=scratch,
        compiler_params=pltpu.CompilerParams(
            collective_id=0, has_side_effects=True, vmem_limit_bytes=60 * 1024 * 1024
        ),
        cost_estimate=pl.CostEstimate(
            flops=6 * 512 * DC * 2048, bytes_accessed=6 * 1024 * 1024, transcendentals=0
        ),
    )(
        inputs,
        norm_gain.reshape(D // 128, 128),
        key_weight,
        value_weight,
        head_gain.reshape(1, H),
        key_cotangent.reshape(4, 2, T, H),
        value_cotangent.reshape(4, 2, T, H),
    )
    ks, vs, ig, dwk, dwv, ng, hg = pl.pallas_call(
        hand_out,
        out_shape=outs,
        in_specs=[pl.BlockSpec(memory_space=pl.ANY)] * 7,
        out_specs=(pl.BlockSpec(memory_space=pl.ANY),) * 7,
        scratch_shapes=[pltpu.VMEM(o.shape, o.dtype) for o in outs]
        + [pltpu.SemaphoreType.DMA((2, 7))],
        compiler_params=pltpu.CompilerParams(vmem_limit_bytes=60 * 1024 * 1024),
    )(*results)
    return (
        ks.reshape(8 * T, H),
        vs.reshape(8 * T, H),
        ig,
        dwk,
        dwv,
        ng.reshape(D),
        hg.reshape(H),
    )


def solution(mesh):
    in_specs = (
        P(("dp", "tensor"), None),
        P(),
        P("dp", "tensor"),
        P("dp", "tensor"),
        P(),
        P("dp", "tensor"),
        P("dp", "tensor"),
    )
    out_specs = (
        P("dp", "tensor"),
        P("dp", "tensor"),
        P(("dp", "tensor"), None),
        P("dp", "tensor"),
        P("dp", "tensor"),
        P(),
        P(),
    )
    return jax.shard_map(
        on_device, mesh=mesh, in_specs=in_specs, out_specs=out_specs, check_vma=False
    )
```

```python
import jax
import jax.numpy as jnp
from jax import lax
from jax.experimental import pallas as pl
from jax.experimental.pallas import tpu as pltpu
from jax.sharding import PartitionSpec as P

eps = 1e-06
MESH = pl.DeviceIdType.MESH
T = 128
D = 5120
DC = 1280
R = 160
RA = 112
H = 128
bf16 = jnp.bfloat16
f32 = jnp.float32


def dot(a, b):
    return jnp.dot(a, b, preferred_element_type=f32)


def dot_nt(a, b):
    return lax.dot_general(a, b, (((1,), (1,)), ((), ())), preferred_element_type=f32)


def loop(n, body):
    def step(i, carry):
        body(i)
        return carry

    lax.fori_loop(0, n, step, 0)


def kernel(
    x_hbm,
    gain_ref,
    wk_ref,
    wv_ref,
    hgain_ref,
    kcot_ref,
    vcot_ref,
    ks_hbm,
    vs_hbm,
    ig_hbm,
    dwk_hbm,
    dwv_hbm,
    ng_hbm,
    hg_hbm,
    hid,
    hc,
    hct,
    w,
    psend,
    precv,
    pfar,
    own,
    cot,
    cb,
    oown,
    orecv,
    dhv,
    dhs,
    dhr,
    dw,
    dwc,
    dwx,
    dwf,
    dwd,
    zs,
    zr,
    fin,
    finr,
    vx,
    vz,
    vc,
    vy,
    rinv_s,
    gain_s,
    x_ref,
    ig_ref,
    ng_ref,
    hg_ref,
    s_w0,
    s_wz,
    s_wx,
    s_wy,
    s_wr,
    s_wc,
    s_hid,
    s_cot,
    s_ag,
    s_p,
    s_pf,
    s_pn,
    s_out,
    s_dh,
    s_dc,
    s_dx,
    s_df,
    s_dz,
    s_dp,
    s_vx,
    s_vz,
    s_vc,
    s_vy,
    s_in,
    s_send,
    s_res,
):
    dp, tn = lax.axis_index("dp"), lax.axis_index("tensor")
    z, xl, c = lax.div(dp, 4), lax.rem(lax.div(dp, 2), 2), lax.rem(dp, 2)
    y, xh = lax.div(tn, 2), lax.rem(tn, 2)
    x = 2 * xh + xl
    zh, ze = lax.div(z, 2), lax.rem(z, 2)

    def device(x, y, z, c):
        return (z * 4 + lax.rem(x, 2) * 2 + c, y * 2 + lax.div(x, 2))

    def ring_x(d):
        return lax.rem(x + d, 4)

    def ring_y(d):
        return lax.rem(y + d, 4)

    def ring_z(d):
        return lax.rem(z + d, 8)

    def at_x(px):
        return device(px, y, z, c)

    def at_y(py):
        return device(x, py, z, c)

    def at_z(pz):
        return device(x, y, pz, c)

    core = device(x, y, z, 1 - c)
    opposite = device(2 * (1 - xh) + xl, y, z, c)
    partner = device(x, zh, 2 * y + ze, c)
    moved = zh != y

    kinds = [
        s_w0,
        s_wz,
        s_wx,
        s_wy,
        s_wr,
        s_wc,
        s_hid,
        s_cot,
        s_ag,
        s_p,
        s_pf,
        s_pn,
        s_out,
        s_dh,
        s_dc,
        s_dx,
        s_df,
        s_dz,
        s_dp,
        s_vx,
        s_vz,
        s_vc,
        s_vy,
    ]

    def kind(sems):
        return next(i for i, known in enumerate(kinds) if known is sems)

    def send(src, dst, sems, at, to):
        pltpu.make_async_remote_copy(
            src_ref=src,
            dst_ref=dst,
            send_sem=s_send.at[kind(sems)],
            recv_sem=sems.at[at],
            device_id=to,
            device_id_type=MESH,
        ).start()

    def copy_of(ref, sems, at):
        return pltpu.make_async_remote_copy(
            src_ref=ref,
            dst_ref=ref,
            send_sem=s_send.at[kind(sems)],
            recv_sem=sems.at[at],
            device_id=core,
            device_id_type=MESH,
        )

    def arrived(ref, sems, at):
        copy_of(ref, sems, at).wait_recv()

    def sent(ref, sems, at):
        copy_of(ref, sems, at).wait_send()

    results = []

    def hand_on(src, dst):
        copy = pltpu.make_async_copy(src, dst, s_res.at[len(results)])
        copy.start()
        results.append(copy)

    barrier = pltpu.get_barrier_semaphore()

    def hello(to):
        pl.semaphore_signal(barrier, inc=1, device_id=to, device_id_type=MESH)

    for d in range(1, 4):
        hello(at_x(ring_x(d)))
        hello(at_y(ring_y(d)))
    for d in range(1, 8):
        hello(at_z(ring_z(d)))
    hello(core)

    @pl.when(moved)
    def _():
        hello(partner)

    local = [
        pltpu.make_async_copy(x_hbm, x_ref, s_in.at[0]),
        pltpu.make_async_copy(vcot_ref.at[:, xh], cb.at[1, y, xh], s_in.at[1]),
        pltpu.make_async_copy(kcot_ref.at[:, xh], cot.at[xh], s_in.at[2]),
    ]
    for copy in local:
        copy.start()
    for k in range(D // 128):
        gain_s[:, k * 128 : (k + 1) * 128] = gain_ref[k : k + 1, :].astype(f32)

    def w_own(kv):
        return w.at[kv, zh, xh, ze, xl, c]

    @pl.when(jnp.logical_not(moved))
    def _():
        for kv, ref in ((0, wk_ref), (1, wv_ref)):
            w[kv, zh, xh, ze, xl, c] = ref[...]

    pl.semaphore_wait(barrier, jnp.where(moved, 15, 14))

    def w_move(kv):
        @pl.when(moved)
        def _():
            ref = (wk_ref, wv_ref)[kv]
            send(ref, w.at[kv, y, xh, ze, xl, c], s_w0, (kv,), partner)

    w_move(0)
    send(vcot_ref.at[:, 1 - xh], cb.at[1, y, xh], s_cot, (1,), opposite)

    def norm_rows(i):
        rows = pl.ds(pl.multiple_of(i * 16, 16), 16)
        xf = x_ref[rows, :].astype(f32)
        rinv = lax.rsqrt(jnp.mean(xf * xf, axis=-1, keepdims=True) + eps)
        rinv_s[rows, :] = jnp.broadcast_to(rinv, (16, 128))
        hd = (xf * rinv * gain_s[...]).astype(bf16)
        for k in range(4):
            hid[k, rows, :] = hd[:, k * DC : (k + 1) * DC]

    local[0].wait()
    loop(8, norm_rows)
    for d in (1, 3, 2):
        py = ring_y(d)
        send(hid.at[py], hc.at[y], s_hid, (0,), at_y(py))
    hc[y] = hid[y]
    local[1].wait()
    local[2].wait()


    def moved_in(kv):
        @pl.when(moved)
        def _():
            arrived(w_own(kv), s_w0, (kv,))

    def w_first(kv):
        moved_in(kv)
        part = w.at[kv, zh, xh, ze, xl, c, 0:RA]

        def z_send(i):
            pz = ring_z(i + 1)
            send(part, part, s_wz, (kv, z), at_z(pz))

        loop(7, z_send)
        rest = w.at[kv, zh, xh, ze, xl, c, RA:R]
        for d in (1, 3, 2):
            px = ring_x(d)
            send(rest, rest, s_wy, (kv,), at_x(px))

    def w_second(kv):
        arrived(zr.at[kv, 0:3, 0 : R - RA], s_wy, (kv,))
        part = w.at[kv, zh, :, ze, :, c, RA:R]

        def z_send(i):
            pz = ring_z(i + 1)
            send(part, part, s_wr, (kv, z), at_z(pz))

        loop(7, z_send)

    def w_x(kv, i):
        h = ring_y(i + 1)

        def wait_z(e):
            pz = 2 * h + e

            @pl.when(pz != z)
            def _():
                arrived(w.at[kv, h, xh, e, xl, c, 0:RA], s_wz, (kv, pz))

        loop(2, wait_z)
        part = w.at[kv, h, xh, :, xl, c, 0:RA]
        for d in (1, 3):
            send(part, part, s_wx, (kv, h, 0), at_x(ring_x(d)))

    def far_x(kv, h, px, e):
        return w.at[kv, h, lax.div(px, 2), e, lax.rem(px, 2), c, 0:RA]

    def w_on(kv, i):
        h = ring_y(i + 1)
        arrived(w.at[kv, h, 0, :, :, c, 0:RA], s_wx, (kv, h, 0))
        for d, to, e in ((3, 1, 0), (1, 3, 1)):
            part = far_x(kv, h, ring_x(d), e)
            send(part, part, s_wx, (kv, h, 1), at_x(ring_x(to)))

    def w_core(kv, i):
        h = ring_y(i + 1)
        arrived(w.at[kv, h, 0, 0, :, c, 0:RA], s_wx, (kv, h, 1))

        def wait_z(e):
            pz = 2 * h + e

            @pl.when(pz != z)
            def _():
                arrived(w.at[kv, h, :, e, :, c, RA:R], s_wr, (kv, pz))

        loop(2, wait_z)
        part = w.at[kv, h, :, :, :, c]
        send(part, part, s_wc, (kv, h), core)

    w_first(0)
    w_move(1)
    loop(4, lambda i: w_x(0, i))
    w_second(0)
    w_first(1)
    loop(4, lambda i: w_on(0, i))
    send(kcot_ref.at[:, 1 - xh], cot.at[xh], s_cot, (0,), opposite)

    def panel(kv, h):
        return jnp.concatenate(
            [w[kv, h, 0].reshape(DC, H), w[kv, h, 1].reshape(DC, H)], axis=1
        )

    def forward(kv, i):
        h = ring_y(i + 1)
        part = dot(hc[...].reshape(4 * T, DC), panel(kv, h))

        @pl.when(h != y)
        def _():
            psend[kv, h] = part.astype(bf16)

        @pl.when(h == y)
        def _():
            own[kv] = part

    def partial_send(kv, d):
        py = ring_y(d)
        send(psend.at[kv, py], precv.at[kv, y], s_p, (0,), at_y(py))

    def halves(ref, half):
        return ref.at[half * 2 * T : (half + 1) * 2 * T]

    def far_send():
        for d, half in ((1, 0), (3, 1)):
            part = halves(psend.at[1, ring_y(2)], half)
            send(part, pfar.at[half], s_pf, (0,), at_y(ring_y(d)))

    def near_send(d, slot, half):
        src = halves(psend.at[1, ring_y(d)], half)
        dst = halves(precv.at[1, slot], half)
        send(src, dst, s_pn, (0,), at_y(ring_y(d)))

    def near_added():
        arrived(pfar, s_pf, (0,))
        for d, slot in ((1, 0), (3, 1)):
            rows = slice(slot * 2 * T, (slot + 1) * 2 * T)
            total = psend[1, ring_y(d), rows].astype(f32) + pfar[slot].astype(f32)
            psend[1, ring_y(d), rows] = total.astype(bf16)
            near_send(d, slot, slot)

    arrived(hc.at[0:3], s_hid, (0,))

    def gather(kv):
        for d in (1, 3):
            send(cb.at[kv, y], cb.at[kv, y], s_ag, (kv, 0), at_y(ring_y(d)))

    def gather_near(kv):
        arrived(cb.at[kv, 0:2], s_ag, (kv, 0))
        for d, to, half in ((3, 1, 0), (1, 3, 2)):
            part = cb.at[kv, ring_y(d), :, half : half + 2]
            send(part, part, s_ag, (kv, 1), at_y(ring_y(to)))

    def gather_far(kv):
        arrived(cb.at[kv, 0], s_ag, (kv, 1))

    arrived(cb.at[1, y, 1 - xh], s_cot, (1,))
    gather(1)
    for k in range(4):
        hct[:, k * T : (k + 1) * T] = hc[k].T

    def key_tile(i):
        h = ring_y(i + 1)
        arrived(w.at[0, h, :, :, :, 1 - c], s_wc, (0, h))
        forward(0, i)

        @pl.when(i < 3)
        def _():
            partial_send(0, i + 1)

    def key_step(i):
        w_core(0, i)

        @pl.when(i > 0)
        def _():
            key_tile(i - 1)

    loop(4, key_step)
    key_tile(3)
    gather_near(1)
    w_second(1)
    loop(4, lambda i: w_x(1, i))

    def cots(kv, h):
        return jnp.concatenate(
            [cb[kv, h, 0].reshape(4 * T, H), cb[kv, h, 1].reshape(4 * T, H)], axis=1
        )

    def grad_tile(kv, h):
        g = dot(hct[...], cots(kv, h)).astype(bf16).reshape(2, 2, 2, R, 2 * H)
        for pc in range(2):
            for ph in range(2):
                for pxl in range(2):
                    dw[kv, h, pc, 2 * ph + pxl] = g[:, pxl, pc, :, ph * H : (ph + 1) * H]
        send(dw.at[kv, h, 1 - c], dwc.at[kv, h], s_dc, (kv, h), core)

    def grad_near(kv, h, d, slot, e):
        src, dst = dw.at[kv, h, c, ring_x(d), e], dwx.at[kv, h, slot, e]
        send(src, dst, s_dx, (kv, h), at_x(ring_x(d)))

    def grad_core(kv, h):
        arrived(dwc.at[kv, h], s_dc, (kv, h))
        dw[kv, h, c] = (dw[kv, h, c].astype(f32) + dwc[kv, h].astype(f32)).astype(bf16)
        for d, e in ((1, 0), (3, 1)):
            part = dw.at[kv, h, c, ring_x(2), e]
            send(part, dwf.at[kv, h, e], s_df, (kv, h), at_x(ring_x(d)))
        grad_near(kv, h, 1, 0, 1)
        grad_near(kv, h, 3, 1, 0)

    def grad_last(h):
        arrived(dwc.at[0, h], s_dc, (0, h))
        dw[0, h, c] = (dw[0, h, c].astype(f32) + dwc[0, h].astype(f32)).astype(bf16)
        for d, slot in ((1, 0), (3, 1)):
            for e in range(2):
                grad_near(0, h, d, slot, e)
        send(dw.at[0, h, c, ring_x(2)], dwd, s_df, (0, h), at_x(ring_x(2)))

    def grad_added(kv, h):
        arrived(dwf.at[kv, h], s_df, (kv, h))
        for d, slot in ((1, 0), (3, 1)):
            mine = dw[kv, h, c, ring_x(d), slot].astype(f32)
            total = mine + dwf[kv, h, slot].astype(f32)
            dw[kv, h, c, ring_x(d), slot] = total.astype(bf16)
            grad_near(kv, h, d, slot, slot)

    def grad_x(kv, h, last=False):
        total = dw[kv, h, c, x].astype(f32)
        if last:
            arrived(dwd, s_df, (0, h))
            total = total + dwd[...].astype(f32)
        arrived(dwx.at[kv, h], s_dx, (kv, h))
        for slot in range(2):
            total = total + dwx[kv, h, slot].astype(f32)
        zs[kv, h] = total.astype(bf16)

        def body(e):
            pz = 2 * h + e

            @pl.when(pz != z)
            def _():
                send(zs.at[kv, h, e], zr.at[kv, z], s_dz, (kv,), at_z(pz))

        loop(2, body)

    def grad_z(kv):
        total = zs[kv, zh, ze].astype(f32)
        arrived(zr.at[kv, 0:7], s_dz, (kv,))
        for d in range(1, 8):
            pz = ring_z(d)
            total = total + zr[kv, pz].astype(f32)

        @pl.when(moved)
        def _():
            fin[kv] = total
            send(fin.at[kv], finr.at[kv], s_dp, (kv,), partner)

        @pl.when(jnp.logical_not(moved))
        def _():
            finr[kv] = total

    loop(3, lambda i: grad_tile(1, ring_y(i + lax.div(i, 2))))
    loop(3, lambda i: grad_core(1, ring_y(i + lax.div(i, 2))))

    arrived(cot.at[1 - xh], s_cot, (0,))

    def rows_cols(t, s):
        return pl.ds(pl.multiple_of(t * T, T), T), slice(s * H, (s + 1) * H)

    def key_sum(t, s):
        rows, cols = rows_cols(t, s)
        total = own[0, rows, cols]
        for d in range(1, 4):
            total = total + precv[0, ring_y(d), rows, cols].astype(f32)
        return total

    def value_sum(t, s):
        rows, cols = rows_cols(t, s)
        near = precv[1, 0, rows, cols].astype(f32) + precv[1, 1, rows, cols].astype(f32)
        return own[1, rows, cols] + near

    loop(4, lambda i: w_on(1, i))
    arrived(precv.at[0, 0:3], s_p, (0,))
    hgain = hgain_ref[...].astype(f32)
    vx[x] = jnp.zeros((1, DC + H), f32)

    def key_block(t):
        for s in range(2):
            key = key_sum(t, s)
            krinv = lax.rsqrt(jnp.mean(key * key, axis=-1, keepdims=True) + eps)
            kn = key * krinv
            oown[0, s, t] = (kn * hgain).astype(bf16)
            ct = cot[s, t].astype(f32)
            back = ct * hgain
            grad = krinv * (back - kn * jnp.mean(back * kn, axis=-1, keepdims=True))
            cb[0, y, s, t] = grad.astype(bf16)
            vx[x, :, DC:] += jnp.sum(ct * kn, axis=0, keepdims=True)

    loop(4, key_block)
    gather(0)
    send(oown.at[0, 1 - xh], orecv.at[0], s_out, (0,), opposite)
    hand_on(oown.at[0, xh], ks_hbm.at[:, xh])

    def back_panel(kv, h, first):
        part = dot_nt(cots(kv, h), panel(kv, h)).reshape(4, T, DC)
        if first:
            dhv[...] = part
        else:
            dhv[...] += part

    loop(3, lambda i: grad_added(1, ring_y(i + lax.div(i, 2))))
    gather_far(1)
    grad_tile(1, ring_y(2))
    grad_tile(0, y)
    loop(4, lambda i: w_core(1, i))
    back_panel(0, y, True)
    grad_core(1, ring_y(2))
    grad_core(0, y)

    def value_tile(i):
        k = jnp.where(i == 0, 1, jnp.where(i == 1, 0, i))
        h = ring_y(k + 1)
        arrived(w.at[1, h, :, :, :, 1 - c], s_wc, (1, h))
        forward(1, k)

        @pl.when(i == 0)
        def _():
            far_send()

        @pl.when(i == 1)
        def _():
            near_send(1, 0, 1)

        @pl.when(i == 2)
        def _():
            near_send(3, 1, 0)

    loop(3, value_tile)
    gather_near(0)
    value_tile(jnp.int32(3))
    loop(3, lambda i: grad_x(1, ring_y(i + lax.div(i, 2))))
    loop(2, lambda i: grad_tile(0, ring_y(2 * i + 1)))
    loop(2, lambda i: grad_core(0, ring_y(2 * i + 1)))
    grad_added(1, ring_y(2))
    grad_added(0, y)
    loop(4, lambda i: back_panel(1, i, False))
    loop(2, lambda i: back_panel(0, ring_y(2 * i + 1), False))
    near_added()
    loop(2, lambda i: grad_added(0, ring_y(2 * i + 1)))
    gather_far(0)

    def hidden_back(i):
        t = ring_y(i + 1)
        far = ring_y(2)
        ct = jnp.concatenate([cb[0, far, 0, t], cb[0, far, 1, t]], axis=1)
        total = dhv[t] + dot_nt(ct, panel(0, far))
        vx[x, :, :DC] += jnp.sum(total * hc[t].astype(f32), axis=0, keepdims=True)

        @pl.when(t != y)
        def _():
            dhs[t] = total.astype(bf16)
            send(dhs.at[t], dhr.at[y], s_dh, (0,), at_y(t))

        @pl.when(t == y)
        def _():
            dhr[y] = total.astype(bf16)

    loop(4, hidden_back)
    for d in range(1, 4):
        px = ring_x(d)
        send(vx.at[x], vx.at[x], s_vx, (0,), at_x(px))
    grad_tile(0, ring_y(2))
    grad_last(ring_y(2))
    grad_x(1, ring_y(2))
    grad_x(0, y)

    arrived(vx.at[0:3], s_vx, (0,))
    vz[z] = (vx[0] + vx[1]) + (vx[2] + vx[3])

    def vz_send(i):
        pz = ring_z(i + 1)
        send(vz.at[z], vz.at[z], s_vz, (0,), at_z(pz))

    loop(7, vz_send)
    loop(2, lambda i: grad_x(0, ring_y(2 * i + 1)))
    grad_z(1)
    grad_x(0, ring_y(2), True)
    arrived(vz.at[0:7], s_vz, (0,))
    vc[c] = ((vz[0] + vz[1]) + (vz[2] + vz[3])) + ((vz[4] + vz[5]) + (vz[6] + vz[7]))
    send(vc.at[c], vc.at[c], s_vc, (0,), core)
    grad_z(0)
    arrived(vc.at[1 - c], s_vc, (0,))
    vy[y] = vc[0] + vc[1]
    for d in range(1, 4):
        py = ring_y(d)
        send(vy.at[y], vy.at[y], s_vy, (0,), at_y(py))

    arrived(precv.at[1, 0:2], s_pn, (0,))

    def value_block(t):
        for s in range(2):
            oown[1, s, t] = value_sum(t, s).astype(bf16)

    loop(4, value_block)
    send(oown.at[1, 1 - xh], orecv.at[1], s_out, (1,), opposite)
    hand_on(oown.at[1, xh], vs_hbm.at[:, xh])

    arrived(dhr.at[0:3], s_dh, (0,))

    def input_rows(i):
        rows = pl.ds(pl.multiple_of(i * 16, 16), 16)
        rinv = rinv_s[rows, 0:1]
        mean = jnp.zeros((16, 1), f32)
        for k in range(4):
            cols = slice(k * DC, (k + 1) * DC)
            normed = x_ref[rows, cols].astype(f32) * rinv
            back = dhr[k, rows, :].astype(f32) * gain_s[:, cols]
            mean = mean + jnp.sum(back * normed, axis=-1, keepdims=True)
        mean = mean * (1.0 / D)
        for k in range(4):
            cols = slice(k * DC, (k + 1) * DC)
            normed = x_ref[rows, cols].astype(f32) * rinv
            back = dhr[k, rows, :].astype(f32) * gain_s[:, cols]
            ig_ref[rows, cols] = (rinv * (back - normed * mean)).astype(bf16)

    loop(8, input_rows)
    hand_on(ig_ref, ig_hbm)
    arrived(vy.at[0:3], s_vy, (0,))
    for k in range(4):
        cols = slice(k * DC, (k + 1) * DC)
        ng_ref[:, cols] = vy[k, :, :DC] / gain_s[:, cols]
    hg_ref[...] = (vy[0, :, DC:] + vy[1, :, DC:]) + (vy[2, :, DC:] + vy[3, :, DC:])
    hand_on(ng_ref, ng_hbm)
    hand_on(hg_ref, hg_hbm)
    for kv, ref in ((0, ks_hbm), (1, vs_hbm)):
        arrived(orecv.at[kv], s_out, (kv,))
        hand_on(orecv.at[kv], ref.at[:, 1 - xh])
    for kv, ref in ((1, dwv_hbm), (0, dwk_hbm)):

        @pl.when(moved)
        def _():
            arrived(finr.at[kv], s_dp, (kv,))

        hand_on(finr.at[kv], ref)

    @pl.when(moved)
    def _():
        sent(w.at[0, 0, 0, 0, 0], s_w0, (0,))
        sent(fin, s_dp, (0,))

    sent(zr.at[:, 0:7, 0:RA], s_wz, (0, 0))
    sent(psend.at[:, :, 0 : 3 * RA], s_wx, (0, 0, 0))
    sent(zr.at[:, 0:3, 0 : R - RA], s_wy, (0,))
    sent(psend.at[0, :, 0 : 7 * (R - RA)], s_wr, (0, 0))
    sent(w.at[:, :, :, :, :, 0], s_wc, (0, 0))
    sent(hid.at[0:3], s_hid, (0,))
    sent(cot, s_cot, (0,))
    sent(cb.at[:, 0:3], s_ag, (0, 0))
    sent(psend.at[0, 0:3], s_p, (0,))
    sent(pfar, s_pf, (0,))
    sent(precv.at[1, 0:2], s_pn, (0,))
    sent(orecv, s_out, (0,))
    sent(dhs.at[0:3], s_dh, (0,))
    sent(dwc, s_dc, (0, 0))
    sent(dwx, s_dx, (0, 0))
    sent(dwf, s_df, (0, 0))
    sent(zr.at[:, 0:7], s_dz, (0,))
    sent(vx.at[0:3], s_vx, (0,))
    sent(vz.at[0:7], s_vz, (0,))
    sent(vc.at[0], s_vc, (0,))
    sent(vy.at[0:3], s_vy, (0,))
    for copy in results:
        copy.wait()


def hand_out(*refs):
    ins, outs, held, sems = refs[:7], refs[7:14], refs[14:21], refs[21]
    first = [pltpu.make_async_copy(ins[i], held[i], sems.at[0, i]) for i in range(7)]
    last = [pltpu.make_async_copy(held[i], outs[i], sems.at[1, i]) for i in range(7)]
    for copy in first:
        copy.start()
    for i in range(7):
        first[i].wait()
        last[i].start()
    for copy in last:
        copy.wait()


def on_device(
    inputs, norm_gain, key_weight, value_weight, head_gain, key_cotangent, value_cotangent
):
    def sems(*shape):
        return pltpu.SemaphoreType.DMA(shape)

    scratch = [
        pltpu.VMEM((4, T, DC), bf16),
        pltpu.VMEM((4, T, DC), bf16),
        pltpu.VMEM((DC, 4 * T), bf16),
        pltpu.VMEM((2, 4, 2, 2, 2, 2, R, H), bf16),
        pltpu.VMEM((2, 4, 4 * T, 2 * H), bf16),
        pltpu.VMEM((2, 4, 4 * T, 2 * H), bf16),
        pltpu.VMEM((2, 2 * T, 2 * H), bf16),
        pltpu.VMEM((2, 4 * T, 2 * H), f32),
        pltpu.VMEM((2, 4, T, H), bf16),
        pltpu.VMEM((2, 4, 2, 4, T, H), bf16),
        pltpu.VMEM((2, 2, 4, T, H), bf16),
        pltpu.VMEM((2, 4, T, H), bf16),
        pltpu.VMEM((4, T, DC), f32),
        pltpu.VMEM((4, T, DC), bf16),
        pltpu.VMEM((4, T, DC), bf16),
        pltpu.VMEM((2, 4, 2, 4, 2, R, H), bf16),
        pltpu.VMEM((2, 4, 4, 2, R, H), bf16),
        pltpu.VMEM((2, 4, 2, 2, R, H), bf16),
        pltpu.VMEM((2, 4, 2, R, H), bf16),
        pltpu.VMEM((2, R, H), bf16),
        pltpu.VMEM((2, 4, 2, R, H), bf16),
        pltpu.VMEM((2, 8, R, H), bf16),
        pltpu.VMEM((2, R, H), f32),
        pltpu.VMEM((2, R, H), f32),
        pltpu.VMEM((4, 1, DC + H), f32),
        pltpu.VMEM((8, 1, DC + H), f32),
        pltpu.VMEM((2, 1, DC + H), f32),
        pltpu.VMEM((4, 1, DC + H), f32),
        pltpu.VMEM((T, 128), f32),
        pltpu.VMEM((1, D), f32),
        pltpu.VMEM((T, D), bf16),
        pltpu.VMEM((T, D), bf16),
        pltpu.VMEM((1, D), f32),
        pltpu.VMEM((1, H), f32),
        sems(2),
        sems(2, 8),
        sems(2, 4, 2),
        sems(2),
        sems(2, 8),
        sems(2, 4),
        sems(1),
        sems(2),
        sems(2, 2),
        sems(1),
        sems(1),
        sems(1),
        sems(2),
        sems(1),
        sems(2, 4),
        sems(2, 4),
        sems(2, 4),
        sems(2),
        sems(2),
        sems(1),
        sems(1),
        sems(1),
        sems(1),
        sems(3),
        sems(23),
        sems(9),
    ]
    outs = (
        jax.ShapeDtypeStruct((4, 2, T, H), bf16),
        jax.ShapeDtypeStruct((4, 2, T, H), bf16),
        jax.ShapeDtypeStruct((T, D), bf16),
        jax.ShapeDtypeStruct((R, H), f32),
        jax.ShapeDtypeStruct((R, H), f32),
        jax.ShapeDtypeStruct((1, D), f32),
        jax.ShapeDtypeStruct((1, H), f32),
    )
    vmem = pl.BlockSpec(memory_space=pltpu.VMEM)
    anywhere = pl.BlockSpec(memory_space=pl.ANY)
    results = pl.pallas_call(
        kernel,
        out_shape=outs,
        in_specs=[anywhere, vmem, vmem, vmem, vmem, anywhere, anywhere],
        out_specs=(anywhere,) * 7,
        scratch_shapes=scratch,
        compiler_params=pltpu.CompilerParams(
            collective_id=0, has_side_effects=True, vmem_limit_bytes=60 * 1024 * 1024
        ),
        cost_estimate=pl.CostEstimate(
            flops=6 * 512 * DC * 2048, bytes_accessed=6 * 1024 * 1024, transcendentals=0
        ),
    )(
        inputs,
        norm_gain.reshape(D // 128, 128),
        key_weight,
        value_weight,
        head_gain.reshape(1, H),
        key_cotangent.reshape(4, 2, T, H),
        value_cotangent.reshape(4, 2, T, H),
    )
    ks, vs, ig, dwk, dwv, ng, hg = pl.pallas_call(
        hand_out,
        out_shape=outs,
        in_specs=[pl.BlockSpec(memory_space=pl.ANY)] * 7,
        out_specs=(pl.BlockSpec(memory_space=pl.ANY),) * 7,
        scratch_shapes=[pltpu.VMEM(o.shape, o.dtype) for o in outs]
        + [pltpu.SemaphoreType.DMA((2, 7))],
        compiler_params=pltpu.CompilerParams(vmem_limit_bytes=60 * 1024 * 1024),
    )(*results)
    return (
        ks.reshape(8 * T, H),
        vs.reshape(8 * T, H),
        ig,
        dwk,
        dwv,
        ng.reshape(D),
        hg.reshape(H),
    )


def solution(mesh):
    in_specs = (
        P(("dp", "tensor"), None),
        P(),
        P("dp", "tensor"),
        P("dp", "tensor"),
        P(),
        P("dp", "tensor"),
        P("dp", "tensor"),
    )
    out_specs = (
        P("dp", "tensor"),
        P("dp", "tensor"),
        P(("dp", "tensor"), None),
        P("dp", "tensor"),
        P("dp", "tensor"),
        P(),
        P(),
    )
    return jax.shard_map(
        on_device, mesh=mesh, in_specs=in_specs, out_specs=out_specs, check_vma=False
    )
```

```python
import jax
import jax.numpy as jnp
from jax import lax
from jax.experimental import pallas as pl
from jax.experimental.pallas import tpu as pltpu
from jax.sharding import PartitionSpec as P

eps = 1e-06
MESH = pl.DeviceIdType.MESH
T = 128
D = 5120
DC = 1280
R = 160
RA = 112
H = 128
bf16 = jnp.bfloat16
f32 = jnp.float32


def dot(a, b):
    return jnp.dot(a, b, preferred_element_type=f32)


def dot_nt(a, b):
    return lax.dot_general(a, b, (((1,), (1,)), ((), ())), preferred_element_type=f32)


def loop(n, body):
    def step(i, carry):
        body(i)
        return carry

    lax.fori_loop(0, n, step, 0)


def kernel(
    x_hbm,
    gain_ref,
    wk_ref,
    wv_ref,
    hgain_ref,
    kcot_ref,
    vcot_ref,
    ks_hbm,
    vs_hbm,
    ig_hbm,
    dwk_hbm,
    dwv_hbm,
    ng_hbm,
    hg_hbm,
    hid,
    hc,
    hct,
    w,
    psend,
    precv,
    pfar,
    own,
    cot,
    cb,
    oown,
    orecv,
    dhv,
    dhs,
    dhr,
    dw,
    dwc,
    dwx,
    dwf,
    dwd,
    zs,
    zr,
    fin,
    finm,
    finr,
    vx,
    vz,
    vc,
    vy,
    rinv_s,
    gain_s,
    x_ref,
    ig_ref,
    ng_ref,
    hg_ref,
    s_w0,
    s_wz,
    s_wx,
    s_wy,
    s_wr,
    s_wc,
    s_hid,
    s_cot,
    s_ag,
    s_p,
    s_pf,
    s_pn,
    s_out,
    s_dh,
    s_dc,
    s_dx,
    s_df,
    s_dz,
    s_dp,
    s_vx,
    s_vz,
    s_vc,
    s_vy,
    s_in,
    s_send,
    s_res,
):
    dp, tn = lax.axis_index("dp"), lax.axis_index("tensor")
    z, xl, c = lax.div(dp, 4), lax.rem(lax.div(dp, 2), 2), lax.rem(dp, 2)
    y, xh = lax.div(tn, 2), lax.rem(tn, 2)
    x = 2 * xh + xl
    zh, ze = lax.div(z, 2), lax.rem(z, 2)

    def device(x, y, z, c):
        return (z * 4 + lax.rem(x, 2) * 2 + c, y * 2 + lax.div(x, 2))

    def ring_x(d):
        return lax.rem(x + d, 4)

    def ring_y(d):
        return lax.rem(y + d, 4)

    def ring_z(d):
        return lax.rem(z + d, 8)

    def at_x(px):
        return device(px, y, z, c)

    def at_y(py):
        return device(x, py, z, c)

    def at_z(pz):
        return device(x, y, pz, c)

    core = device(x, y, z, 1 - c)
    opposite = device(2 * (1 - xh) + xl, y, z, c)
    partner = device(x, zh, 2 * y + ze, c)
    moved = zh != y

    kinds = [
        s_w0,
        s_wz,
        s_wx,
        s_wy,
        s_wr,
        s_wc,
        s_hid,
        s_cot,
        s_ag,
        s_p,
        s_pf,
        s_pn,
        s_out,
        s_dh,
        s_dc,
        s_dx,
        s_df,
        s_dz,
        s_dp,
        s_vx,
        s_vz,
        s_vc,
        s_vy,
    ]

    def kind(sems):
        return next(i for i, known in enumerate(kinds) if known is sems)

    def send(src, dst, sems, at, to):
        pltpu.make_async_remote_copy(
            src_ref=src,
            dst_ref=dst,
            send_sem=s_send.at[kind(sems)],
            recv_sem=sems.at[at],
            device_id=to,
            device_id_type=MESH,
        ).start()

    def copy_of(ref, sems, at):
        return pltpu.make_async_remote_copy(
            src_ref=ref,
            dst_ref=ref,
            send_sem=s_send.at[kind(sems)],
            recv_sem=sems.at[at],
            device_id=core,
            device_id_type=MESH,
        )

    def arrived(ref, sems, at):
        copy_of(ref, sems, at).wait_recv()

    def sent(ref, sems, at):
        copy_of(ref, sems, at).wait_send()

    results = []

    def hand_on(src, dst):
        copy = pltpu.make_async_copy(src, dst, s_res.at[len(results)])
        copy.start()
        results.append(copy)

    barrier = pltpu.get_barrier_semaphore()

    def hello(to):
        pl.semaphore_signal(barrier, inc=1, device_id=to, device_id_type=MESH)

    for d in range(1, 4):
        hello(at_x(ring_x(d)))
        hello(at_y(ring_y(d)))
    for d in range(1, 8):
        hello(at_z(ring_z(d)))
    hello(core)

    @pl.when(moved)
    def _():
        hello(partner)

    local = [
        pltpu.make_async_copy(x_hbm, x_ref, s_in.at[0]),
        pltpu.make_async_copy(vcot_ref.at[:, xh], cb.at[1, y, xh], s_in.at[1]),
        pltpu.make_async_copy(kcot_ref.at[:, xh], cot.at[xh], s_in.at[2]),
    ]
    for copy in local:
        copy.start()
    for k in range(D // 128):
        gain_s[:, k * 128 : (k + 1) * 128] = gain_ref[k : k + 1, :].astype(f32)

    def w_own(kv):
        return w.at[kv, zh, xh, ze, xl, c]

    @pl.when(jnp.logical_not(moved))
    def _():
        for kv, ref in ((0, wk_ref), (1, wv_ref)):
            w[kv, zh, xh, ze, xl, c] = ref[...]

    pl.semaphore_wait(barrier, jnp.where(moved, 15, 14))

    def w_move(kv):
        @pl.when(moved)
        def _():
            ref = (wk_ref, wv_ref)[kv]
            send(ref, w.at[kv, y, xh, ze, xl, c], s_w0, (kv,), partner)

    w_move(0)
    send(vcot_ref.at[:, 1 - xh], cb.at[1, y, xh], s_cot, (1,), opposite)

    def norm_rows(i):
        rows = pl.ds(pl.multiple_of(i * 16, 16), 16)
        xf = x_ref[rows, :].astype(f32)
        rinv = lax.rsqrt(jnp.mean(xf * xf, axis=-1, keepdims=True) + eps)
        rinv_s[rows, :] = jnp.broadcast_to(rinv, (16, 128))
        hd = (xf * rinv * gain_s[...]).astype(bf16)
        for k in range(4):
            hid[k, rows, :] = hd[:, k * DC : (k + 1) * DC]

    local[0].wait()
    loop(8, norm_rows)
    for d in (1, 3, 2):
        py = ring_y(d)
        send(hid.at[py], hc.at[y], s_hid, (0,), at_y(py))
    hc[y] = hid[y]
    local[1].wait()
    local[2].wait()


    def moved_in(kv):
        @pl.when(moved)
        def _():
            arrived(w_own(kv), s_w0, (kv,))

    def w_first(kv):
        moved_in(kv)
        part = w.at[kv, zh, xh, ze, xl, c, 0:RA]

        def z_send(i):
            pz = ring_z(i + 1)
            send(part, part, s_wz, (kv, z), at_z(pz))

        loop(7, z_send)
        rest = w.at[kv, zh, xh, ze, xl, c, RA:R]
        for d in (1, 3, 2):
            px = ring_x(d)
            send(rest, rest, s_wy, (kv,), at_x(px))

    def w_second(kv):
        arrived(zr.at[kv, 0:3, 0 : R - RA], s_wy, (kv,))
        part = w.at[kv, zh, :, ze, :, c, RA:R]

        def z_send(i):
            pz = ring_z(i + 1)
            send(part, part, s_wr, (kv, z), at_z(pz))

        loop(7, z_send)

    def w_x(kv, i):
        h = ring_y(i + 1)

        def wait_z(e):
            pz = 2 * h + e

            @pl.when(pz != z)
            def _():
                arrived(w.at[kv, h, xh, e, xl, c, 0:RA], s_wz, (kv, pz))

        loop(2, wait_z)
        part = w.at[kv, h, xh, :, xl, c, 0:RA]
        for d in (1, 3):
            send(part, part, s_wx, (kv, h, 0), at_x(ring_x(d)))

    def far_x(kv, h, px, e):
        return w.at[kv, h, lax.div(px, 2), e, lax.rem(px, 2), c, 0:RA]

    def w_on(kv, i):
        h = ring_y(i + 1)
        arrived(w.at[kv, h, 0, :, :, c, 0:RA], s_wx, (kv, h, 0))
        for d, to, e in ((3, 1, 0), (1, 3, 1)):
            part = far_x(kv, h, ring_x(d), e)
            send(part, part, s_wx, (kv, h, 1), at_x(ring_x(to)))

    def w_core(kv, i):
        h = ring_y(i + 1)
        arrived(w.at[kv, h, 0, 0, :, c, 0:RA], s_wx, (kv, h, 1))

        def wait_z(e):
            pz = 2 * h + e

            @pl.when(pz != z)
            def _():
                arrived(w.at[kv, h, :, e, :, c, RA:R], s_wr, (kv, pz))

        loop(2, wait_z)
        part = w.at[kv, h, :, :, :, c]
        send(part, part, s_wc, (kv, h), core)

    w_first(0)
    w_move(1)
    loop(4, lambda i: w_x(0, i))
    w_second(0)
    w_first(1)
    loop(4, lambda i: w_on(0, i))
    send(kcot_ref.at[:, 1 - xh], cot.at[xh], s_cot, (0,), opposite)

    def panel(kv, h):
        return jnp.concatenate(
            [w[kv, h, 0].reshape(DC, H), w[kv, h, 1].reshape(DC, H)], axis=1
        )

    def forward(kv, i):
        h = ring_y(i + 1)
        part = dot(hc[...].reshape(4 * T, DC), panel(kv, h))

        @pl.when(h != y)
        def _():
            psend[kv, h] = part.astype(bf16)

        @pl.when(h == y)
        def _():
            own[kv] = part

    def partial_send(kv, d):
        py = ring_y(d)
        send(psend.at[kv, py], precv.at[kv, y], s_p, (0,), at_y(py))

    def halves(ref, half):
        return ref.at[half * 2 * T : (half + 1) * 2 * T]

    def far_send():
        for d, half in ((1, 0), (3, 1)):
            part = halves(psend.at[1, ring_y(2)], half)
            send(part, pfar.at[half], s_pf, (0,), at_y(ring_y(d)))

    def near_send(d, slot, half):
        src = halves(psend.at[1, ring_y(d)], half)
        dst = halves(precv.at[1, slot], half)
        send(src, dst, s_pn, (0,), at_y(ring_y(d)))

    def near_added():
        arrived(pfar, s_pf, (0,))
        for d, slot in ((1, 0), (3, 1)):
            rows = slice(slot * 2 * T, (slot + 1) * 2 * T)
            total = psend[1, ring_y(d), rows].astype(f32) + pfar[slot].astype(f32)
            psend[1, ring_y(d), rows] = total.astype(bf16)
            near_send(d, slot, slot)

    arrived(hc.at[0:3], s_hid, (0,))

    def gather(kv):
        for d in (1, 3):
            send(cb.at[kv, y], cb.at[kv, y], s_ag, (kv, 0), at_y(ring_y(d)))

    def gather_near(kv):
        arrived(cb.at[kv, 0:2], s_ag, (kv, 0))
        for d, to, half in ((3, 1, 0), (1, 3, 2)):
            part = cb.at[kv, ring_y(d), :, half : half + 2]
            send(part, part, s_ag, (kv, 1), at_y(ring_y(to)))

    def gather_far(kv):
        arrived(cb.at[kv, 0], s_ag, (kv, 1))

    arrived(cb.at[1, y, 1 - xh], s_cot, (1,))
    gather(1)
    for k in range(4):
        hct[:, k * T : (k + 1) * T] = hc[k].T

    def key_tile(i):
        h = ring_y(i + 1)
        arrived(w.at[0, h, :, :, :, 1 - c], s_wc, (0, h))
        forward(0, i)

        @pl.when(i < 3)
        def _():
            partial_send(0, i + 1)

    def key_step(i):
        w_core(0, i)

        @pl.when(i > 0)
        def _():
            key_tile(i - 1)

    loop(4, key_step)
    key_tile(3)
    gather_near(1)
    w_second(1)
    loop(4, lambda i: w_x(1, i))

    def cots(kv, h):
        return jnp.concatenate(
            [cb[kv, h, 0].reshape(4 * T, H), cb[kv, h, 1].reshape(4 * T, H)], axis=1
        )

    def grad_tile(kv, h):
        g = dot(hct[...], cots(kv, h)).astype(bf16).reshape(2, 2, 2, R, 2 * H)
        for pc in range(2):
            for ph in range(2):
                for pxl in range(2):
                    dw[kv, h, pc, 2 * ph + pxl] = g[:, pxl, pc, :, ph * H : (ph + 1) * H]
        send(dw.at[kv, h, 1 - c], dwc.at[kv, h], s_dc, (kv, h), core)

    def grad_near(kv, h, d, slot, e):
        src, dst = dw.at[kv, h, c, ring_x(d), e], dwx.at[kv, h, slot, e]
        send(src, dst, s_dx, (kv, h), at_x(ring_x(d)))

    def grad_core(kv, h):
        arrived(dwc.at[kv, h], s_dc, (kv, h))
        dw[kv, h, c] = (dw[kv, h, c].astype(f32) + dwc[kv, h].astype(f32)).astype(bf16)
        for d, e in ((1, 0), (3, 1)):
            part = dw.at[kv, h, c, ring_x(2), e]
            send(part, dwf.at[kv, h, e], s_df, (kv, h), at_x(ring_x(d)))
        grad_near(kv, h, 1, 0, 1)
        grad_near(kv, h, 3, 1, 0)

    def grad_last(h):
        arrived(dwc.at[0, h], s_dc, (0, h))
        dw[0, h, c] = (dw[0, h, c].astype(f32) + dwc[0, h].astype(f32)).astype(bf16)
        for d, slot in ((1, 0), (3, 1)):
            for e in range(2):
                grad_near(0, h, d, slot, e)
        send(dw.at[0, h, c, ring_x(2)], dwd, s_df, (0, h), at_x(ring_x(2)))

    def grad_added(kv, h):
        arrived(dwf.at[kv, h], s_df, (kv, h))
        for d, slot in ((1, 0), (3, 1)):
            mine = dw[kv, h, c, ring_x(d), slot].astype(f32)
            total = mine + dwf[kv, h, slot].astype(f32)
            dw[kv, h, c, ring_x(d), slot] = total.astype(bf16)
            grad_near(kv, h, d, slot, slot)

    def grad_x(kv, h, last=False):
        total = dw[kv, h, c, x].astype(f32)
        if last:
            arrived(dwd, s_df, (0, h))
            total = total + dwd[...].astype(f32)
        arrived(dwx.at[kv, h], s_dx, (kv, h))
        for slot in range(2):
            total = total + dwx[kv, h, slot].astype(f32)
        zs[kv, h] = total.astype(bf16)

        def body(e):
            pz = 2 * h + e

            @pl.when(pz != z)
            def _():
                send(zs.at[kv, h, e], zr.at[kv, z], s_dz, (kv,), at_z(pz))

        loop(2, body)

    def grad_z(kv):
        total = zs[kv, zh, ze].astype(f32)
        arrived(zr.at[kv, 0:7], s_dz, (kv,))
        for d in range(1, 8):
            pz = ring_z(d)
            total = total + zr[kv, pz].astype(f32)

        @pl.when(moved)
        def _():
            fin[kv] = total.astype(bf16)
            send(fin.at[kv], finm.at[kv], s_dp, (kv,), partner)

        @pl.when(jnp.logical_not(moved))
        def _():
            finr[kv] = total

    loop(3, lambda i: grad_tile(1, ring_y(i + lax.div(i, 2))))
    loop(3, lambda i: grad_core(1, ring_y(i + lax.div(i, 2))))

    arrived(cot.at[1 - xh], s_cot, (0,))

    def rows_cols(t, s):
        return pl.ds(pl.multiple_of(t * T, T), T), slice(s * H, (s + 1) * H)

    def key_sum(t, s):
        rows, cols = rows_cols(t, s)
        total = own[0, rows, cols]
        for d in range(1, 4):
            total = total + precv[0, ring_y(d), rows, cols].astype(f32)
        return total

    def value_sum(t, s):
        rows, cols = rows_cols(t, s)
        near = precv[1, 0, rows, cols].astype(f32) + precv[1, 1, rows, cols].astype(f32)
        return own[1, rows, cols] + near

    loop(4, lambda i: w_on(1, i))
    arrived(precv.at[0, 0:3], s_p, (0,))
    hgain = hgain_ref[...].astype(f32)
    vx[x] = jnp.zeros((1, DC + H), f32)

    def key_block(t):
        for s in range(2):
            key = key_sum(t, s)
            krinv = lax.rsqrt(jnp.mean(key * key, axis=-1, keepdims=True) + eps)
            kn = key * krinv
            oown[0, s, t] = (kn * hgain).astype(bf16)
            ct = cot[s, t].astype(f32)
            back = ct * hgain
            grad = krinv * (back - kn * jnp.mean(back * kn, axis=-1, keepdims=True))
            cb[0, y, s, t] = grad.astype(bf16)
            vx[x, :, DC:] += jnp.sum(ct * kn, axis=0, keepdims=True)

    loop(4, key_block)
    gather(0)
    send(oown.at[0, 1 - xh], orecv.at[0], s_out, (0,), opposite)
    hand_on(oown.at[0, xh], ks_hbm.at[:, xh])

    def back_panel(kv, h, first):
        part = dot_nt(cots(kv, h), panel(kv, h)).reshape(4, T, DC)
        if first:
            dhv[...] = part
        else:
            dhv[...] += part

    loop(3, lambda i: grad_added(1, ring_y(i + lax.div(i, 2))))
    gather_far(1)
    grad_tile(1, ring_y(2))
    grad_tile(0, y)
    loop(4, lambda i: w_core(1, i))
    back_panel(0, y, True)
    grad_core(1, ring_y(2))
    grad_core(0, y)

    def value_tile(i):
        k = jnp.where(i == 0, 1, jnp.where(i == 1, 0, i))
        h = ring_y(k + 1)
        arrived(w.at[1, h, :, :, :, 1 - c], s_wc, (1, h))
        forward(1, k)

        @pl.when(i == 0)
        def _():
            far_send()

        @pl.when(i == 1)
        def _():
            near_send(1, 0, 1)

        @pl.when(i == 2)
        def _():
            near_send(3, 1, 0)

    loop(3, value_tile)
    gather_near(0)
    value_tile(jnp.int32(3))
    loop(3, lambda i: grad_x(1, ring_y(i + lax.div(i, 2))))
    loop(2, lambda i: grad_tile(0, ring_y(2 * i + 1)))
    loop(2, lambda i: grad_core(0, ring_y(2 * i + 1)))
    grad_added(1, ring_y(2))
    grad_added(0, y)
    loop(4, lambda i: back_panel(1, i, False))
    loop(2, lambda i: back_panel(0, ring_y(2 * i + 1), False))
    near_added()
    loop(2, lambda i: grad_added(0, ring_y(2 * i + 1)))
    gather_far(0)

    def hidden_back(i):
        t = ring_y(i + 1)
        far = ring_y(2)
        ct = jnp.concatenate([cb[0, far, 0, t], cb[0, far, 1, t]], axis=1)
        total = dhv[t] + dot_nt(ct, panel(0, far))
        vx[x, :, :DC] += jnp.sum(total * hc[t].astype(f32), axis=0, keepdims=True)

        @pl.when(t != y)
        def _():
            dhs[t] = total.astype(bf16)
            send(dhs.at[t], dhr.at[y], s_dh, (0,), at_y(t))

        @pl.when(t == y)
        def _():
            dhr[y] = total.astype(bf16)

    grad_tile(0, ring_y(2))
    loop(4, hidden_back)
    for d in range(1, 4):
        px = ring_x(d)
        send(vx.at[x], vx.at[x], s_vx, (0,), at_x(px))
    grad_last(ring_y(2))
    grad_x(1, ring_y(2))
    grad_x(0, y)

    arrived(vx.at[0:3], s_vx, (0,))
    vz[z] = (vx[0] + vx[1]) + (vx[2] + vx[3])

    def vz_send(i):
        pz = ring_z(i + 1)
        send(vz.at[z], vz.at[z], s_vz, (0,), at_z(pz))

    loop(7, vz_send)
    loop(2, lambda i: grad_x(0, ring_y(2 * i + 1)))
    grad_z(1)
    grad_x(0, ring_y(2), True)
    arrived(vz.at[0:7], s_vz, (0,))
    vc[c] = ((vz[0] + vz[1]) + (vz[2] + vz[3])) + ((vz[4] + vz[5]) + (vz[6] + vz[7]))
    send(vc.at[c], vc.at[c], s_vc, (0,), core)
    grad_z(0)
    arrived(vc.at[1 - c], s_vc, (0,))
    vy[y] = vc[0] + vc[1]
    for d in range(1, 4):
        py = ring_y(d)
        send(vy.at[y], vy.at[y], s_vy, (0,), at_y(py))

    arrived(precv.at[1, 0:2], s_pn, (0,))

    def value_block(t):
        for s in range(2):
            oown[1, s, t] = value_sum(t, s).astype(bf16)

    loop(4, value_block)
    send(oown.at[1, 1 - xh], orecv.at[1], s_out, (1,), opposite)
    hand_on(oown.at[1, xh], vs_hbm.at[:, xh])

    arrived(dhr.at[0:3], s_dh, (0,))

    def input_rows(i):
        rows = pl.ds(pl.multiple_of(i * 16, 16), 16)
        rinv = rinv_s[rows, 0:1]
        mean = jnp.zeros((16, 1), f32)
        for k in range(4):
            cols = slice(k * DC, (k + 1) * DC)
            normed = x_ref[rows, cols].astype(f32) * rinv
            back = dhr[k, rows, :].astype(f32) * gain_s[:, cols]
            mean = mean + jnp.sum(back * normed, axis=-1, keepdims=True)
        mean = mean * (1.0 / D)
        for k in range(4):
            cols = slice(k * DC, (k + 1) * DC)
            normed = x_ref[rows, cols].astype(f32) * rinv
            back = dhr[k, rows, :].astype(f32) * gain_s[:, cols]
            ig_ref[rows, cols] = (rinv * (back - normed * mean)).astype(bf16)

    loop(8, input_rows)
    hand_on(ig_ref, ig_hbm)
    arrived(vy.at[0:3], s_vy, (0,))
    for k in range(4):
        cols = slice(k * DC, (k + 1) * DC)
        ng_ref[:, cols] = vy[k, :, :DC] / gain_s[:, cols]
    hg_ref[...] = (vy[0, :, DC:] + vy[1, :, DC:]) + (vy[2, :, DC:] + vy[3, :, DC:])
    hand_on(ng_ref, ng_hbm)
    hand_on(hg_ref, hg_hbm)
    for kv, ref in ((0, ks_hbm), (1, vs_hbm)):
        arrived(orecv.at[kv], s_out, (kv,))
        hand_on(orecv.at[kv], ref.at[:, 1 - xh])
    for kv, ref in ((1, dwv_hbm), (0, dwk_hbm)):

        @pl.when(moved)
        def _():
            arrived(finm.at[kv], s_dp, (kv,))
            finr[kv] = finm[kv].astype(f32)

        hand_on(finr.at[kv], ref)

    @pl.when(moved)
    def _():
        sent(w.at[0, 0, 0, 0, 0], s_w0, (0,))
        sent(fin, s_dp, (0,))

    sent(zr.at[:, 0:7, 0:RA], s_wz, (0, 0))
    sent(psend.at[:, :, 0 : 3 * RA], s_wx, (0, 0, 0))
    sent(zr.at[:, 0:3, 0 : R - RA], s_wy, (0,))
    sent(psend.at[0, :, 0 : 7 * (R - RA)], s_wr, (0, 0))
    sent(w.at[:, :, :, :, :, 0], s_wc, (0, 0))
    sent(hid.at[0:3], s_hid, (0,))
    sent(cot, s_cot, (0,))
    sent(cb.at[:, 0:3], s_ag, (0, 0))
    sent(psend.at[0, 0:3], s_p, (0,))
    sent(pfar, s_pf, (0,))
    sent(precv.at[1, 0:2], s_pn, (0,))
    sent(orecv, s_out, (0,))
    sent(dhs.at[0:3], s_dh, (0,))
    sent(dwc, s_dc, (0, 0))
    sent(dwx, s_dx, (0, 0))
    sent(dwf, s_df, (0, 0))
    sent(zr.at[:, 0:7], s_dz, (0,))
    sent(vx.at[0:3], s_vx, (0,))
    sent(vz.at[0:7], s_vz, (0,))
    sent(vc.at[0], s_vc, (0,))
    sent(vy.at[0:3], s_vy, (0,))
    for copy in results:
        copy.wait()


def hand_out(*refs):
    ins, outs, held, sems = refs[:7], refs[7:14], refs[14:21], refs[21]
    parts = [(2, k) for k in range(4)] + [(0, None), (1, None)]
    parts += [(i, None) for i in range(3, 7)]

    def view(ref, k):
        return ref if k is None else ref.at[32 * k : 32 * k + 32]

    first, last = [], []
    for n, (i, k) in enumerate(parts):
        src, mid, dst = view(ins[i], k), view(held[i], k), view(outs[i], k)
        first.append(pltpu.make_async_copy(src, mid, sems.at[0, n]))
        last.append(pltpu.make_async_copy(mid, dst, sems.at[1, n]))
    for copy in first:
        copy.start()
    for n in range(len(parts)):
        first[n].wait()
        last[n].start()
    for copy in last:
        copy.wait()


def on_device(
    inputs, norm_gain, key_weight, value_weight, head_gain, key_cotangent, value_cotangent
):
    def sems(*shape):
        return pltpu.SemaphoreType.DMA(shape)

    scratch = [
        pltpu.VMEM((4, T, DC), bf16),
        pltpu.VMEM((4, T, DC), bf16),
        pltpu.VMEM((DC, 4 * T), bf16),
        pltpu.VMEM((2, 4, 2, 2, 2, 2, R, H), bf16),
        pltpu.VMEM((2, 4, 4 * T, 2 * H), bf16),
        pltpu.VMEM((2, 4, 4 * T, 2 * H), bf16),
        pltpu.VMEM((2, 2 * T, 2 * H), bf16),
        pltpu.VMEM((2, 4 * T, 2 * H), f32),
        pltpu.VMEM((2, 4, T, H), bf16),
        pltpu.VMEM((2, 4, 2, 4, T, H), bf16),
        pltpu.VMEM((2, 2, 4, T, H), bf16),
        pltpu.VMEM((2, 4, T, H), bf16),
        pltpu.VMEM((4, T, DC), f32),
        pltpu.VMEM((4, T, DC), bf16),
        pltpu.VMEM((4, T, DC), bf16),
        pltpu.VMEM((2, 4, 2, 4, 2, R, H), bf16),
        pltpu.VMEM((2, 4, 4, 2, R, H), bf16),
        pltpu.VMEM((2, 4, 2, 2, R, H), bf16),
        pltpu.VMEM((2, 4, 2, R, H), bf16),
        pltpu.VMEM((2, R, H), bf16),
        pltpu.VMEM((2, 4, 2, R, H), bf16),
        pltpu.VMEM((2, 8, R, H), bf16),
        pltpu.VMEM((2, R, H), bf16),
        pltpu.VMEM((2, R, H), bf16),
        pltpu.VMEM((2, R, H), f32),
        pltpu.VMEM((4, 1, DC + H), f32),
        pltpu.VMEM((8, 1, DC + H), f32),
        pltpu.VMEM((2, 1, DC + H), f32),
        pltpu.VMEM((4, 1, DC + H), f32),
        pltpu.VMEM((T, 128), f32),
        pltpu.VMEM((1, D), f32),
        pltpu.VMEM((T, D), bf16),
        pltpu.VMEM((T, D), bf16),
        pltpu.VMEM((1, D), f32),
        pltpu.VMEM((1, H), f32),
        sems(2),
        sems(2, 8),
        sems(2, 4, 2),
        sems(2),
        sems(2, 8),
        sems(2, 4),
        sems(1),
        sems(2),
        sems(2, 2),
        sems(1),
        sems(1),
        sems(1),
        sems(2),
        sems(1),
        sems(2, 4),
        sems(2, 4),
        sems(2, 4),
        sems(2),
        sems(2),
        sems(1),
        sems(1),
        sems(1),
        sems(1),
        sems(3),
        sems(23),
        sems(9),
    ]
    outs = (
        jax.ShapeDtypeStruct((4, 2, T, H), bf16),
        jax.ShapeDtypeStruct((4, 2, T, H), bf16),
        jax.ShapeDtypeStruct((T, D), bf16),
        jax.ShapeDtypeStruct((R, H), f32),
        jax.ShapeDtypeStruct((R, H), f32),
        jax.ShapeDtypeStruct((1, D), f32),
        jax.ShapeDtypeStruct((1, H), f32),
    )
    vmem = pl.BlockSpec(memory_space=pltpu.VMEM)
    anywhere = pl.BlockSpec(memory_space=pl.ANY)
    results = pl.pallas_call(
        kernel,
        out_shape=outs,
        in_specs=[anywhere, vmem, vmem, vmem, vmem, anywhere, anywhere],
        out_specs=(anywhere,) * 7,
        scratch_shapes=scratch,
        compiler_params=pltpu.CompilerParams(
            collective_id=0, has_side_effects=True, vmem_limit_bytes=60 * 1024 * 1024
        ),
        cost_estimate=pl.CostEstimate(
            flops=6 * 512 * DC * 2048, bytes_accessed=6 * 1024 * 1024, transcendentals=0
        ),
    )(
        inputs,
        norm_gain.reshape(D // 128, 128),
        key_weight,
        value_weight,
        head_gain.reshape(1, H),
        key_cotangent.reshape(4, 2, T, H),
        value_cotangent.reshape(4, 2, T, H),
    )
    ks, vs, ig, dwk, dwv, ng, hg = pl.pallas_call(
        hand_out,
        out_shape=outs,
        in_specs=[pl.BlockSpec(memory_space=pl.ANY)] * 7,
        out_specs=(pl.BlockSpec(memory_space=pl.ANY),) * 7,
        scratch_shapes=[pltpu.VMEM(o.shape, o.dtype) for o in outs]
        + [pltpu.SemaphoreType.DMA((2, 10))],
        compiler_params=pltpu.CompilerParams(vmem_limit_bytes=60 * 1024 * 1024),
    )(*results)
    return (
        ks.reshape(8 * T, H),
        vs.reshape(8 * T, H),
        ig,
        dwk,
        dwv,
        ng.reshape(D),
        hg.reshape(H),
    )


def solution(mesh):
    in_specs = (
        P(("dp", "tensor"), None),
        P(),
        P("dp", "tensor"),
        P("dp", "tensor"),
        P(),
        P("dp", "tensor"),
        P("dp", "tensor"),
    )
    out_specs = (
        P("dp", "tensor"),
        P("dp", "tensor"),
        P(("dp", "tensor"), None),
        P("dp", "tensor"),
        P("dp", "tensor"),
        P(),
        P(),
    )
    return jax.shard_map(
        on_device, mesh=mesh, in_specs=in_specs, out_specs=out_specs, check_vma=False
    )
```

```python
import jax
import jax.numpy as jnp
from jax import lax
from jax.experimental import pallas as pl
from jax.experimental.pallas import tpu as pltpu
from jax.sharding import PartitionSpec as P

eps = 1e-06
MESH = pl.DeviceIdType.MESH
T = 128
D = 5120
DC = 1280
R = 160
RA = 112
H = 128
bf16 = jnp.bfloat16
f32 = jnp.float32


def dot(a, b):
    return jnp.dot(a, b, preferred_element_type=f32)


def dot_nt(a, b):
    return lax.dot_general(a, b, (((1,), (1,)), ((), ())), preferred_element_type=f32)


def loop(n, body):
    def step(i, carry):
        body(i)
        return carry

    lax.fori_loop(0, n, step, 0)


def kernel(
    x_hbm,
    gain_ref,
    wk_ref,
    wv_ref,
    hgain_ref,
    kcot_ref,
    vcot_ref,
    ks_hbm,
    vs_hbm,
    ig_hbm,
    dwk_hbm,
    dwv_hbm,
    ng_hbm,
    hg_hbm,
    hid,
    hc,
    hct,
    w,
    psend,
    precv,
    pfar,
    own,
    cot,
    cb,
    oown,
    orecv,
    dhv,
    dhs,
    dhr,
    dw,
    dwc,
    dwx,
    dwf,
    dwd,
    zs,
    zr,
    fin,
    finm,
    finr,
    vx,
    vz,
    vc,
    vy,
    rinv_s,
    gain_s,
    x_ref,
    ig_ref,
    ng_ref,
    hg_ref,
    s_w0,
    s_wz,
    s_wx,
    s_wy,
    s_wr,
    s_wc,
    s_hid,
    s_cot,
    s_ag,
    s_p,
    s_pf,
    s_pn,
    s_out,
    s_dh,
    s_dc,
    s_dx,
    s_df,
    s_dz,
    s_dp,
    s_vx,
    s_vz,
    s_vc,
    s_vy,
    s_in,
    s_send,
    s_res,
):
    dp, tn = lax.axis_index("dp"), lax.axis_index("tensor")
    z, xl, c = lax.div(dp, 4), lax.rem(lax.div(dp, 2), 2), lax.rem(dp, 2)
    y, xh = lax.div(tn, 2), lax.rem(tn, 2)
    x = 2 * xh + xl
    zh, ze = lax.div(z, 2), lax.rem(z, 2)

    def device(x, y, z, c):
        return (z * 4 + lax.rem(x, 2) * 2 + c, y * 2 + lax.div(x, 2))

    def ring_x(d):
        return lax.rem(x + d, 4)

    def ring_y(d):
        return lax.rem(y + d, 4)

    def ring_z(d):
        return lax.rem(z + d, 8)

    def at_x(px):
        return device(px, y, z, c)

    def at_y(py):
        return device(x, py, z, c)

    def at_z(pz):
        return device(x, y, pz, c)

    core = device(x, y, z, 1 - c)
    opposite = device(2 * (1 - xh) + xl, y, z, c)
    partner = device(x, zh, 2 * y + ze, c)
    moved = zh != y

    kinds = [
        s_w0,
        s_wz,
        s_wx,
        s_wy,
        s_wr,
        s_wc,
        s_hid,
        s_cot,
        s_ag,
        s_p,
        s_pf,
        s_pn,
        s_out,
        s_dh,
        s_dc,
        s_dx,
        s_df,
        s_dz,
        s_dp,
        s_vx,
        s_vz,
        s_vc,
        s_vy,
    ]

    def kind(sems):
        return next(i for i, known in enumerate(kinds) if known is sems)

    def send(src, dst, sems, at, to):
        pltpu.make_async_remote_copy(
            src_ref=src,
            dst_ref=dst,
            send_sem=s_send.at[kind(sems)],
            recv_sem=sems.at[at],
            device_id=to,
            device_id_type=MESH,
        ).start()

    def copy_of(ref, sems, at):
        return pltpu.make_async_remote_copy(
            src_ref=ref,
            dst_ref=ref,
            send_sem=s_send.at[kind(sems)],
            recv_sem=sems.at[at],
            device_id=core,
            device_id_type=MESH,
        )

    def arrived(ref, sems, at):
        copy_of(ref, sems, at).wait_recv()

    def sent(ref, sems, at):
        copy_of(ref, sems, at).wait_send()

    results = []

    def hand_on(src, dst):
        copy = pltpu.make_async_copy(src, dst, s_res.at[len(results)])
        copy.start()
        results.append(copy)

    barrier = pltpu.get_barrier_semaphore()

    def hello(to):
        pl.semaphore_signal(barrier, inc=1, device_id=to, device_id_type=MESH)

    for d in range(1, 4):
        hello(at_x(ring_x(d)))
        hello(at_y(ring_y(d)))
    for d in range(1, 8):
        hello(at_z(ring_z(d)))
    hello(core)

    @pl.when(moved)
    def _():
        hello(partner)

    local = [
        pltpu.make_async_copy(x_hbm, x_ref, s_in.at[0]),
        pltpu.make_async_copy(vcot_ref.at[:, xh], cb.at[1, y, xh], s_in.at[1]),
        pltpu.make_async_copy(kcot_ref.at[:, xh], cot.at[xh], s_in.at[2]),
    ]
    for copy in local:
        copy.start()
    for k in range(D // 128):
        gain_s[:, k * 128 : (k + 1) * 128] = gain_ref[k : k + 1, :].astype(f32)

    def w_own(kv):
        return w.at[kv, zh, xh, ze, xl, c]

    @pl.when(jnp.logical_not(moved))
    def _():
        for kv, ref in ((0, wk_ref), (1, wv_ref)):
            w[kv, zh, xh, ze, xl, c] = ref[...]

    pl.semaphore_wait(barrier, jnp.where(moved, 15, 14))

    def w_move(kv):
        @pl.when(moved)
        def _():
            ref = (wk_ref, wv_ref)[kv]
            send(ref, w.at[kv, y, xh, ze, xl, c], s_w0, (kv,), partner)

    w_move(0)
    send(vcot_ref.at[:, 1 - xh], cb.at[1, y, xh], s_cot, (1,), opposite)

    def norm_rows(i):
        rows = pl.ds(pl.multiple_of(i * 16, 16), 16)
        xf = x_ref[rows, :].astype(f32)
        rinv = lax.rsqrt(jnp.mean(xf * xf, axis=-1, keepdims=True) + eps)
        rinv_s[rows, :] = jnp.broadcast_to(rinv, (16, 128))
        hd = (xf * rinv * gain_s[...]).astype(bf16)
        for k in range(4):
            hid[k, rows, :] = hd[:, k * DC : (k + 1) * DC]

    local[0].wait()
    loop(8, norm_rows)
    for d in (1, 3, 2):
        py = ring_y(d)
        send(hid.at[py], hc.at[y], s_hid, (0,), at_y(py))
    hc[y] = hid[y]
    local[1].wait()
    local[2].wait()


    def moved_in(kv):
        @pl.when(moved)
        def _():
            arrived(w_own(kv), s_w0, (kv,))

    def w_first(kv):
        moved_in(kv)
        part = w.at[kv, zh, xh, ze, xl, c, 0:RA]

        def z_send(i):
            pz = ring_z(i + 1)
            send(part, part, s_wz, (kv, z), at_z(pz))

        loop(7, z_send)
        rest = w.at[kv, zh, xh, ze, xl, c, RA:R]
        for d in (1, 3, 2):
            px = ring_x(d)
            send(rest, rest, s_wy, (kv,), at_x(px))

    def w_second(kv):
        arrived(zr.at[kv, 0:3, 0 : R - RA], s_wy, (kv,))
        part = w.at[kv, zh, :, ze, :, c, RA:R]

        def z_send(i):
            pz = ring_z(i + 1)
            send(part, part, s_wr, (kv, z), at_z(pz))

        loop(7, z_send)

    def w_x(kv, i):
        h = ring_y(i + 1)

        def wait_z(e):
            pz = 2 * h + e

            @pl.when(pz != z)
            def _():
                arrived(w.at[kv, h, xh, e, xl, c, 0:RA], s_wz, (kv, pz))

        loop(2, wait_z)
        part = w.at[kv, h, xh, :, xl, c, 0:RA]
        for d in (1, 3):
            send(part, part, s_wx, (kv, h, 0), at_x(ring_x(d)))

    def far_x(kv, h, px, e):
        return w.at[kv, h, lax.div(px, 2), e, lax.rem(px, 2), c, 0:RA]

    def w_on(kv, i):
        h = ring_y(i + 1)
        arrived(w.at[kv, h, 0, :, :, c, 0:RA], s_wx, (kv, h, 0))
        for d, to, e in ((3, 1, 0), (1, 3, 1)):
            part = far_x(kv, h, ring_x(d), e)
            send(part, part, s_wx, (kv, h, 1), at_x(ring_x(to)))

    def w_core(kv, i):
        h = ring_y(i + 1)
        arrived(w.at[kv, h, 0, 0, :, c, 0:RA], s_wx, (kv, h, 1))

        def wait_z(e):
            pz = 2 * h + e

            @pl.when(pz != z)
            def _():
                arrived(w.at[kv, h, :, e, :, c, RA:R], s_wr, (kv, pz))

        loop(2, wait_z)
        part = w.at[kv, h, :, :, :, c]
        send(part, part, s_wc, (kv, h), core)

    w_first(0)
    w_move(1)
    loop(4, lambda i: w_x(0, i))
    w_second(0)
    w_first(1)
    loop(4, lambda i: w_on(0, i))
    send(kcot_ref.at[:, 1 - xh], cot.at[xh], s_cot, (0,), opposite)

    def panel(kv, h):
        return jnp.concatenate(
            [w[kv, h, 0].reshape(DC, H), w[kv, h, 1].reshape(DC, H)], axis=1
        )

    def forward(kv, i):
        h = ring_y(i + 1)
        part = dot(hc[...].reshape(4 * T, DC), panel(kv, h))

        @pl.when(h != y)
        def _():
            psend[kv, h] = part.astype(bf16)

        @pl.when(h == y)
        def _():
            own[kv] = part

    def partial_send(kv, d):
        py = ring_y(d)
        send(psend.at[kv, py], precv.at[kv, y], s_p, (0,), at_y(py))

    def halves(ref, half):
        return ref.at[half * 2 * T : (half + 1) * 2 * T]

    def far_send():
        for d, half in ((1, 0), (3, 1)):
            part = halves(psend.at[1, ring_y(2)], half)
            send(part, pfar.at[half], s_pf, (0,), at_y(ring_y(d)))

    def near_send(d, slot, half):
        src = halves(psend.at[1, ring_y(d)], half)
        dst = halves(precv.at[1, slot], half)
        send(src, dst, s_pn, (0,), at_y(ring_y(d)))

    def near_added():
        arrived(pfar, s_pf, (0,))
        for d, slot in ((1, 0), (3, 1)):
            rows = slice(slot * 2 * T, (slot + 1) * 2 * T)
            total = psend[1, ring_y(d), rows].astype(f32) + pfar[slot].astype(f32)
            psend[1, ring_y(d), rows] = total.astype(bf16)
            near_send(d, slot, slot)

    arrived(hc.at[0:3], s_hid, (0,))

    def gather(kv):
        for d in (1, 3):
            send(cb.at[kv, y], cb.at[kv, y], s_ag, (kv, 0), at_y(ring_y(d)))

    def gather_near(kv):
        arrived(cb.at[kv, 0:2], s_ag, (kv, 0))
        for d, to, half in ((3, 1, 0), (1, 3, 2)):
            part = cb.at[kv, ring_y(d), :, half : half + 2]
            send(part, part, s_ag, (kv, 1), at_y(ring_y(to)))

    def gather_far(kv):
        arrived(cb.at[kv, 0], s_ag, (kv, 1))

    arrived(cb.at[1, y, 1 - xh], s_cot, (1,))
    gather(1)
    for k in range(4):
        hct[:, k * T : (k + 1) * T] = hc[k].T

    def key_tile(i):
        h = ring_y(i + 1)
        arrived(w.at[0, h, :, :, :, 1 - c], s_wc, (0, h))
        forward(0, i)

        @pl.when(i < 3)
        def _():
            partial_send(0, i + 1)

    def key_step(i):
        w_core(0, i)

        @pl.when(i > 0)
        def _():
            key_tile(i - 1)

    loop(4, key_step)
    key_tile(3)
    gather_near(1)
    w_second(1)
    loop(4, lambda i: w_x(1, i))

    def cots(kv, h):
        return jnp.concatenate(
            [cb[kv, h, 0].reshape(4 * T, H), cb[kv, h, 1].reshape(4 * T, H)], axis=1
        )

    def grad_tile(kv, h):
        g = dot(hct[...], cots(kv, h)).astype(bf16).reshape(2, 2, 2, R, 2 * H)
        for pc in range(2):
            for ph in range(2):
                for pxl in range(2):
                    dw[kv, h, pc, 2 * ph + pxl] = g[:, pxl, pc, :, ph * H : (ph + 1) * H]
        send(dw.at[kv, h, 1 - c], dwc.at[kv, h], s_dc, (kv, h), core)

    def grad_near(kv, h, d, slot, e):
        src, dst = dw.at[kv, h, c, ring_x(d), e], dwx.at[kv, h, slot, e]
        send(src, dst, s_dx, (kv, h), at_x(ring_x(d)))

    def grad_core(kv, h):
        arrived(dwc.at[kv, h], s_dc, (kv, h))
        dw[kv, h, c] = (dw[kv, h, c].astype(f32) + dwc[kv, h].astype(f32)).astype(bf16)
        for d, e in ((1, 0), (3, 1)):
            part = dw.at[kv, h, c, ring_x(2), e]
            send(part, dwf.at[kv, h, e], s_df, (kv, h), at_x(ring_x(d)))
        grad_near(kv, h, 1, 0, 1)
        grad_near(kv, h, 3, 1, 0)

    def grad_last(h):
        arrived(dwc.at[0, h], s_dc, (0, h))
        dw[0, h, c] = (dw[0, h, c].astype(f32) + dwc[0, h].astype(f32)).astype(bf16)
        for d, slot in ((1, 0), (3, 1)):
            for e in range(2):
                grad_near(0, h, d, slot, e)
        send(dw.at[0, h, c, ring_x(2)], dwd, s_df, (0, h), at_x(ring_x(2)))

    def grad_added(kv, h):
        arrived(dwf.at[kv, h], s_df, (kv, h))
        for d, slot in ((1, 0), (3, 1)):
            mine = dw[kv, h, c, ring_x(d), slot].astype(f32)
            total = mine + dwf[kv, h, slot].astype(f32)
            dw[kv, h, c, ring_x(d), slot] = total.astype(bf16)
            grad_near(kv, h, d, slot, slot)

    def grad_x(kv, h, last=False):
        total = dw[kv, h, c, x].astype(f32)
        if last:
            arrived(dwd, s_df, (0, h))
            total = total + dwd[...].astype(f32)
        arrived(dwx.at[kv, h], s_dx, (kv, h))
        for slot in range(2):
            total = total + dwx[kv, h, slot].astype(f32)
        zs[kv, h] = total.astype(bf16)

        def body(e):
            pz = 2 * h + e

            @pl.when(pz != z)
            def _():
                send(zs.at[kv, h, e], zr.at[kv, z], s_dz, (kv,), at_z(pz))

        loop(2, body)

    def grad_z(kv):
        total = zs[kv, zh, ze].astype(f32)
        arrived(zr.at[kv, 0:7], s_dz, (kv,))
        for d in range(1, 8):
            pz = ring_z(d)
            total = total + zr[kv, pz].astype(f32)

        @pl.when(moved)
        def _():
            fin[kv] = total.astype(bf16)
            send(fin.at[kv], finm.at[kv], s_dp, (kv,), partner)

        @pl.when(jnp.logical_not(moved))
        def _():
            finr[kv] = total

    loop(3, lambda i: grad_tile(1, ring_y(i + lax.div(i, 2))))
    loop(3, lambda i: grad_core(1, ring_y(i + lax.div(i, 2))))

    arrived(cot.at[1 - xh], s_cot, (0,))

    def rows_cols(t, s):
        return pl.ds(pl.multiple_of(t * T, T), T), slice(s * H, (s + 1) * H)

    def key_sum(t, s):
        rows, cols = rows_cols(t, s)
        total = own[0, rows, cols]
        for d in range(1, 4):
            total = total + precv[0, ring_y(d), rows, cols].astype(f32)
        return total

    def value_sum(t, s):
        rows, cols = rows_cols(t, s)
        near = precv[1, 0, rows, cols].astype(f32) + precv[1, 1, rows, cols].astype(f32)
        return own[1, rows, cols] + near

    loop(4, lambda i: w_on(1, i))
    arrived(precv.at[0, 0:3], s_p, (0,))
    hgain = hgain_ref[...].astype(f32)
    vx[x] = jnp.zeros((1, DC + H), f32)

    def key_block(t):
        for s in range(2):
            key = key_sum(t, s)
            krinv = lax.rsqrt(jnp.mean(key * key, axis=-1, keepdims=True) + eps)
            kn = key * krinv
            oown[0, s, t] = (kn * hgain).astype(bf16)
            ct = cot[s, t].astype(f32)
            back = ct * hgain
            grad = krinv * (back - kn * jnp.mean(back * kn, axis=-1, keepdims=True))
            cb[0, y, s, t] = grad.astype(bf16)
            vx[x, :, DC:] += jnp.sum(ct * kn, axis=0, keepdims=True)

    loop(4, key_block)
    gather(0)
    send(oown.at[0, 1 - xh], orecv.at[0], s_out, (0,), opposite)
    hand_on(oown.at[0, xh], ks_hbm.at[:, xh])

    def back_panel(kv, h, first):
        part = dot_nt(cots(kv, h), panel(kv, h)).reshape(4, T, DC)
        if first:
            dhv[...] = part
        else:
            dhv[...] += part

    loop(3, lambda i: grad_added(1, ring_y(i + lax.div(i, 2))))
    grad_tile(0, y)
    back_panel(0, y, True)
    gather_far(1)
    grad_tile(1, ring_y(2))
    loop(4, lambda i: w_core(1, i))
    grad_core(1, ring_y(2))
    grad_core(0, y)

    def value_tile(i):
        k = jnp.where(i == 0, 1, jnp.where(i == 1, 0, i))
        h = ring_y(k + 1)
        arrived(w.at[1, h, :, :, :, 1 - c], s_wc, (1, h))
        forward(1, k)

        @pl.when(i == 0)
        def _():
            far_send()

        @pl.when(i == 1)
        def _():
            near_send(1, 0, 1)

        @pl.when(i == 2)
        def _():
            near_send(3, 1, 0)

    loop(3, value_tile)
    gather_near(0)
    value_tile(jnp.int32(3))
    loop(3, lambda i: grad_x(1, ring_y(i + lax.div(i, 2))))
    loop(2, lambda i: grad_tile(0, ring_y(2 * i + 1)))
    loop(2, lambda i: grad_core(0, ring_y(2 * i + 1)))
    grad_added(1, ring_y(2))
    grad_added(0, y)
    loop(4, lambda i: back_panel(1, i, False))
    loop(2, lambda i: back_panel(0, ring_y(2 * i + 1), False))
    near_added()
    gather_far(0)

    def hidden_back(i):
        t = ring_y(i + 1)
        far = ring_y(2)
        ct = jnp.concatenate([cb[0, far, 0, t], cb[0, far, 1, t]], axis=1)
        total = dhv[t] + dot_nt(ct, panel(0, far))
        vx[x, :, :DC] += jnp.sum(total * hc[t].astype(f32), axis=0, keepdims=True)

        @pl.when(t != y)
        def _():
            dhs[t] = total.astype(bf16)
            send(dhs.at[t], dhr.at[y], s_dh, (0,), at_y(t))

        @pl.when(t == y)
        def _():
            dhr[y] = total.astype(bf16)

    grad_tile(0, ring_y(2))
    loop(2, lambda i: grad_added(0, ring_y(2 * i + 1)))
    loop(4, hidden_back)
    for d in range(1, 4):
        px = ring_x(d)
        send(vx.at[x], vx.at[x], s_vx, (0,), at_x(px))
    grad_last(ring_y(2))
    grad_x(1, ring_y(2))
    grad_x(0, y)

    arrived(vx.at[0:3], s_vx, (0,))
    vz[z] = (vx[0] + vx[1]) + (vx[2] + vx[3])

    def vz_send(i):
        pz = ring_z(i + 1)
        send(vz.at[z], vz.at[z], s_vz, (0,), at_z(pz))

    loop(7, vz_send)
    loop(2, lambda i: grad_x(0, ring_y(2 * i + 1)))
    grad_z(1)
    grad_x(0, ring_y(2), True)
    arrived(vz.at[0:7], s_vz, (0,))
    vc[c] = ((vz[0] + vz[1]) + (vz[2] + vz[3])) + ((vz[4] + vz[5]) + (vz[6] + vz[7]))
    send(vc.at[c], vc.at[c], s_vc, (0,), core)
    grad_z(0)
    arrived(vc.at[1 - c], s_vc, (0,))
    vy[y] = vc[0] + vc[1]
    for d in range(1, 4):
        py = ring_y(d)
        send(vy.at[y], vy.at[y], s_vy, (0,), at_y(py))

    arrived(precv.at[1, 0:2], s_pn, (0,))

    def value_block(t):
        for s in range(2):
            oown[1, s, t] = value_sum(t, s).astype(bf16)

    loop(4, value_block)
    send(oown.at[1, 1 - xh], orecv.at[1], s_out, (1,), opposite)
    hand_on(oown.at[1, xh], vs_hbm.at[:, xh])

    arrived(dhr.at[0:3], s_dh, (0,))

    def input_rows(i):
        rows = pl.ds(pl.multiple_of(i * 16, 16), 16)
        rinv = rinv_s[rows, 0:1]
        mean = jnp.zeros((16, 1), f32)
        for k in range(4):
            cols = slice(k * DC, (k + 1) * DC)
            normed = x_ref[rows, cols].astype(f32) * rinv
            back = dhr[k, rows, :].astype(f32) * gain_s[:, cols]
            mean = mean + jnp.sum(back * normed, axis=-1, keepdims=True)
        mean = mean * (1.0 / D)
        for k in range(4):
            cols = slice(k * DC, (k + 1) * DC)
            normed = x_ref[rows, cols].astype(f32) * rinv
            back = dhr[k, rows, :].astype(f32) * gain_s[:, cols]
            ig_ref[rows, cols] = (rinv * (back - normed * mean)).astype(bf16)

    loop(8, input_rows)
    hand_on(ig_ref, ig_hbm)
    arrived(vy.at[0:3], s_vy, (0,))
    for k in range(4):
        cols = slice(k * DC, (k + 1) * DC)
        ng_ref[:, cols] = vy[k, :, :DC] / gain_s[:, cols]
    hg_ref[...] = (vy[0, :, DC:] + vy[1, :, DC:]) + (vy[2, :, DC:] + vy[3, :, DC:])
    hand_on(ng_ref, ng_hbm)
    hand_on(hg_ref, hg_hbm)
    for kv, ref in ((0, ks_hbm), (1, vs_hbm)):
        arrived(orecv.at[kv], s_out, (kv,))
        hand_on(orecv.at[kv], ref.at[:, 1 - xh])
    for kv, ref in ((1, dwv_hbm), (0, dwk_hbm)):

        @pl.when(moved)
        def _():
            arrived(finm.at[kv], s_dp, (kv,))
            finr[kv] = finm[kv].astype(f32)

        hand_on(finr.at[kv], ref)

    @pl.when(moved)
    def _():
        sent(w.at[0, 0, 0, 0, 0], s_w0, (0,))
        sent(fin, s_dp, (0,))

    sent(zr.at[:, 0:7, 0:RA], s_wz, (0, 0))
    sent(psend.at[:, :, 0 : 3 * RA], s_wx, (0, 0, 0))
    sent(zr.at[:, 0:3, 0 : R - RA], s_wy, (0,))
    sent(psend.at[0, :, 0 : 7 * (R - RA)], s_wr, (0, 0))
    sent(w.at[:, :, :, :, :, 0], s_wc, (0, 0))
    sent(hid.at[0:3], s_hid, (0,))
    sent(cot, s_cot, (0,))
    sent(cb.at[:, 0:3], s_ag, (0, 0))
    sent(psend.at[0, 0:3], s_p, (0,))
    sent(pfar, s_pf, (0,))
    sent(precv.at[1, 0:2], s_pn, (0,))
    sent(orecv, s_out, (0,))
    sent(dhs.at[0:3], s_dh, (0,))
    sent(dwc, s_dc, (0, 0))
    sent(dwx, s_dx, (0, 0))
    sent(dwf, s_df, (0, 0))
    sent(zr.at[:, 0:7], s_dz, (0,))
    sent(vx.at[0:3], s_vx, (0,))
    sent(vz.at[0:7], s_vz, (0,))
    sent(vc.at[0], s_vc, (0,))
    sent(vy.at[0:3], s_vy, (0,))
    for copy in results:
        copy.wait()


def hand_out(*refs):
    ins, outs, held, sems = refs[:7], refs[7:14], refs[14:21], refs[21]
    parts = [(2, k) for k in range(4)] + [(0, None), (1, None)]
    parts += [(i, None) for i in range(3, 7)]

    def view(ref, k):
        return ref if k is None else ref.at[32 * k : 32 * k + 32]

    first, last = [], []
    for n, (i, k) in enumerate(parts):
        src, mid, dst = view(ins[i], k), view(held[i], k), view(outs[i], k)
        first.append(pltpu.make_async_copy(src, mid, sems.at[0, n]))
        last.append(pltpu.make_async_copy(mid, dst, sems.at[1, n]))
    for copy in first:
        copy.start()
    for n in range(len(parts)):
        first[n].wait()
        last[n].start()
    for copy in last:
        copy.wait()


def on_device(
    inputs, norm_gain, key_weight, value_weight, head_gain, key_cotangent, value_cotangent
):
    def sems(*shape):
        return pltpu.SemaphoreType.DMA(shape)

    scratch = [
        pltpu.VMEM((4, T, DC), bf16),
        pltpu.VMEM((4, T, DC), bf16),
        pltpu.VMEM((DC, 4 * T), bf16),
        pltpu.VMEM((2, 4, 2, 2, 2, 2, R, H), bf16),
        pltpu.VMEM((2, 4, 4 * T, 2 * H), bf16),
        pltpu.VMEM((2, 4, 4 * T, 2 * H), bf16),
        pltpu.VMEM((2, 2 * T, 2 * H), bf16),
        pltpu.VMEM((2, 4 * T, 2 * H), f32),
        pltpu.VMEM((2, 4, T, H), bf16),
        pltpu.VMEM((2, 4, 2, 4, T, H), bf16),
        pltpu.VMEM((2, 2, 4, T, H), bf16),
        pltpu.VMEM((2, 4, T, H), bf16),
        pltpu.VMEM((4, T, DC), f32),
        pltpu.VMEM((4, T, DC), bf16),
        pltpu.VMEM((4, T, DC), bf16),
        pltpu.VMEM((2, 4, 2, 4, 2, R, H), bf16),
        pltpu.VMEM((2, 4, 4, 2, R, H), bf16),
        pltpu.VMEM((2, 4, 2, 2, R, H), bf16),
        pltpu.VMEM((2, 4, 2, R, H), bf16),
        pltpu.VMEM((2, R, H), bf16),
        pltpu.VMEM((2, 4, 2, R, H), bf16),
        pltpu.VMEM((2, 8, R, H), bf16),
        pltpu.VMEM((2, R, H), bf16),
        pltpu.VMEM((2, R, H), bf16),
        pltpu.VMEM((2, R, H), f32),
        pltpu.VMEM((4, 1, DC + H), f32),
        pltpu.VMEM((8, 1, DC + H), f32),
        pltpu.VMEM((2, 1, DC + H), f32),
        pltpu.VMEM((4, 1, DC + H), f32),
        pltpu.VMEM((T, 128), f32),
        pltpu.VMEM((1, D), f32),
        pltpu.VMEM((T, D), bf16),
        pltpu.VMEM((T, D), bf16),
        pltpu.VMEM((1, D), f32),
        pltpu.VMEM((1, H), f32),
        sems(2),
        sems(2, 8),
        sems(2, 4, 2),
        sems(2),
        sems(2, 8),
        sems(2, 4),
        sems(1),
        sems(2),
        sems(2, 2),
        sems(1),
        sems(1),
        sems(1),
        sems(2),
        sems(1),
        sems(2, 4),
        sems(2, 4),
        sems(2, 4),
        sems(2),
        sems(2),
        sems(1),
        sems(1),
        sems(1),
        sems(1),
        sems(3),
        sems(23),
        sems(9),
    ]
    outs = (
        jax.ShapeDtypeStruct((4, 2, T, H), bf16),
        jax.ShapeDtypeStruct((4, 2, T, H), bf16),
        jax.ShapeDtypeStruct((T, D), bf16),
        jax.ShapeDtypeStruct((R, H), f32),
        jax.ShapeDtypeStruct((R, H), f32),
        jax.ShapeDtypeStruct((1, D), f32),
        jax.ShapeDtypeStruct((1, H), f32),
    )
    vmem = pl.BlockSpec(memory_space=pltpu.VMEM)
    anywhere = pl.BlockSpec(memory_space=pl.ANY)
    results = pl.pallas_call(
        kernel,
        out_shape=outs,
        in_specs=[anywhere, vmem, vmem, vmem, vmem, anywhere, anywhere],
        out_specs=(anywhere,) * 7,
        scratch_shapes=scratch,
        compiler_params=pltpu.CompilerParams(
            collective_id=0, has_side_effects=True, vmem_limit_bytes=60 * 1024 * 1024
        ),
        cost_estimate=pl.CostEstimate(
            flops=6 * 512 * DC * 2048, bytes_accessed=6 * 1024 * 1024, transcendentals=0
        ),
    )(
        inputs,
        norm_gain.reshape(D // 128, 128),
        key_weight,
        value_weight,
        head_gain.reshape(1, H),
        key_cotangent.reshape(4, 2, T, H),
        value_cotangent.reshape(4, 2, T, H),
    )
    ks, vs, ig, dwk, dwv, ng, hg = pl.pallas_call(
        hand_out,
        out_shape=outs,
        in_specs=[pl.BlockSpec(memory_space=pl.ANY)] * 7,
        out_specs=(pl.BlockSpec(memory_space=pl.ANY),) * 7,
        scratch_shapes=[pltpu.VMEM(o.shape, o.dtype) for o in outs]
        + [pltpu.SemaphoreType.DMA((2, 10))],
        compiler_params=pltpu.CompilerParams(vmem_limit_bytes=60 * 1024 * 1024),
    )(*results)
    return (
        ks.reshape(8 * T, H),
        vs.reshape(8 * T, H),
        ig,
        dwk,
        dwv,
        ng.reshape(D),
        hg.reshape(H),
    )


def solution(mesh):
    in_specs = (
        P(("dp", "tensor"), None),
        P(),
        P("dp", "tensor"),
        P("dp", "tensor"),
        P(),
        P("dp", "tensor"),
        P("dp", "tensor"),
    )
    out_specs = (
        P("dp", "tensor"),
        P("dp", "tensor"),
        P(("dp", "tensor"), None),
        P("dp", "tensor"),
        P("dp", "tensor"),
        P(),
        P(),
    )
    return jax.shard_map(
        on_device, mesh=mesh, in_specs=in_specs, out_specs=out_specs, check_vma=False
    )
```

```python
import jax
import jax.numpy as jnp
from jax import lax
from jax.experimental import pallas as pl
from jax.experimental.pallas import tpu as pltpu
from jax.sharding import PartitionSpec as P

eps = 1e-06
MESH = pl.DeviceIdType.MESH
T = 128
D = 5120
DC = 1280
R = 160
RA = 112
H = 128
bf16 = jnp.bfloat16
f32 = jnp.float32


def dot(a, b):
    return jnp.dot(a, b, preferred_element_type=f32)


def dot_nt(a, b):
    return lax.dot_general(a, b, (((1,), (1,)), ((), ())), preferred_element_type=f32)


def loop(n, body):
    def step(i, carry):
        body(i)
        return carry

    lax.fori_loop(0, n, step, 0)


def kernel(
    x_hbm,
    gain_ref,
    wk_ref,
    wv_ref,
    hgain_ref,
    kcot_ref,
    vcot_ref,
    ks_hbm,
    vs_hbm,
    ig_hbm,
    dwk_hbm,
    dwv_hbm,
    ng_hbm,
    hg_hbm,
    hid,
    hc,
    hct,
    w,
    psend,
    precv,
    pfar,
    own,
    cot,
    cb,
    oown,
    orecv,
    dhv,
    dhs,
    dhr,
    dw,
    dwc,
    dwx,
    dwf,
    dwd,
    zs,
    zr,
    fin,
    finm,
    finr,
    vx,
    vz,
    vc,
    vy,
    rinv_s,
    gain_s,
    x_ref,
    ig_ref,
    ng_ref,
    hg_ref,
    s_w0,
    s_wz,
    s_wx,
    s_wy,
    s_wr,
    s_wc,
    s_hid,
    s_cot,
    s_ag,
    s_p,
    s_pf,
    s_pn,
    s_out,
    s_dh,
    s_dc,
    s_dx,
    s_df,
    s_dz,
    s_dp,
    s_vx,
    s_vz,
    s_vc,
    s_vy,
    s_in,
    s_send,
    s_res,
):
    dp, tn = lax.axis_index("dp"), lax.axis_index("tensor")
    z, xl, c = lax.div(dp, 4), lax.rem(lax.div(dp, 2), 2), lax.rem(dp, 2)
    y, xh = lax.div(tn, 2), lax.rem(tn, 2)
    x = 2 * xh + xl
    zh, ze = lax.div(z, 2), lax.rem(z, 2)

    def device(x, y, z, c):
        return (z * 4 + lax.rem(x, 2) * 2 + c, y * 2 + lax.div(x, 2))

    def ring_x(d):
        return lax.rem(x + d, 4)

    def ring_y(d):
        return lax.rem(y + d, 4)

    def ring_z(d):
        return lax.rem(z + d, 8)

    def at_x(px):
        return device(px, y, z, c)

    def at_y(py):
        return device(x, py, z, c)

    def at_z(pz):
        return device(x, y, pz, c)

    core = device(x, y, z, 1 - c)
    opposite = device(2 * (1 - xh) + xl, y, z, c)
    partner = device(x, zh, 2 * y + ze, c)
    moved = zh != y

    kinds = [
        s_w0,
        s_wz,
        s_wx,
        s_wy,
        s_wr,
        s_wc,
        s_hid,
        s_cot,
        s_ag,
        s_p,
        s_pf,
        s_pn,
        s_out,
        s_dh,
        s_dc,
        s_dx,
        s_df,
        s_dz,
        s_dp,
        s_vx,
        s_vz,
        s_vc,
        s_vy,
    ]

    def kind(sems):
        return next(i for i, known in enumerate(kinds) if known is sems)

    def send(src, dst, sems, at, to):
        pltpu.make_async_remote_copy(
            src_ref=src,
            dst_ref=dst,
            send_sem=s_send.at[kind(sems)],
            recv_sem=sems.at[at],
            device_id=to,
            device_id_type=MESH,
        ).start()

    def copy_of(ref, sems, at):
        return pltpu.make_async_remote_copy(
            src_ref=ref,
            dst_ref=ref,
            send_sem=s_send.at[kind(sems)],
            recv_sem=sems.at[at],
            device_id=core,
            device_id_type=MESH,
        )

    def arrived(ref, sems, at):
        copy_of(ref, sems, at).wait_recv()

    def sent(ref, sems, at):
        copy_of(ref, sems, at).wait_send()

    results = []

    def hand_on(src, dst):
        copy = pltpu.make_async_copy(src, dst, s_res.at[len(results)])
        copy.start()
        results.append(copy)

    barrier = pltpu.get_barrier_semaphore()

    def hello(to):
        pl.semaphore_signal(barrier, inc=1, device_id=to, device_id_type=MESH)

    for d in range(1, 4):
        hello(at_x(ring_x(d)))
        hello(at_y(ring_y(d)))
    for d in range(1, 8):
        hello(at_z(ring_z(d)))
    hello(core)

    @pl.when(moved)
    def _():
        hello(partner)

    local = [
        pltpu.make_async_copy(x_hbm, x_ref, s_in.at[0]),
        pltpu.make_async_copy(vcot_ref.at[:, xh], cb.at[1, y, xh], s_in.at[1]),
        pltpu.make_async_copy(kcot_ref.at[:, xh], cot.at[xh], s_in.at[2]),
    ]
    for copy in local:
        copy.start()
    gains = gain_ref[...].astype(f32)
    for k in range(D // 128):
        gain_s[:, k * 128 : (k + 1) * 128] = gains[k : k + 1, :]

    def w_own(kv):
        return w.at[kv, zh, xh, ze, xl, c]

    @pl.when(jnp.logical_not(moved))
    def _():
        for kv, ref in ((0, wk_ref), (1, wv_ref)):
            w[kv, zh, xh, ze, xl, c] = ref[...]

    pl.semaphore_wait(barrier, jnp.where(moved, 15, 14))

    def w_move(kv):
        @pl.when(moved)
        def _():
            ref = (wk_ref, wv_ref)[kv]
            send(ref, w.at[kv, y, xh, ze, xl, c], s_w0, (kv,), partner)

    w_move(0)
    send(vcot_ref.at[:, 1 - xh], cb.at[1, y, xh], s_cot, (1,), opposite)

    def norm_rows(i):
        rows = pl.ds(pl.multiple_of(i * 16, 16), 16)
        xf = x_ref[rows, :].astype(f32)
        rinv = lax.rsqrt(jnp.mean(xf * xf, axis=-1, keepdims=True) + eps)
        rinv_s[rows, :] = jnp.broadcast_to(rinv, (16, 128))
        hd = (xf * rinv * gain_s[...]).astype(bf16)
        for k in range(4):
            hid[k, rows, :] = hd[:, k * DC : (k + 1) * DC]

    local[0].wait()
    loop(8, norm_rows)
    for d in (1, 3, 2):
        py = ring_y(d)
        send(hid.at[py], hc.at[y], s_hid, (0,), at_y(py))
    hc[y] = hid[y]
    local[1].wait()
    local[2].wait()


    def moved_in(kv):
        @pl.when(moved)
        def _():
            arrived(w_own(kv), s_w0, (kv,))

    def w_first(kv):
        moved_in(kv)
        part = w.at[kv, zh, xh, ze, xl, c, 0:RA]

        def z_send(i):
            pz = ring_z(i + 1)
            send(part, part, s_wz, (kv, z), at_z(pz))

        loop(7, z_send)
        rest = w.at[kv, zh, xh, ze, xl, c, RA:R]
        for d in (1, 3, 2):
            px = ring_x(d)
            send(rest, rest, s_wy, (kv,), at_x(px))

    def w_second(kv):
        arrived(zr.at[kv, 0:3, 0 : R - RA], s_wy, (kv,))
        part = w.at[kv, zh, :, ze, :, c, RA:R]

        def z_send(i):
            pz = ring_z(i + 1)
            send(part, part, s_wr, (kv, z), at_z(pz))

        loop(7, z_send)

    def w_x(kv, i):
        h = ring_y(i + 1)

        def wait_z(e):
            pz = 2 * h + e

            @pl.when(pz != z)
            def _():
                arrived(w.at[kv, h, xh, e, xl, c, 0:RA], s_wz, (kv, pz))

        loop(2, wait_z)
        part = w.at[kv, h, xh, :, xl, c, 0:RA]
        for d in (1, 3):
            send(part, part, s_wx, (kv, h, 0), at_x(ring_x(d)))

    def far_x(kv, h, px, e):
        return w.at[kv, h, lax.div(px, 2), e, lax.rem(px, 2), c, 0:RA]

    def w_on(kv, i):
        h = ring_y(i + 1)
        arrived(w.at[kv, h, 0, :, :, c, 0:RA], s_wx, (kv, h, 0))
        for d, to, e in ((3, 1, 0), (1, 3, 1)):
            part = far_x(kv, h, ring_x(d), e)
            send(part, part, s_wx, (kv, h, 1), at_x(ring_x(to)))

    def w_core(kv, i):
        h = ring_y(i + 1)
        arrived(w.at[kv, h, 0, 0, :, c, 0:RA], s_wx, (kv, h, 1))

        def wait_z(e):
            pz = 2 * h + e

            @pl.when(pz != z)
            def _():
                arrived(w.at[kv, h, :, e, :, c, RA:R], s_wr, (kv, pz))

        loop(2, wait_z)
        part = w.at[kv, h, :, :, :, c]
        send(part, part, s_wc, (kv, h), core)

    w_first(0)
    w_move(1)
    loop(4, lambda i: w_x(0, i))
    w_second(0)
    w_first(1)
    loop(4, lambda i: w_on(0, i))
    send(kcot_ref.at[:, 1 - xh], cot.at[xh], s_cot, (0,), opposite)

    def panel(kv, h):
        return jnp.concatenate(
            [w[kv, h, 0].reshape(DC, H), w[kv, h, 1].reshape(DC, H)], axis=1
        )

    def forward(kv, i):
        h = ring_y(i + 1)
        part = dot(hc[...].reshape(4 * T, DC), panel(kv, h))

        @pl.when(h != y)
        def _():
            psend[kv, h] = part.astype(bf16)

        @pl.when(h == y)
        def _():
            own[kv] = part

    def partial_send(kv, d):
        py = ring_y(d)
        send(psend.at[kv, py], precv.at[kv, y], s_p, (0,), at_y(py))

    def halves(ref, half):
        return ref.at[half * 2 * T : (half + 1) * 2 * T]

    def far_send():
        for d, half in ((1, 0), (3, 1)):
            part = halves(psend.at[1, ring_y(2)], half)
            send(part, pfar.at[half], s_pf, (0,), at_y(ring_y(d)))

    def near_send(d, slot, half):
        src = halves(psend.at[1, ring_y(d)], half)
        dst = halves(precv.at[1, slot], half)
        send(src, dst, s_pn, (0,), at_y(ring_y(d)))

    def near_added():
        arrived(pfar, s_pf, (0,))
        for d, slot in ((1, 0), (3, 1)):
            rows = slice(slot * 2 * T, (slot + 1) * 2 * T)
            total = psend[1, ring_y(d), rows].astype(f32) + pfar[slot].astype(f32)
            psend[1, ring_y(d), rows] = total.astype(bf16)
            near_send(d, slot, slot)

    arrived(hc.at[0:3], s_hid, (0,))

    def gather(kv):
        for d in (1, 3):
            send(cb.at[kv, y], cb.at[kv, y], s_ag, (kv, 0), at_y(ring_y(d)))

    def gather_near(kv):
        arrived(cb.at[kv, 0:2], s_ag, (kv, 0))
        for d, to, half in ((3, 1, 0), (1, 3, 2)):
            part = cb.at[kv, ring_y(d), :, half : half + 2]
            send(part, part, s_ag, (kv, 1), at_y(ring_y(to)))

    def gather_far(kv):
        arrived(cb.at[kv, 0], s_ag, (kv, 1))

    arrived(cb.at[1, y, 1 - xh], s_cot, (1,))
    gather(1)
    for k in range(4):
        hct[:, k * T : (k + 1) * T] = hc[k].T

    def key_tile(i):
        h = ring_y(i + 1)
        arrived(w.at[0, h, :, :, :, 1 - c], s_wc, (0, h))
        forward(0, i)

        @pl.when(i < 3)
        def _():
            partial_send(0, i + 1)

    def key_step(i):
        w_core(0, i)

        @pl.when(i > 0)
        def _():
            key_tile(i - 1)

    loop(4, key_step)
    key_tile(3)
    gather_near(1)
    w_second(1)
    loop(4, lambda i: w_x(1, i))

    def cots(kv, h):
        return jnp.concatenate(
            [cb[kv, h, 0].reshape(4 * T, H), cb[kv, h, 1].reshape(4 * T, H)], axis=1
        )

    def grad_tile(kv, h):
        g = dot(hct[...], cots(kv, h)).astype(bf16).reshape(2, 2, 2, R, 2 * H)
        for pc in range(2):
            for ph in range(2):
                for pxl in range(2):
                    dw[kv, h, pc, 2 * ph + pxl] = g[:, pxl, pc, :, ph * H : (ph + 1) * H]
        send(dw.at[kv, h, 1 - c], dwc.at[kv, h], s_dc, (kv, h), core)

    def grad_near(kv, h, d, slot, e):
        src, dst = dw.at[kv, h, c, ring_x(d), e], dwx.at[kv, h, slot, e]
        send(src, dst, s_dx, (kv, h), at_x(ring_x(d)))

    def grad_core(kv, h):
        arrived(dwc.at[kv, h], s_dc, (kv, h))
        dw[kv, h, c] = (dw[kv, h, c].astype(f32) + dwc[kv, h].astype(f32)).astype(bf16)
        for d, e in ((1, 0), (3, 1)):
            part = dw.at[kv, h, c, ring_x(2), e]
            send(part, dwf.at[kv, h, e], s_df, (kv, h), at_x(ring_x(d)))
        grad_near(kv, h, 1, 0, 1)
        grad_near(kv, h, 3, 1, 0)

    def grad_last(h):
        arrived(dwc.at[0, h], s_dc, (0, h))
        dw[0, h, c] = (dw[0, h, c].astype(f32) + dwc[0, h].astype(f32)).astype(bf16)
        for d, slot in ((1, 0), (3, 1)):
            for e in range(2):
                grad_near(0, h, d, slot, e)
        send(dw.at[0, h, c, ring_x(2)], dwd, s_df, (0, h), at_x(ring_x(2)))

    def grad_added(kv, h):
        arrived(dwf.at[kv, h], s_df, (kv, h))
        for d, slot in ((1, 0), (3, 1)):
            mine = dw[kv, h, c, ring_x(d), slot].astype(f32)
            total = mine + dwf[kv, h, slot].astype(f32)
            dw[kv, h, c, ring_x(d), slot] = total.astype(bf16)
            grad_near(kv, h, d, slot, slot)

    def grad_x(kv, h, last=False):
        total = dw[kv, h, c, x].astype(f32)
        if last:
            arrived(dwd, s_df, (0, h))
            total = total + dwd[...].astype(f32)
        arrived(dwx.at[kv, h], s_dx, (kv, h))
        for slot in range(2):
            total = total + dwx[kv, h, slot].astype(f32)
        zs[kv, h] = total.astype(bf16)

        def body(e):
            pz = 2 * h + e

            @pl.when(pz != z)
            def _():
                send(zs.at[kv, h, e], zr.at[kv, z], s_dz, (kv,), at_z(pz))

        loop(2, body)

    def grad_z(kv):
        total = zs[kv, zh, ze].astype(f32)
        arrived(zr.at[kv, 0:7], s_dz, (kv,))
        for d in range(1, 8):
            pz = ring_z(d)
            total = total + zr[kv, pz].astype(f32)

        @pl.when(moved)
        def _():
            fin[kv] = total.astype(bf16)
            send(fin.at[kv], finm.at[kv], s_dp, (kv,), partner)

        @pl.when(jnp.logical_not(moved))
        def _():
            finr[kv] = total

    loop(3, lambda i: grad_tile(1, ring_y(i + lax.div(i, 2))))
    loop(3, lambda i: grad_core(1, ring_y(i + lax.div(i, 2))))

    arrived(cot.at[1 - xh], s_cot, (0,))

    def rows_cols(t, s):
        return pl.ds(pl.multiple_of(t * T, T), T), slice(s * H, (s + 1) * H)

    def key_sum(t, s):
        rows, cols = rows_cols(t, s)
        total = own[0, rows, cols]
        for d in range(1, 4):
            total = total + precv[0, ring_y(d), rows, cols].astype(f32)
        return total

    def value_sum(t, s):
        rows, cols = rows_cols(t, s)
        near = precv[1, 0, rows, cols].astype(f32) + precv[1, 1, rows, cols].astype(f32)
        return own[1, rows, cols] + near

    loop(4, lambda i: w_on(1, i))
    arrived(precv.at[0, 0:3], s_p, (0,))
    hgain = hgain_ref[...].astype(f32)
    vx[x] = jnp.zeros((1, DC + H), f32)

    def key_block(t):
        for s in range(2):
            key = key_sum(t, s)
            krinv = lax.rsqrt(jnp.mean(key * key, axis=-1, keepdims=True) + eps)
            kn = key * krinv
            oown[0, s, t] = (kn * hgain).astype(bf16)
            ct = cot[s, t].astype(f32)
            back = ct * hgain
            grad = krinv * (back - kn * jnp.mean(back * kn, axis=-1, keepdims=True))
            cb[0, y, s, t] = grad.astype(bf16)
            vx[x, :, DC:] += jnp.sum(ct * kn, axis=0, keepdims=True)

    loop(4, key_block)
    gather(0)
    send(oown.at[0, 1 - xh], orecv.at[0], s_out, (0,), opposite)
    hand_on(oown.at[0, xh], ks_hbm.at[:, xh])

    def back_panel(kv, h, first):
        part = dot_nt(cots(kv, h), panel(kv, h)).reshape(4, T, DC)
        if first:
            dhv[...] = part
        else:
            dhv[...] += part

    loop(3, lambda i: grad_added(1, ring_y(i + lax.div(i, 2))))
    grad_tile(0, y)
    back_panel(0, y, True)
    gather_far(1)
    grad_tile(1, ring_y(2))
    loop(4, lambda i: w_core(1, i))
    grad_core(1, ring_y(2))
    grad_core(0, y)

    def value_tile(i):
        k = jnp.where(i == 0, 1, jnp.where(i == 1, 0, i))
        h = ring_y(k + 1)
        arrived(w.at[1, h, :, :, :, 1 - c], s_wc, (1, h))
        forward(1, k)

        @pl.when(i == 0)
        def _():
            far_send()

        @pl.when(i == 1)
        def _():
            near_send(1, 0, 1)

        @pl.when(i == 2)
        def _():
            near_send(3, 1, 0)

    loop(3, value_tile)
    gather_near(0)
    value_tile(jnp.int32(3))
    loop(3, lambda i: grad_x(1, ring_y(i + lax.div(i, 2))))
    loop(2, lambda i: grad_tile(0, ring_y(2 * i + 1)))
    loop(2, lambda i: grad_core(0, ring_y(2 * i + 1)))
    grad_added(1, ring_y(2))
    grad_added(0, y)
    loop(4, lambda i: back_panel(1, i, False))
    loop(2, lambda i: back_panel(0, ring_y(2 * i + 1), False))
    near_added()
    gather_far(0)

    def hidden_back(i):
        t = ring_y(i + 1)
        far = ring_y(2)
        ct = jnp.concatenate([cb[0, far, 0, t], cb[0, far, 1, t]], axis=1)
        total = dhv[t] + dot_nt(ct, panel(0, far))
        vx[x, :, :DC] += jnp.sum(total * hc[t].astype(f32), axis=0, keepdims=True)

        @pl.when(t != y)
        def _():
            dhs[t] = total.astype(bf16)
            send(dhs.at[t], dhr.at[y], s_dh, (0,), at_y(t))

        @pl.when(t == y)
        def _():
            dhr[y] = total.astype(bf16)

    grad_tile(0, ring_y(2))
    loop(2, lambda i: grad_added(0, ring_y(2 * i + 1)))
    loop(4, hidden_back)
    for d in range(1, 4):
        px = ring_x(d)
        send(vx.at[x], vx.at[x], s_vx, (0,), at_x(px))
    grad_last(ring_y(2))
    grad_x(1, ring_y(2))
    grad_x(0, y)

    arrived(vx.at[0:3], s_vx, (0,))
    vz[z] = (vx[0] + vx[1]) + (vx[2] + vx[3])

    def vz_send(i):
        pz = ring_z(i + 1)
        send(vz.at[z], vz.at[z], s_vz, (0,), at_z(pz))

    loop(7, vz_send)
    loop(2, lambda i: grad_x(0, ring_y(2 * i + 1)))
    grad_z(1)
    grad_x(0, ring_y(2), True)
    arrived(vz.at[0:7], s_vz, (0,))
    vc[c] = ((vz[0] + vz[1]) + (vz[2] + vz[3])) + ((vz[4] + vz[5]) + (vz[6] + vz[7]))
    send(vc.at[c], vc.at[c], s_vc, (0,), core)
    grad_z(0)
    arrived(vc.at[1 - c], s_vc, (0,))
    vy[y] = vc[0] + vc[1]
    for d in range(1, 4):
        py = ring_y(d)
        send(vy.at[y], vy.at[y], s_vy, (0,), at_y(py))

    arrived(precv.at[1, 0:2], s_pn, (0,))

    def value_block(t):
        for s in range(2):
            oown[1, s, t] = value_sum(t, s).astype(bf16)

    loop(4, value_block)
    send(oown.at[1, 1 - xh], orecv.at[1], s_out, (1,), opposite)
    hand_on(oown.at[1, xh], vs_hbm.at[:, xh])

    arrived(dhr.at[0:3], s_dh, (0,))

    def input_rows(i):
        rows = pl.ds(pl.multiple_of(i * 16, 16), 16)
        rinv = rinv_s[rows, 0:1]
        mean = jnp.zeros((16, 1), f32)
        for k in range(4):
            cols = slice(k * DC, (k + 1) * DC)
            normed = x_ref[rows, cols].astype(f32) * rinv
            back = dhr[k, rows, :].astype(f32) * gain_s[:, cols]
            mean = mean + jnp.sum(back * normed, axis=-1, keepdims=True)
        mean = mean * (1.0 / D)
        for k in range(4):
            cols = slice(k * DC, (k + 1) * DC)
            normed = x_ref[rows, cols].astype(f32) * rinv
            back = dhr[k, rows, :].astype(f32) * gain_s[:, cols]
            ig_ref[rows, cols] = (rinv * (back - normed * mean)).astype(bf16)

    loop(8, input_rows)
    hand_on(ig_ref, ig_hbm)
    arrived(vy.at[0:3], s_vy, (0,))
    for k in range(4):
        cols = slice(k * DC, (k + 1) * DC)
        ng_ref[:, cols] = vy[k, :, :DC] / gain_s[:, cols]
    hg_ref[...] = (vy[0, :, DC:] + vy[1, :, DC:]) + (vy[2, :, DC:] + vy[3, :, DC:])
    hand_on(ng_ref, ng_hbm)
    hand_on(hg_ref, hg_hbm)
    for kv, ref in ((0, ks_hbm), (1, vs_hbm)):
        arrived(orecv.at[kv], s_out, (kv,))
        hand_on(orecv.at[kv], ref.at[:, 1 - xh])
    for kv, ref in ((1, dwv_hbm), (0, dwk_hbm)):

        @pl.when(moved)
        def _():
            arrived(finm.at[kv], s_dp, (kv,))
            finr[kv] = finm[kv].astype(f32)

        hand_on(finr.at[kv], ref)

    @pl.when(moved)
    def _():
        sent(w.at[0, 0, 0, 0, 0], s_w0, (0,))
        sent(fin, s_dp, (0,))

    sent(zr.at[:, 0:7, 0:RA], s_wz, (0, 0))
    sent(psend.at[:, :, 0 : 3 * RA], s_wx, (0, 0, 0))
    sent(zr.at[:, 0:3, 0 : R - RA], s_wy, (0,))
    sent(psend.at[0, :, 0 : 7 * (R - RA)], s_wr, (0, 0))
    sent(w.at[:, :, :, :, :, 0], s_wc, (0, 0))
    sent(hid.at[0:3], s_hid, (0,))
    sent(cot, s_cot, (0,))
    sent(cb.at[:, 0:3], s_ag, (0, 0))
    sent(psend.at[0, 0:3], s_p, (0,))
    sent(pfar, s_pf, (0,))
    sent(precv.at[1, 0:2], s_pn, (0,))
    sent(orecv, s_out, (0,))
    sent(dhs.at[0:3], s_dh, (0,))
    sent(dwc, s_dc, (0, 0))
    sent(dwx, s_dx, (0, 0))
    sent(dwf, s_df, (0, 0))
    sent(zr.at[:, 0:7], s_dz, (0,))
    sent(vx.at[0:3], s_vx, (0,))
    sent(vz.at[0:7], s_vz, (0,))
    sent(vc.at[0], s_vc, (0,))
    sent(vy.at[0:3], s_vy, (0,))
    for copy in results:
        copy.wait()


def hand_out(*refs):
    ins, outs, held, sems = refs[:7], refs[7:14], refs[14:21], refs[21]
    parts = [(2, k) for k in range(4)] + [(0, None), (1, None)]
    parts += [(i, None) for i in range(3, 7)]

    def view(ref, k):
        return ref if k is None else ref.at[32 * k : 32 * k + 32]

    first, last = [], []
    for n, (i, k) in enumerate(parts):
        src, mid, dst = view(ins[i], k), view(held[i], k), view(outs[i], k)
        first.append(pltpu.make_async_copy(src, mid, sems.at[0, n]))
        last.append(pltpu.make_async_copy(mid, dst, sems.at[1, n]))
    for copy in first:
        copy.start()
    for n in range(len(parts)):
        first[n].wait()
        last[n].start()
    for copy in last:
        copy.wait()


def on_device(
    inputs, norm_gain, key_weight, value_weight, head_gain, key_cotangent, value_cotangent
):
    def sems(*shape):
        return pltpu.SemaphoreType.DMA(shape)

    scratch = [
        pltpu.VMEM((4, T, DC), bf16),
        pltpu.VMEM((4, T, DC), bf16),
        pltpu.VMEM((DC, 4 * T), bf16),
        pltpu.VMEM((2, 4, 2, 2, 2, 2, R, H), bf16),
        pltpu.VMEM((2, 4, 4 * T, 2 * H), bf16),
        pltpu.VMEM((2, 4, 4 * T, 2 * H), bf16),
        pltpu.VMEM((2, 2 * T, 2 * H), bf16),
        pltpu.VMEM((2, 4 * T, 2 * H), f32),
        pltpu.VMEM((2, 4, T, H), bf16),
        pltpu.VMEM((2, 4, 2, 4, T, H), bf16),
        pltpu.VMEM((2, 2, 4, T, H), bf16),
        pltpu.VMEM((2, 4, T, H), bf16),
        pltpu.VMEM((4, T, DC), f32),
        pltpu.VMEM((4, T, DC), bf16),
        pltpu.VMEM((4, T, DC), bf16),
        pltpu.VMEM((2, 4, 2, 4, 2, R, H), bf16),
        pltpu.VMEM((2, 4, 4, 2, R, H), bf16),
        pltpu.VMEM((2, 4, 2, 2, R, H), bf16),
        pltpu.VMEM((2, 4, 2, R, H), bf16),
        pltpu.VMEM((2, R, H), bf16),
        pltpu.VMEM((2, 4, 2, R, H), bf16),
        pltpu.VMEM((2, 8, R, H), bf16),
        pltpu.VMEM((2, R, H), bf16),
        pltpu.VMEM((2, R, H), bf16),
        pltpu.VMEM((2, R, H), f32),
        pltpu.VMEM((4, 1, DC + H), f32),
        pltpu.VMEM((8, 1, DC + H), f32),
        pltpu.VMEM((2, 1, DC + H), f32),
        pltpu.VMEM((4, 1, DC + H), f32),
        pltpu.VMEM((T, 128), f32),
        pltpu.VMEM((1, D), f32),
        pltpu.VMEM((T, D), bf16),
        pltpu.VMEM((T, D), bf16),
        pltpu.VMEM((1, D), f32),
        pltpu.VMEM((1, H), f32),
        sems(2),
        sems(2, 8),
        sems(2, 4, 2),
        sems(2),
        sems(2, 8),
        sems(2, 4),
        sems(1),
        sems(2),
        sems(2, 2),
        sems(1),
        sems(1),
        sems(1),
        sems(2),
        sems(1),
        sems(2, 4),
        sems(2, 4),
        sems(2, 4),
        sems(2),
        sems(2),
        sems(1),
        sems(1),
        sems(1),
        sems(1),
        sems(3),
        sems(23),
        sems(9),
    ]
    outs = (
        jax.ShapeDtypeStruct((4, 2, T, H), bf16),
        jax.ShapeDtypeStruct((4, 2, T, H), bf16),
        jax.ShapeDtypeStruct((T, D), bf16),
        jax.ShapeDtypeStruct((R, H), f32),
        jax.ShapeDtypeStruct((R, H), f32),
        jax.ShapeDtypeStruct((1, D), f32),
        jax.ShapeDtypeStruct((1, H), f32),
    )
    vmem = pl.BlockSpec(memory_space=pltpu.VMEM)
    anywhere = pl.BlockSpec(memory_space=pl.ANY)
    results = pl.pallas_call(
        kernel,
        out_shape=outs,
        in_specs=[anywhere, vmem, vmem, vmem, vmem, anywhere, anywhere],
        out_specs=(anywhere,) * 7,
        scratch_shapes=scratch,
        compiler_params=pltpu.CompilerParams(
            collective_id=0, has_side_effects=True, vmem_limit_bytes=60 * 1024 * 1024
        ),
        cost_estimate=pl.CostEstimate(
            flops=6 * 512 * DC * 2048, bytes_accessed=6 * 1024 * 1024, transcendentals=0
        ),
    )(
        inputs,
        norm_gain.reshape(D // 128, 128),
        key_weight,
        value_weight,
        head_gain.reshape(1, H),
        key_cotangent.reshape(4, 2, T, H),
        value_cotangent.reshape(4, 2, T, H),
    )
    ks, vs, ig, dwk, dwv, ng, hg = pl.pallas_call(
        hand_out,
        out_shape=outs,
        in_specs=[pl.BlockSpec(memory_space=pl.ANY)] * 7,
        out_specs=(pl.BlockSpec(memory_space=pl.ANY),) * 7,
        scratch_shapes=[pltpu.VMEM(o.shape, o.dtype) for o in outs]
        + [pltpu.SemaphoreType.DMA((2, 10))],
        compiler_params=pltpu.CompilerParams(vmem_limit_bytes=60 * 1024 * 1024),
    )(*results)
    return (
        ks.reshape(8 * T, H),
        vs.reshape(8 * T, H),
        ig,
        dwk,
        dwv,
        ng.reshape(D),
        hg.reshape(H),
    )


def solution(mesh):
    in_specs = (
        P(("dp", "tensor"), None),
        P(),
        P("dp", "tensor"),
        P("dp", "tensor"),
        P(),
        P("dp", "tensor"),
        P("dp", "tensor"),
    )
    out_specs = (
        P("dp", "tensor"),
        P("dp", "tensor"),
        P(("dp", "tensor"), None),
        P("dp", "tensor"),
        P("dp", "tensor"),
        P(),
        P(),
    )
    return jax.shard_map(
        on_device, mesh=mesh, in_specs=in_specs, out_specs=out_specs, check_vma=False
    )
```
